32 devices in a mesh: dp: 8 (over z, x), tensor: 4 (over y, core).
Axes of the slice: x: 2, y: 2, z: 4, core: 2. Of those that a mesh axis runs over, the one named last changes fastest.
Arguments:
- inputs: bfloat16 [8192, 2048], P('dp'), may hold values from -6 to 6
- segments: int32 [8, 1024], P('dp'), may hold values from 0 to 3, never falling along the last dimension, each value on 1 to 512 neighbouring positions
- decay_order: int32 [8], P('tensor'), may hold values from 0 to 7, each once
- ln1_gain: float32 [2048], replicated, may hold values from 0.1 to 1.9
- ln1_bias: float32 [2048], replicated, may hold values from -1.5 to 1.5
- w_query: bfloat16 [2048, 2048], P(None, 'tensor'), may hold values from -0.125 to 0.125
- w_key: bfloat16 [2048, 2048], P(None, 'tensor'), may hold values from -0.125 to 0.125
- w_value: bfloat16 [2048, 4096], P(None, 'tensor'), may hold values from -0.125 to 0.125
- w_swish: bfloat16 [2048, 4096], P(None, 'tensor'), may hold values from -0.125 to 0.125
- w_out: bfloat16 [4096, 2048], P('tensor'), may hold values from -0.1875 to 0.1875
- ln2_gain: float32 [2048], replicated, may hold values from 0.1 to 1.9
- ln2_bias: float32 [2048], replicated, may hold values from -1.5 to 1.5
- w_gate: bfloat16 [2048, 4096], P(None, 'tensor'), may hold values from -0.125 to 0.125
- w_up: bfloat16 [2048, 4096], P(None, 'tensor'), may hold values from -0.125 to 0.125
- w_down: bfloat16 [4096, 2048], P('tensor'), may hold values from -0.1875 to 0.1875
- cotangent: bfloat16 [8192, 2048], P('dp'), may hold values from -6 to 6
Outputs:
- output: bfloat16 [8192, 2048], P('dp')
- grad_inputs: float32 [8192, 2048], P('dp')
- grad_ln1_gain: float32 [2048], P('dp')
- grad_ln1_bias: float32 [2048], P('dp')
- grad_query: float32 [2048, 2048], P('dp', 'tensor')
- grad_key: float32 [2048, 2048], P('dp', 'tensor')
- grad_value: float32 [2048, 4096], P('dp', 'tensor')
- grad_swish: float32 [2048, 4096], P('dp', 'tensor')
- grad_out: float32 [4096, 2048], P('tensor', 'dp')
- grad_ln2_gain: float32 [2048], P('dp')
- grad_ln2_bias: float32 [2048], P('dp')
- grad_gate: float32 [2048, 4096], P('dp', 'tensor')
- grad_up: float32 [2048, 4096], P('dp', 'tensor')
- grad_down: float32 [4096, 2048], P('tensor', 'dp')
The draws below stay inside these ranges and needn't reach their ends.
Inputs may be any that keep to these rules, and one draw needn't show every extreme that they name: `segments`: along each sequence the document number never falls; each document has 1 to 512 tokens. `decay_order`: every head has its own number.
All inputs are finite; a program needn't handle non-finite values.
Results may differ from the reference program's by a relative error of at most 0.017.
Values sent between devices are 32-bit elements; how exact they have to be, the bound alone decides.
A program may use at most 320 MiB of HBM per device.

```python
import math
import jax
import jax.numpy as jnp
import numpy as np
from jax import lax

D = 2048
HEADS = 8
KEY = 256
VALUE = 512
FF = 4096
SEQ_LEN = 1024
DOCS = 4
DOC_MOST = 512
SEQS = 8
TOKENS = 8192


def raised(entries, rng, source, target, parts, factor):
    owner, partner = [(jnp.arange(entries.shape[dim]) // (entries.shape[dim] // parts)).reshape([-1 if axis == dim else 1 for axis in range(entries.ndim)]) for dim in (source, target)]
    chosen = jax.random.permutation(rng, parts)[partner]
    strong = (owner == chosen) | (owner == (partner + parts // 2) % parts)
    return jnp.where(strong, factor * entries, entries)


def shard_levels(own_key, dims, shards, low, largest):
    def one(dim, shards_of):
        steps = jax.random.uniform(jax.random.fold_in(jax.random.fold_in(own_key, 6), dim), (shards_of,), jnp.float32, low / len(shards), largest / len(shards))
        return jnp.repeat(jnp.exp(steps), dims[dim] // shards_of).reshape((-1,) + (1,) * (len(dims) - dim - 1))

    level = one(*shards[0])
    for cut in shards[1:]:
        level = level * one(*cut)
    return level


def profile(number_of, total, reach, skew):
    loads = [(1 << 20) // math.isqrt(rank ** skew) + 1 for rank in range(2, number_of + 1)]
    surplus, counts = total - reach - (number_of - 1), [1] * (number_of - 1)
    while surplus > 0:
        candidates = [i for i in range(number_of - 1) if counts[i] < reach]
        mass, left = sum([loads[i] for i in candidates]), surplus
        for i in candidates:
            addition = min(reach - counts[i], max(1, left * loads[i] // mass), surplus)
            counts[i] = counts[i] + addition
            surplus = surplus - addition
    return np.array([reach] + counts)


def ragged(rng, count, total, bound, lean):
    if count == 2:
        one = jax.random.randint(rng, (), max(1, total - bound), min(bound, total - 1) + 1)
        return jnp.stack([one, total - one])
    lengths = jnp.asarray(profile(count, total, bound, lean), jnp.int32)
    pairs = (count - 1) // 2
    giver, taker = lengths[1:1 + 2 * pairs:2], lengths[2:2 + 2 * pairs:2]
    room = jnp.minimum(giver - 1, bound - taker)
    shifted = jax.random.randint(jax.random.fold_in(rng, 1), (pairs,), 0, 1 << 20) % (room + 1)
    lengths = lengths.at[1:1 + 2 * pairs:2].set(giver - shifted).at[2:2 + 2 * pairs:2].set(taker + shifted)
    return lengths[jax.random.permutation(jax.random.fold_in(rng, 2), count)]


def noise(key, dims, width, reach, cuts=(), held_as=jnp.bfloat16):
    values = jax.random.normal(key, dims, jnp.float32) * width
    if len(cuts) > 0:
        values = shard_levels(key, dims, cuts, -0.22, 0.18) * values
    return jnp.clip(values, min=-reach, max=reach).astype(held_as)


def heavy_noise(stream_key, shape, scale, bound, pieces, heavy, kind=jnp.bfloat16):
    drawn = scale * jax.random.normal(stream_key, shape, jnp.float32)
    if pieces:
        drawn = drawn * shard_levels(stream_key, shape, pieces, -0.22, 0.18)
    return jnp.clip(raised(drawn, jax.random.fold_in(stream_key, 3), *heavy), -bound, bound).astype(kind)


def setup_inputs(seed: int = 0) -> dict:
    seeds = jax.random.split(jax.random.key(seed), 17)
    return {
        "inputs": heavy_noise(seeds[0], (TOKENS, D), 1.0, 6.0, ((0, 8),), (0, 1, 8, 2.0)),
        "segments": jax.vmap(lambda own: jnp.searchsorted(jnp.cumsum(ragged(own, DOCS, SEQ_LEN, DOC_MOST, 1)), jnp.arange(SEQ_LEN), side="right"))(jax.random.split(seeds[1], SEQS)).reshape((SEQS, SEQ_LEN)).astype(jnp.int32),
        "decay_order": jax.random.permutation(seeds[2], HEADS).astype(jnp.int32),
        "ln1_gain": jnp.clip(1.0 + 0.18 * jax.random.normal(seeds[3], (D,), jnp.float32), 0.1, 1.9),
        "ln1_bias": noise(seeds[4], (D,), 0.3, 1.5, (), jnp.float32),
        "w_query": noise(seeds[5], (D, HEADS * KEY), D ** -0.5, 0.125, ((1, 4),)),
        "w_key": noise(seeds[6], (D, HEADS * KEY), D ** -0.5, 0.125, ((1, 4),)),
        "w_value": noise(seeds[7], (D, HEADS * VALUE), D ** -0.5, 0.125, ((1, 4),)),
        "w_swish": noise(seeds[8], (D, HEADS * VALUE), D ** -0.5, 0.125, ((1, 4),)),
        "w_out": noise(seeds[9], (HEADS * VALUE, D), (HEADS * VALUE // 4) ** -0.5, 0.1875, ((0, 4),)),
        "ln2_gain": jnp.clip(1.0 + 0.18 * jax.random.normal(seeds[10], (D,), jnp.float32), 0.1, 1.9),
        "ln2_bias": noise(seeds[11], (D,), 0.3, 1.5, (), jnp.float32),
        "w_gate": noise(seeds[12], (D, FF), D ** -0.5, 0.125, ((1, 4),)),
        "w_up": noise(seeds[13], (D, FF), D ** -0.5, 0.125, ((1, 4),)),
        "w_down": noise(seeds[14], (FF, D), (FF // 4) ** -0.5, 0.1875, ((0, 4),)),
        "cotangent": heavy_noise(seeds[15], (TOKENS, D), 1.0, 6.0, ((0, 8),), (0, 1, 8, 2.0)),
    }


@jax.custom_vjp
def low(v):
    return lax.optimization_barrier(v.astype(jnp.bfloat16)).astype(jnp.float32)

@jax.custom_vjp
def low_back(v):
    return v

def low_keep(v):
    return (low(v), None)

def low_pass(kept, grad):
    return (grad,)

def back_keep(v):
    return (v, None)

def back_low(kept, grad):
    return (low(grad),)
low.defvjp(low_keep, low_pass)
low_back.defvjp(back_keep, back_low)

def layer_norm(values, scales, shifts):
    average = lax.optimization_barrier(jnp.mean(values, axis=-1, keepdims=True))
    centred = values - average
    spread = lax.optimization_barrier(jnp.mean(centred * centred, axis=-1, keepdims=True))
    return centred * lax.rsqrt(spread + 1e-05) * scales + shifts

def head_norm(values):
    average = lax.optimization_barrier(jnp.mean(values, axis=-1, keepdims=True))
    centred = values - average
    spread = lax.optimization_barrier(jnp.mean(centred * centred, axis=-1, keepdims=True))
    return centred * lax.rsqrt(spread + 1.0)

def gate_apply(retained, switch):
    row_count = retained.shape[0]
    normed = head_norm(retained).reshape(row_count, -1)
    return normed * jax.nn.silu(switch)

def gelu_product(gate_proj, up_proj):
    return jax.nn.gelu(gate_proj) * up_proj

def rotate(values, cosines, sines, sign):
    full_width = values.shape[-1]
    parity = lax.broadcasted_iota(jnp.int32, (1, full_width), 1) % 2 == 0
    partner = jnp.where(parity, -jnp.roll(values, -1, axis=-1), jnp.roll(values, 1, axis=-1))
    return values * cosines + sign * partner * sines

def angle_tables(length, heads_here):
    half_width = KEY // 2
    column = jnp.arange(KEY, dtype=jnp.int32) // 2
    frequency = jnp.power(10000.0, -column.astype(jnp.float32) / (half_width - 1))
    position = jnp.arange(length, dtype=jnp.int32).astype(jnp.float32)
    angles = position[:, None] * frequency[None, :]
    return (jnp.tile(jnp.cos(angles), (1, heads_here)), jnp.tile(jnp.sin(angles), (1, heads_here)))

def decay_mask(seq_segments, decay_order, length):
    exponent = (decay_order + 5).astype(jnp.float32)
    log_keep = jnp.log1p(-jnp.exp2(-exponent))
    row_index = lax.broadcasted_iota(jnp.int32, (length, length), 0)
    col_index = lax.broadcasted_iota(jnp.int32, (length, length), 1)
    offset_gap = jnp.maximum(row_index - col_index, 0).astype(jnp.float32)
    decays = jnp.exp(offset_gap[None] * log_keep[:, None, None])
    same_doc = (seq_segments[:, :, None] == seq_segments[:, None, :]) & (row_index >= col_index)[None]
    return jnp.where(same_doc[:, None], decays[None], jnp.zeros_like(decays[None]))

def matmul(left, right):
    return jnp.dot(left, right, precision=lax.Precision.HIGHEST)

def full_forward(params, segments, decay_order):
    inputs, g_one, b_one, w_query, w_key, w_value, w_swish, w_out, g_two, b_two, w_gate, w_up, w_down = params
    cosines, sines = angle_tables(SEQ_LEN, HEADS)
    key_scale = float(KEY) ** (-0.5)

    def one_sequence(pair):
        seq_inputs, seq_segments = pair
        weights_mask = decay_mask(seq_segments[None], decay_order, SEQ_LEN)[0]
        normed_one = low(layer_norm(seq_inputs, g_one, b_one))
        query_proj = low_back(matmul(normed_one, w_query))
        key_proj = low_back(matmul(normed_one, w_key))
        value_proj = low(low_back(matmul(normed_one, w_value)))
        switch = low_back(matmul(normed_one, w_swish))
        query_rot = low(rotate(query_proj, cosines, sines, 1.0)).reshape(SEQ_LEN, HEADS, KEY)
        key_rot = low(rotate(key_proj, cosines, sines, 1.0) * key_scale).reshape(SEQ_LEN, HEADS, KEY)
        value_four = value_proj.reshape(SEQ_LEN, HEADS, VALUE)
        scores = jnp.einsum('nhk,mhk->hnm', query_rot, key_rot, precision=lax.Precision.HIGHEST)
        weighted = low(low_back(scores) * weights_mask)
        retained = low_back(jnp.einsum('hnm,mhv->nhv', weighted, value_four, precision=lax.Precision.HIGHEST))
        gated = low(gate_apply(retained, switch))
        branch = low_back(matmul(gated, w_out))
        middle = seq_inputs + branch
        normed_two = low(layer_norm(middle, g_two, b_two))
        gate_proj = low_back(matmul(normed_two, w_gate))
        up_proj = low_back(matmul(normed_two, w_up))
        hidden = low(gelu_product(gate_proj, up_proj))
        feed_out = low_back(matmul(hidden, w_down))
        return middle + feed_out
    stacked = lax.map(jax.checkpoint(one_sequence), (inputs.reshape(SEQS, SEQ_LEN, D), segments))
    return stacked.reshape(TOKENS, D)

def reference(inputs, segments, decay_order, ln1_gain, ln1_bias, w_query, w_key, w_value, w_swish, w_out, ln2_gain, ln2_bias, w_gate, w_up, w_down, cotangent):
    floats = tuple((item.astype(jnp.float32) for item in (inputs, ln1_gain, ln1_bias, w_query, w_key, w_value, w_swish, w_out, ln2_gain, ln2_bias, w_gate, w_up, w_down)))

    def forward(params):
        return full_forward(params, segments, decay_order)
    result, pullback = jax.vjp(forward, floats)
    grads = pullback(cotangent.astype(jnp.float32))[0]
    return (result.astype(jnp.bfloat16), grads[0], grads[1], grads[2], grads[3], grads[4], grads[5], grads[6], grads[7], grads[8], grads[9], grads[10], grads[11], grads[12])
```

```python
import functools

import jax
import jax.numpy as jnp
from jax import lax
from jax.experimental import pallas as pl
from jax.experimental.pallas import tpu as pltpu
from jax.sharding import PartitionSpec as P

KEY = 256
VALUE = 512
SEQ_LEN = 1024
DOC_MOST = 512
BLOCK = 256
CHUNKS = SEQ_LEN // BLOCK
HALF = BLOCK // 2
BF16 = jnp.bfloat16
F32 = jnp.float32
MIB = 1 << 20


def product_tn(left, right):
    return lax.dot_general(left, right, (((0,), (0,)), ((), ())), preferred_element_type=F32)


def product_nt(left, right):
    return lax.dot_general(left, right, (((1,), (1,)), ((), ())), preferred_element_type=F32)


def product_nn(left, right):
    return jnp.dot(left, right, preferred_element_type=F32)


def angle_tables(length):
    half_width = KEY // 2
    column = jnp.arange(KEY, dtype=jnp.int32) // 2
    frequency = jnp.power(10000.0, -column.astype(F32) / (half_width - 1))
    position = jnp.arange(length, dtype=jnp.int32).astype(F32)
    angles = position[:, None] * frequency[None, :]
    return jnp.cos(angles), jnp.sin(angles)


def rotate(values, cosines, sines, sign):
    even = lax.broadcasted_iota(jnp.int32, values.shape, 1) % 2 == 0
    after = pltpu.roll(values, KEY - 1, 1)
    before = pltpu.roll(values, 1, 1)
    return values * cosines + sign * jnp.where(even, -after, before) * sines


def normal_rows(values, eps):
    average = jnp.mean(values, axis=-1, keepdims=True)
    centred = values - average
    spread = jnp.mean(centred * centred, axis=-1, keepdims=True)
    return centred, lax.rsqrt(spread + eps)


def decay_block(log_keep, seg_rows, seg_columns, row_start, column_start):
    rows = row_start + lax.broadcasted_iota(jnp.int32, (BLOCK, BLOCK), 0)
    columns = column_start + lax.broadcasted_iota(jnp.int32, (BLOCK, BLOCK), 1)
    gap = rows - columns
    keep = (seg_rows == seg_columns) & (gap >= 0)
    return jnp.where(keep, jnp.exp(jnp.maximum(gap, 0).astype(F32) * log_keep), 0.0)


def first_key_block(chunk):
    return max(0, chunk - (DOC_MOST + BLOCK - 2) // BLOCK)


class Line:
    def __init__(self):
        self.last = []
        self.shared = 0

    def call(
        self,
        kernel,
        outs,
        out_specs,
        ins,
        in_specs,
        grid=(1,),
        scalars=None,
        scratch=(),
        vmem=63,
        onto=(),
        paired=False,
    ):
        extra = [array for _, array in onto] + self.last
        scalar_count = 0 if scalars is None else 1
        in_count = len(ins)
        skipped = len(extra)

        def body(*refs):
            head, rest = refs[: scalar_count + in_count], refs[scalar_count + in_count + skipped :]
            kernel(*head, *rest)

        specs = list(in_specs) + [pl.BlockSpec(memory_space=pl.ANY)] * skipped
        arguments = ([] if scalars is None else [scalars]) + list(ins) + extra
        extras = {}
        if paired:
            extras = dict(collective_id=self.shared, has_side_effects=True)
            self.shared += 1
        result = pl.pallas_call(
            body,
            out_shape=tuple(outs),
            grid_spec=pltpu.PrefetchScalarGridSpec(
                num_scalar_prefetch=scalar_count,
                grid=grid,
                in_specs=specs,
                out_specs=tuple(out_specs),
                scratch_shapes=list(scratch),
            ),
            input_output_aliases={scalar_count + in_count + n: out for n, (out, _) in enumerate(onto)},
            compiler_params=pltpu.CompilerParams(
                vmem_limit_bytes=vmem * MIB,
                dimension_semantics=("arbitrary",) * len(grid),
                **extras,
            ),
            cost_estimate=pl.CostEstimate(flops=1, bytes_accessed=1, transcendentals=0),
        )(*arguments)
        self.last = [result[0]]
        return result


def my_core():
    return lax.rem(lax.axis_index("tensor"), 2)


def other_core():
    rank = lax.axis_index("tensor")
    return {"tensor": rank + 1 - 2 * lax.rem(rank, 2)}


def meet_other_core():
    barrier = pltpu.get_barrier_semaphore()
    pl.semaphore_signal(barrier, inc=1, device_id=other_core(), device_id_type=pl.DeviceIdType.MESH)
    pl.semaphore_wait(barrier, 1)


def to_other_core(source, target, sent, arrived):
    return pltpu.make_async_remote_copy(
        src_ref=source,
        dst_ref=target,
        send_sem=sent,
        recv_sem=arrived,
        device_id=other_core(),
        device_id_type=pl.DeviceIdType.MESH,
    )


def core_rows(mine, block):
    core = my_core() if mine else 1 - my_core()
    return pl.ds(pl.multiple_of(block * BLOCK + core * HALF, HALF), HALF)


def shape(dims, kind):
    return jax.ShapeDtypeStruct(dims, kind)


def const_spec(dims):
    return pl.BlockSpec(dims, lambda *_: (0,) * len(dims))


def once_spec(dims):
    return pl.BlockSpec(dims, lambda *_: (0,) * len(dims), pipeline_mode=pl.Buffered(1))


def row_spec(rows, columns, chunk):
    return pl.BlockSpec((rows, columns), lambda *_: (chunk, 0))


SMEM = pl.BlockSpec(memory_space=pltpu.SMEM)


def proj_kernel(x, gain, bias, cos, sin, wq, wk, wv, ws, a_out, q_out, k_out, v_out, s_out):
    centred, scale = normal_rows(x[...].astype(F32), 1e-05)
    normed = (centred * scale * gain[...] + bias[...]).astype(BF16)
    a_out[...] = normed
    query = product_nn(normed, wq[...])
    key = product_nn(normed, wk[...])
    for first in range(0, query.shape[1], KEY):
        part = slice(first, first + KEY)
        q_out[:, part] = rotate(query[:, part], cos[...], sin[...], 1.0).astype(BF16)
        turned = rotate(key[:, part], cos[...], sin[...], 1.0) * float(KEY) ** (-0.5)
        k_out[:, part] = turned.astype(BF16)
    v_out[...] = product_nn(normed, wv[...]).astype(BF16)
    s_out[...] = product_nn(normed, ws[...])


def projections(line, x, gain, bias, cos, sin, wq, wk, wv, ws):
    rows, width = x.shape

    def rowed(columns):
        return pl.BlockSpec((BLOCK, columns), lambda i: (i, 0))

    kw, vw = wq.shape[1], wv.shape[1]
    return line.call(
        proj_kernel,
        [
            shape((rows, width), BF16),
            shape((rows, kw), BF16),
            shape((rows, kw), BF16),
            shape((rows, vw), BF16),
            shape((rows, vw), F32),
        ],
        [rowed(width), rowed(kw), rowed(kw), rowed(vw), rowed(vw)],
        [x, gain, bias, cos, sin, wq, wk, wv, ws],
        [
            rowed(width),
            const_spec((1, width)),
            const_spec((1, width)),
            rowed(KEY),
            rowed(KEY),
            once_spec(wq.shape),
            once_spec(wk.shape),
            once_spec(wv.shape),
            once_spec(ws.shape),
        ],
        grid=(rows // BLOCK,),
    )


TILES = 4


def retain_kernel(chunk, q, k, v, switch, seg_col, seg_row, logs, w, chip, u_out, o_out, p_out, full, sent, got, s1, s2):
    meet_other_core()
    heads = q.shape[1] // KEY
    low = first_key_block(chunk)
    for head in range(heads):
        kpart, vpart = slice(head * KEY, (head + 1) * KEY), slice(head * VALUE, (head + 1) * VALUE)
        total = None
        for block in range(low, chunk + 1):
            rows = slice(block * BLOCK, (block + 1) * BLOCK)
            raw = product_nt(q[:, kpart], k[rows, kpart])
            mask = decay_block(logs[head], seg_col[...], seg_row[:, rows], chunk * BLOCK, block * BLOCK)
            weights = (raw * mask).astype(BF16)
            p_out[head, :, (block - low) * BLOCK : (block - low + 1) * BLOCK] = weights
            part = product_nn(weights, v[rows, vpart])
            total = part if total is None else total + part
        o_out[:, vpart] = total
        centred, scale = normal_rows(total, 1.0)
        gate = switch[:, vpart]
        u_out[:, vpart] = (centred * scale * (gate * jax.nn.sigmoid(gate))).astype(BF16)
    tile = w.shape[1] // TILES
    copies = []
    for j in range(TILES):
        columns = slice(j * tile, (j + 1) * tile)
        full[:, columns] = product_nn(u_out[...], w[:, columns])
        sent[j] = full[core_rows(False, 0), columns]
        copies.append(to_other_core(sent.at[j], got.at[j], s1.at[j], s2.at[j]))
        copies[-1].start()
    for j in range(TILES):
        columns = slice(j * tile, (j + 1) * tile)
        copies[j].wait()
        chip[:, columns] = full[core_rows(True, 0), columns] + got[j]


def retention(line, chunk, q, k, v, switch, seg_col, seg_row, logs, w):
    kw, vw, width = q.shape[1], v.shape[1], w.shape[1]
    heads = kw // KEY
    blocks = chunk + 1 - first_key_block(chunk)
    return line.call(
        functools.partial(retain_kernel, chunk),
        [
            shape((HALF, width), F32),
            shape((BLOCK, vw), BF16),
            shape((BLOCK, vw), F32),
            shape((heads, BLOCK, blocks * BLOCK), BF16),
        ],
        [
            const_spec((HALF, width)),
            const_spec((BLOCK, vw)),
            const_spec((BLOCK, vw)),
            const_spec((heads, BLOCK, blocks * BLOCK)),
        ],
        [q, k, v, switch, seg_col, seg_row, logs, w],
        [
            row_spec(BLOCK, kw, chunk),
            const_spec(k.shape),
            const_spec(v.shape),
            row_spec(BLOCK, vw, chunk),
            row_spec(BLOCK, 1, chunk),
            const_spec(seg_row.shape),
            SMEM,
            const_spec(w.shape),
        ],
        scratch=[
            pltpu.VMEM((BLOCK, width), F32),
            pltpu.VMEM((TILES, HALF, width // TILES), F32),
            pltpu.VMEM((TILES, HALF, width // TILES), F32),
            pltpu.SemaphoreType.DMA((TILES,)),
            pltpu.SemaphoreType.DMA((TILES,)),
        ],
        paired=True,
    )


def feed_kernel(a, c, wg, wu, wd, hid_out, dg_out, du_out):
    gate = product_nn(a[...], wg[...])
    up = product_nn(a[...], wu[...])
    back = product_nt(c[...], wd[...])
    factor = 0.7978845608028654
    bent = jnp.tanh(factor * (gate + 0.044715 * (gate * gate * gate)))
    half = 0.5 * (1.0 + bent)
    active = gate * half
    slope = half + 0.5 * gate * (1.0 - bent * bent) * (factor * (1.0 + 3 * 0.044715 * gate * gate))
    hid_out[...] = (active * up).astype(BF16)
    dg_out[...] = (back * up * slope).astype(BF16)
    du_out[...] = (back * active).astype(BF16)


def feed_forward(line, chunk, rows, a, c, wg, wu, wd, before):
    width, ff = wg.shape
    tile = min(256, ff)
    whole = a.shape[0]
    return line.call(
        feed_kernel,
        [shape((whole, ff), BF16)] * 3,
        [pl.BlockSpec((rows, tile), lambda i: (chunk, i))] * 3,
        [a, c, wg, wu, wd],
        [
            row_spec(rows, width, chunk),
            row_spec(rows, width, chunk),
            pl.BlockSpec((width, tile), lambda i: (0, i)),
            pl.BlockSpec((width, tile), lambda i: (0, i)),
            pl.BlockSpec((tile, width), lambda i: (i, 0)),
        ],
        grid=(ff // tile,),
        onto=() if before is None else tuple(enumerate(before)),
    )


def chip_kernel(count, transposed, steps, *refs):
    lefts, rights = refs[:count], refs[count : 2 * count]
    out, full, kept, sent, got, s1, s2 = refs[2 * count :]
    half = kept.shape[1]
    j = pl.program_id(0)

    @pl.when(j == 0)
    def _():
        meet_other_core()

    @pl.when(j < steps)
    def _():
        total = None
        for left, right in zip(lefts, rights):
            part = product_nt(left[...], right[...]) if transposed else product_nn(left[...], right[...])
            total = part if total is None else total + part
        full[...] = total
        for n in range(half // HALF):
            part = slice(n * HALF, (n + 1) * HALF)
            sent[j, part] = full[core_rows(False, n), :]
            kept[j, part] = full[core_rows(True, n), :]
        to_other_core(sent.at[j], got.at[j], s1.at[j], s2.at[j]).start()

    @pl.when(j > 0)
    def _():
        to_other_core(sent.at[j - 1], got.at[j - 1], s1.at[j - 1], s2.at[j - 1]).wait()
        out[...] = kept[j - 1] + got[j - 1]


def chip_sum(line, rows, lefts, rights, transposed, chunk):
    width = rights[0].shape[0] if transposed else rights[0].shape[1]
    tile = 512
    steps = width // tile
    half = rows // 2
    right_specs = [
        pl.BlockSpec((tile, right.shape[1]), lambda i: (jnp.minimum(i, steps - 1), 0))
        if transposed
        else pl.BlockSpec((right.shape[0], tile), lambda i: (0, jnp.minimum(i, steps - 1)))
        for right in rights
    ]
    left_specs = [row_spec(rows, left.shape[1], chunk) for left in lefts]
    return line.call(
        functools.partial(chip_kernel, len(lefts), transposed, steps),
        [shape((half, width), F32)],
        [pl.BlockSpec((half, tile), lambda i: (0, jnp.maximum(i, 1) - 1))],
        list(lefts) + list(rights),
        left_specs + right_specs,
        grid=(steps + 1,),
        scratch=[
            pltpu.VMEM((rows, tile), F32),
            pltpu.VMEM((steps, half, tile), F32),
            pltpu.VMEM((steps, half, tile), F32),
            pltpu.VMEM((steps, half, tile), F32),
            pltpu.SemaphoreType.DMA((steps,)),
            pltpu.SemaphoreType.DMA((steps,)),
        ],
        paired=True,
    )[0]


def across_chips(values, size):
    return lax.ppermute(values, "tensor", [(i, i ^ 2) for i in range(size)])


def shared_kernel(work, in_count, *refs):
    ins, out = refs[:in_count], refs[in_count]
    extras, (sent, got, s1, s2) = refs[in_count + 1 : -4], refs[-4:]
    meet_other_core()
    copies = []
    for n in range(sent.shape[0] // HALF):
        part = pl.ds(n * HALF, HALF)
        value = work(n, part, core_rows(True, n), *ins, *extras)
        sent[part, :] = value
        copies.append(to_other_core(sent.at[part], got.at[part], s1.at[n], s2.at[n]))
        copies[-1].start()
        out[core_rows(True, n), :] = value.astype(out.dtype)
    for n, copy in enumerate(copies):
        copy.wait()
        out[core_rows(False, n), :] = got[pl.ds(n * HALF, HALF), :].astype(out.dtype)


def shared_rows(line, work, chunk, rows, ins, in_specs, kind, total_rows, width, extras, before):
    half = rows // 2
    return line.call(
        functools.partial(shared_kernel, work, len(ins)),
        [shape((total_rows, width), kind)] + [shape(dims, F32) for dims in extras],
        [row_spec(rows, width, chunk)] + [const_spec(dims) for dims in extras],
        ins,
        in_specs,
        scratch=[
            pltpu.VMEM((half, width), F32),
            pltpu.VMEM((half, width), F32),
            pltpu.SemaphoreType.DMA((half // HALF,)),
            pltpu.SemaphoreType.DMA((half // HALF,)),
        ],
        onto=() if before is None else ((0, before),),
        paired=True,
    )


def norm_work(n, part, rows, chip, crossed, x, gain, bias, h_out):
    middle = x[rows, :].astype(F32) + (chip[part, :] + crossed[part, :])
    h_out[part, :] = middle
    centred, scale = normal_rows(middle, 1e-05)
    return (centred * scale * gain[...] + bias[...]).astype(BF16).astype(F32)


def second_norm(line, chunk, rows, chip, crossed, x, gain, bias, before):
    width = x.shape[1]
    half = rows // 2
    return shared_rows(
        line,
        norm_work,
        chunk,
        rows,
        [chip, crossed, x, gain, bias],
        [const_spec((half, width)), const_spec((half, width)), row_spec(rows, width, chunk)]
        + [const_spec((1, width))] * 2,
        BF16,
        x.shape[0],
        width,
        [(half, width)],
        before,
    )


def norm_back(n, back, centred, scale, gain, gain_out, bias_out):
    normed = centred * scale
    one, two = jnp.sum(back * normed, axis=0, keepdims=True), jnp.sum(back, axis=0, keepdims=True)
    gain_out[...] = one if n == 0 else gain_out[...] + one
    bias_out[...] = two if n == 0 else bias_out[...] + two
    scaled = back * gain[...]
    first = jnp.mean(scaled, axis=-1, keepdims=True)
    second = jnp.mean(scaled * normed, axis=-1, keepdims=True)
    return scale * (scaled - first - normed * second)


def mid_work(n, part, rows, chip, crossed, h, gain, c, dh_out, gain_out, bias_out):
    centred, scale = normal_rows(h[part, :], 1e-05)
    back = chip[part, :] + crossed[part, :]
    value = c[rows, :].astype(F32) + norm_back(n, back, centred, scale, gain, gain_out, bias_out)
    dh_out[part, :] = value
    return value


def second_norm_back(line, chunk, rows, chip, crossed, h, gain, c, before):
    width = c.shape[1]
    half = rows // 2
    return shared_rows(
        line,
        mid_work,
        chunk,
        rows,
        [chip, crossed, h, gain, c],
        [const_spec((half, width))] * 3 + [const_spec((1, width)), row_spec(rows, width, chunk)],
        BF16,
        c.shape[0],
        width,
        [(half, width), (1, width), (1, width)],
        before,
    )


def first_work(n, part, rows, chip, crossed, x, gain, dh, gain_out, bias_out):
    centred, scale = normal_rows(x[rows, :].astype(F32), 1e-05)
    back = chip[part, :] + crossed[part, :]
    return dh[part, :] + norm_back(n, back, centred, scale, gain, gain_out, bias_out)


def first_norm_back(line, chunk, rows, chip, crossed, x, gain, dh, before):
    width = x.shape[1]
    half = rows // 2
    return shared_rows(
        line,
        first_work,
        chunk,
        rows,
        [chip, crossed, x, gain, dh],
        [const_spec((half, width))] * 2
        + [row_spec(rows, width, chunk), const_spec((1, width)), const_spec((half, width))],
        F32,
        x.shape[0],
        width,
        [(1, width), (1, width)],
        before,
    )


def output_work(n, part, rows, chip, crossed, h):
    return h[part, :] + (chip[part, :] + crossed[part, :])


def output_rows(line, chunk, rows, chip, crossed, h, total_rows, before):
    width = h.shape[1]
    half = rows // 2
    return shared_rows(
        line,
        output_work,
        chunk,
        rows,
        [chip, crossed, h],
        [const_spec((half, width))] * 3,
        BF16,
        total_rows,
        width,
        [],
        before,
    )


def gate_kernel(dz, w, o, switch, do_out, ds_out):
    grad = product_nt(dz[...], w[...])
    centred, scale = normal_rows(o[...], 1.0)
    gate = switch[...]
    sig = jax.nn.sigmoid(gate)
    ds_out[...] = (grad * (centred * scale) * (sig * (1.0 + gate * (1.0 - sig)))).astype(BF16)
    dn = grad * (gate * sig)
    one = jnp.mean(dn, axis=-1, keepdims=True)
    two = jnp.mean(dn * centred, axis=-1, keepdims=True)
    do_out[...] = (scale * (dn - one) - (scale * scale * scale) * centred * two).astype(BF16)


def gate_back(line, dz, w, o, switch):
    rows, width = dz.shape
    vw = w.shape[0]
    part = 512
    tiled = pl.BlockSpec((part, VALUE), lambda h, i: (i, h))
    return line.call(
        gate_kernel,
        [shape((rows, vw), BF16)] * 2,
        [tiled] * 2,
        [dz, w, o, switch],
        [
            pl.BlockSpec((part, width), lambda h, i: (i, 0)),
            pl.BlockSpec((VALUE, width), lambda h, i: (h, 0)),
            tiled,
            tiled,
        ],
        grid=(vw // VALUE, rows // part),
    )


def retain_back_kernel(q, k, v, do, seg_col, seg_row, logs, cos, sin, *rest):
    weights = rest[:CHUNKS]
    dq_out, dk_out, dv_out, dq_sum, dk_sum, dv_sum = rest[CHUNKS:]
    head = pl.program_id(0)
    dk_sum[...] = jnp.zeros_like(dk_sum)
    dv_sum[...] = jnp.zeros_like(dv_sum)
    for chunk in range(CHUNKS):
        low = first_key_block(chunk)
        here = slice(chunk * BLOCK, (chunk + 1) * BLOCK)
        total = None
        for block in range(low, chunk + 1):
            rows = slice(block * BLOCK, (block + 1) * BLOCK)
            part = slice((block - low) * BLOCK, (block - low + 1) * BLOCK)
            mask = decay_block(logs[head], seg_col[here, :], seg_row[:, rows], chunk * BLOCK, block * BLOCK)
            scores = (product_nt(do[here, :], v[rows, :]) * mask).astype(BF16)
            dv_sum[rows, :] += product_tn(weights[chunk][0, :, part], do[here, :])
            dk_sum[rows, :] += product_tn(scores, q[here, :])
            term = product_nn(scores, k[rows, :])
            total = term if total is None else total + term
        dq_sum[here, :] = total
    dq_out[...] = rotate(dq_sum[...], cos[...], sin[...], -1.0).astype(BF16)
    dk_out[...] = (rotate(dk_sum[...], cos[...], sin[...], -1.0) * float(KEY) ** (-0.5)).astype(BF16)
    dv_out[...] = dv_sum[...].astype(BF16)


def retention_back(line, q, k, v, do, seg_col, seg_row, logs, cos, sin, weights):
    rows, kw = q.shape
    vw = v.shape[1]

    def headed(columns):
        return pl.BlockSpec((rows, columns), lambda h: (0, h))

    return line.call(
        retain_back_kernel,
        [shape((rows, kw), BF16), shape((rows, kw), BF16), shape((rows, vw), BF16)],
        [headed(KEY), headed(KEY), headed(VALUE)],
        [q, k, v, do, seg_col, seg_row, logs, cos, sin] + list(weights),
        [
            headed(KEY),
            headed(KEY),
            headed(VALUE),
            headed(VALUE),
            const_spec(seg_col.shape),
            const_spec(seg_row.shape),
            SMEM,
            const_spec(cos.shape),
            const_spec(sin.shape),
        ]
        + [pl.BlockSpec((1,) + part.shape[1:], lambda h: (h, 0, 0)) for part in weights],
        grid=(kw // KEY,),
        scratch=[pltpu.VMEM((rows, KEY), F32), pltpu.VMEM((rows, KEY), F32), pltpu.VMEM((rows, VALUE), F32)],
    )


def block_kernel(by_rows, extra, where, left, right, *refs):
    total = product_tn(left[...], right[...])
    for term in refs[:extra]:
        total = total + term[...].reshape(total.shape)
    out = refs[extra]
    out[...] = total.reshape(out.shape)


class Weight:
    def __init__(self, line, where, left, right, by_rows, dp):
        self.line, self.where, self.left, self.right, self.by_rows, self.dp = line, where, left, right, by_rows, dp
        self.groups = dp // 2
        split = left if by_rows else right
        self.width = split.shape[1] // dp
        self.block = (self.width, right.shape[1]) if by_rows else (left.shape[1], self.width)

    def blocks(self, position, count, own, received=None, travelling=None):
        groups, width = self.groups, self.width
        if width % 128:
            return self.plain_blocks(position, count, own, received, travelling)

        def column(j, where):
            outer = lax.rem(where[1] + 2 * groups - 1 - position - j, groups)
            return outer * 2 + (where[0] if own else 1 - where[0])

        rows = self.left.shape[0]
        moving = pl.BlockSpec((rows, width), lambda j, where: (0, column(j, where)))
        left = moving if self.by_rows else const_spec(self.left.shape)
        right = const_spec(self.right.shape) if self.by_rows else moving
        ins, specs = [self.left, self.right], [left, right]
        if received is not None:
            ins.append(received)
            specs.append(pl.BlockSpec((1,) + self.block, lambda j, where: (position + j, 0, 0)))
        if travelling is not None:
            ins.append(travelling)
            specs.append(const_spec(self.block))
        if received is None:
            out, out_spec = (count,) + self.block, pl.BlockSpec((1,) + self.block, lambda j, where: (j, 0, 0))
        else:
            out, out_spec = self.block, const_spec(self.block)
        return self.line.call(
            functools.partial(block_kernel, self.by_rows, len(ins) - 2),
            [shape(out, F32)],
            [out_spec],
            ins,
            specs,
            grid=(count,),
            scalars=self.where,
        )[0]

    def plain_blocks(self, position, count, own, received, travelling):
        where, groups, width = self.where, self.groups, self.width
        parts = []
        for j in range(position, position + count):
            outer = lax.rem(where[1] + 2 * groups - 1 - j, groups)
            column = (outer * 2 + (where[0] if own else 1 - where[0])) * width
            if self.by_rows:
                part = product_tn(lax.dynamic_slice_in_dim(self.left, column, width, 1), self.right)
            else:
                part = product_tn(self.left, lax.dynamic_slice_in_dim(self.right, column, width, 1))
            if received is not None:
                part = part + received[j]
            if travelling is not None:
                part = part + travelling
            parts.append(part)
        return parts[0] if received is not None else jnp.stack(parts)

    def steps(self):
        dp, groups = self.dp, self.groups
        sent = self.blocks(0, groups, False)
        received = lax.ppermute(sent, "dp", [(i, i ^ 1) for i in range(dp)])
        yield None
        travelling = None
        for position in range(groups):
            block = self.blocks(position, 1, True, received, travelling)
            if position < groups - 1:
                travelling = lax.ppermute(block, "dp", [(i, (i + 2) % dp) for i in range(dp)])
                yield None
            else:
                yield block


def on_device(
    dp,
    tensor,
    inputs,
    segments,
    decay_order,
    ln1_gain,
    ln1_bias,
    w_query,
    w_key,
    w_value,
    w_swish,
    w_out,
    ln2_gain,
    ln2_bias,
    w_gate,
    w_up,
    w_down,
    cotangent,
):
    line = Line()
    place = lax.axis_index("dp")
    where = jnp.stack([lax.rem(place, 2), lax.div(place, 2)]).astype(jnp.int32)
    cos, sin = angle_tables(SEQ_LEN)
    logs = jnp.log1p(-jnp.exp2(-(decay_order + 5).astype(F32)))
    seg_row = segments.reshape(1, SEQ_LEN)
    seg_col = segments.reshape(SEQ_LEN, 1)
    gain1, bias1, gain2, bias2 = (v.reshape(1, -1) for v in (ln1_gain, ln1_bias, ln2_gain, ln2_bias))
    rows_here = inputs.shape[0]

    normed, query, key, value, switch = projections(
        line, inputs, gain1, bias1, cos, sin, w_query, w_key, w_value, w_swish
    )
    every = range(CHUNKS)
    firsts, gated, retained, weights = [], [], [], []
    for chunk in every:
        chip, u, o, p = retention(line, chunk, query, key, value, switch, seg_col, seg_row, logs, w_out)
        firsts.append((chip, across_chips(chip, tensor)))
        gated.append(u)
        retained.append(o)
        weights.append(p)
    middle, normed2, inner = [], None, None
    for chunk in every:
        normed2, h = second_norm(line, chunk, BLOCK, *firsts[chunk], inputs, gain2, bias2, normed2)
        inner = feed_forward(line, chunk, BLOCK, normed2, cotangent, w_gate, w_up, w_down, inner)
        middle.append(h)
    hidden, back_gate, back_up = inner
    gated, retained = jnp.concatenate(gated, axis=0), jnp.concatenate(retained, axis=0)
    results = {}

    def gradient(name, left, right, by_rows):
        for step in Weight(line, where, left, right, by_rows, dp).steps():
            if step is not None:
                results[name] = step
            yield

    rows = 2 * BLOCK
    pair = range(2)
    joined = [jnp.concatenate([middle[2 * i], middle[2 * i + 1]], axis=0) for i in pair]

    def summed(lefts, rights, transposed, chunk):
        chip = chip_sum(line, rows, lefts, rights, transposed, chunk)
        return chip, across_chips(chip, tensor)

    down = gradient("down", hidden, cotangent, False)
    gate = gradient("gate", normed2, back_gate, True)
    up = gradient("up", normed2, back_up, True)
    next(down)
    seconds = [summed([back_gate, back_up], [w_gate, w_up], True, i) for i in pair]
    next(gate)
    next(up)
    dz, dh, ln2g, ln2b = None, [], [], []

    def middle_step(i):
        out, own, one, two = second_norm_back(line, i, rows, *seconds[i], joined[i], gain2, cotangent, dz)
        dh.append(own)
        ln2g.append(one)
        ln2b.append(two)
        return out

    dz = middle_step(0)
    next(down)
    dz = middle_step(1)
    do, ds = gate_back(line, dz, w_out, retained, switch)
    next(down)
    dq, dk, dv = retention_back(line, query, key, value, do, seg_col, seg_row, logs, cos, sin, weights)
    next(down)
    thirds = [
        summed([dq, dk, dv, ds], [w_query, w_key, w_value, w_swish], True, i) for i in pair
    ]
    out = gradient("out", gated, dz, False)
    next(down)
    next(out)
    next(gate)
    swish = gradient("swish", normed, ds, True)
    vgrad = gradient("value", normed, dv, True)
    qgrad = gradient("query", normed, dq, True)
    kgrad = gradient("key", normed, dk, True)
    next(gate)
    grad_inputs, ln1g, ln1b = None, [], []

    def first_step(i):
        out, one, two = first_norm_back(line, i, rows, *thirds[i], inputs, gain1, dh[i], grad_inputs)
        ln1g.append(one)
        ln1b.append(two)
        return out

    grad_inputs = first_step(0)
    next(gate)
    grad_inputs = first_step(1)
    next(gate)
    fourths = [summed([hidden], [w_down], False, i) for i in pair]
    next(swish)
    next(up)
    small = jnp.concatenate([sum(v) for v in (ln1g, ln1b, ln2g, ln2b)], axis=0)
    small = small + lax.ppermute(small, "tensor", [(i, i ^ 1) for i in range(tensor)])
    small = lax.psum_scatter(small, "dp", scatter_dimension=1, tiled=True)
    next(up)
    output = output_rows(line, 0, rows, *fourths[0], joined[0], rows_here, None)[0]
    next(up)
    output = output_rows(line, 1, rows, *fourths[1], joined[1], rows_here, output)[0]
    next(up)
    next(vgrad)
    next(out)
    next(out)
    next(out)
    line.last.append(small)
    next(out)
    next(qgrad)
    for _ in range(4):
        next(swish)
    next(kgrad)
    for _ in range(4):
        next(vgrad)
    for _ in range(4):
        next(qgrad)
    for left in (down, gate, up, out, swish, vgrad, qgrad, kgrad):
        for _ in left:
            pass
    return (
        output,
        grad_inputs,
        small[0],
        small[1],
        results["query"],
        results["key"],
        results["value"],
        results["swish"],
        results["out"],
        small[2],
        small[3],
        results["gate"],
        results["up"],
        results["down"],
    )


def solution(mesh):
    dp, tensor = mesh.shape["dp"], mesh.shape["tensor"]

    def body(*arrays):
        return on_device(dp, tensor, *arrays)

    return jax.shard_map(
        body,
        mesh=mesh,
        in_specs=(
            P("dp", None),
            P("dp", None),
            P("tensor"),
            P(),
            P(),
            P(None, "tensor"),
            P(None, "tensor"),
            P(None, "tensor"),
            P(None, "tensor"),
            P("tensor", None),
            P(),
            P(),
            P(None, "tensor"),
            P(None, "tensor"),
            P("tensor", None),
            P("dp", None),
        ),
        out_specs=(
            P("dp", None),
            P("dp", None),
            P("dp"),
            P("dp"),
            P("dp", "tensor"),
            P("dp", "tensor"),
            P("dp", "tensor"),
            P("dp", "tensor"),
            P("tensor", "dp"),
            P("dp"),
            P("dp"),
            P("dp", "tensor"),
            P("dp", "tensor"),
            P("tensor", "dp"),
        ),
        check_vma=False,
    )
```

```python
import functools

import jax
import jax.numpy as jnp
from jax import lax
from jax.experimental import pallas as pl
from jax.experimental.pallas import tpu as pltpu
from jax.sharding import PartitionSpec as P

KEY = 256
VALUE = 512
SEQ_LEN = 1024
DOC_MOST = 512
BLOCK = 256
CHUNKS = SEQ_LEN // BLOCK
HALF = BLOCK // 2
BF16 = jnp.bfloat16
F32 = jnp.float32
MIB = 1 << 20


def product_tn(left, right):
    return lax.dot_general(left, right, (((0,), (0,)), ((), ())), preferred_element_type=F32)


def product_nt(left, right):
    return lax.dot_general(left, right, (((1,), (1,)), ((), ())), preferred_element_type=F32)


def product_nn(left, right):
    return jnp.dot(left, right, preferred_element_type=F32)


def angle_tables(length):
    half_width = KEY // 2
    column = jnp.arange(KEY, dtype=jnp.int32) // 2
    frequency = jnp.power(10000.0, -column.astype(F32) / (half_width - 1))
    inside = jnp.arange(BLOCK, dtype=jnp.int32).astype(F32)[:, None] * frequency[None, :]
    starts = jnp.arange(0, length, BLOCK, dtype=jnp.int32).astype(F32)[:, None] * frequency[None, :]
    return jnp.cos(inside), jnp.sin(inside), jnp.cos(starts), jnp.sin(starts)


def rotate(values, cosines, sines, sign):
    even = lax.broadcasted_iota(jnp.int32, values.shape, 1) % 2 == 0
    after = pltpu.roll(values, KEY - 1, 1)
    before = pltpu.roll(values, 1, 1)
    return values * cosines + sign * jnp.where(even, -after, before) * sines


def normal_rows(values, eps):
    average = jnp.mean(values, axis=-1, keepdims=True)
    centred = values - average
    spread = jnp.mean(centred * centred, axis=-1, keepdims=True)
    return centred, lax.rsqrt(spread + eps)


def down_rows(seg):
    return jnp.transpose(jnp.broadcast_to(seg.astype(F32), (BLOCK, BLOCK)))


def decay_block(log_keep, seg_rows, seg, row_start, column_start):
    rows = row_start + lax.broadcasted_iota(jnp.int32, (BLOCK, BLOCK), 0)
    columns = column_start + lax.broadcasted_iota(jnp.int32, (BLOCK, BLOCK), 1)
    gap = rows - columns
    keep = (seg_rows == seg.astype(F32)) & (gap >= 0)
    return jnp.where(keep, jnp.exp(jnp.maximum(gap, 0).astype(F32) * log_keep), 0.0)


def first_key_block(chunk):
    return max(0, chunk - (DOC_MOST + BLOCK - 2) // BLOCK)


class Line:
    def __init__(self):
        self.last = []
        self.shared = 0

    def call(
        self,
        kernel,
        outs,
        out_specs,
        ins,
        in_specs,
        grid=(1,),
        scalars=None,
        scratch=(),
        vmem=63,
        onto=(),
        paired=False,
    ):
        held = list(ins) + [array for _, array in onto]
        extra = held[len(ins) :] + [array for array in self.last if not any(array is other for other in held)]
        scalar_count = 0 if scalars is None else 1
        in_count = len(ins)
        skipped = len(extra)

        def body(*refs):
            head, rest = refs[: scalar_count + in_count], refs[scalar_count + in_count + skipped :]
            kernel(*head, *rest)

        specs = list(in_specs) + [pl.BlockSpec(memory_space=pl.ANY)] * skipped
        arguments = ([] if scalars is None else [scalars]) + list(ins) + extra
        extras = {}
        if paired:
            extras = dict(collective_id=self.shared, has_side_effects=True)
            self.shared += 1
        result = pl.pallas_call(
            body,
            out_shape=tuple(outs),
            grid_spec=pltpu.PrefetchScalarGridSpec(
                num_scalar_prefetch=scalar_count,
                grid=grid,
                in_specs=specs,
                out_specs=tuple(out_specs),
                scratch_shapes=list(scratch),
            ),
            input_output_aliases={scalar_count + in_count + n: out for n, (out, _) in enumerate(onto)},
            compiler_params=pltpu.CompilerParams(
                vmem_limit_bytes=vmem * MIB,
                dimension_semantics=("arbitrary",) * len(grid),
                **extras,
            ),
            cost_estimate=pl.CostEstimate(flops=1, bytes_accessed=1, transcendentals=0),
        )(*arguments)
        self.last = [result[0]]
        return result


def my_core():
    return lax.rem(lax.axis_index("tensor"), 2)


def other_core():
    rank = lax.axis_index("tensor")
    return {"tensor": rank + 1 - 2 * lax.rem(rank, 2)}


def meet_other_core():
    barrier = pltpu.get_barrier_semaphore()
    pl.semaphore_signal(barrier, inc=1, device_id=other_core(), device_id_type=pl.DeviceIdType.MESH)
    pl.semaphore_wait(barrier, 1)


def to_other_core(source, target, sent, arrived):
    return pltpu.make_async_remote_copy(
        src_ref=source,
        dst_ref=target,
        send_sem=sent,
        recv_sem=arrived,
        device_id=other_core(),
        device_id_type=pl.DeviceIdType.MESH,
    )


def core_rows(mine, block):
    core = my_core() if mine else 1 - my_core()
    return pl.ds(pl.multiple_of(block * BLOCK + core * HALF, HALF), HALF)


def shape(dims, kind):
    return jax.ShapeDtypeStruct(dims, kind)


def const_spec(dims):
    return pl.BlockSpec(dims, lambda *_: (0,) * len(dims))


def once_spec(dims):
    return pl.BlockSpec(dims, lambda *_: (0,) * len(dims), pipeline_mode=pl.Buffered(1))


def row_spec(rows, columns, chunk):
    return pl.BlockSpec((rows, columns), lambda *_: (chunk, 0))


SMEM = pl.BlockSpec(memory_space=pltpu.SMEM)


def proj_kernel(
    begin, x, gain, bias, cos, sin, cos0, sin0, wq, wk, wv, ws, a_out, q_out, k_out, v_out, s_out, c_out, n_out
):
    chunk = begin + pl.program_id(0)
    centred, scale = normal_rows(x[...].astype(F32), 1e-05)
    normed = (centred * scale * gain[...] + bias[...]).astype(BF16)
    a_out[...] = normed
    first_cos, first_sin = cos0[pl.ds(chunk, 1), :], sin0[pl.ds(chunk, 1), :]
    cosines = cos[...] * first_cos - sin[...] * first_sin
    sines = sin[...] * first_cos + cos[...] * first_sin
    c_out[...] = cosines
    n_out[...] = sines
    query = product_nn(normed, wq[...])
    key = product_nn(normed, wk[...])
    for first in range(0, query.shape[1], KEY):
        part = slice(first, first + KEY)
        q_out[:, part] = rotate(query[:, part], cosines, sines, 1.0).astype(BF16)
        turned = rotate(key[:, part], cosines, sines, 1.0) * float(KEY) ** (-0.5)
        k_out[:, part] = turned.astype(BF16)
    v_out[...] = product_nn(normed, wv[...]).astype(BF16)
    s_out[...] = product_nn(normed, ws[...])


def projections(line, begin, end, x, gain, bias, tables, wq, wk, wv, ws, before):
    rows, width = x.shape
    kw, vw = wq.shape[1], wv.shape[1]
    wide = [(width, BF16), (kw, BF16), (kw, BF16), (vw, BF16), (vw, F32), (KEY, F32), (KEY, F32)]

    def chunked(columns):
        return pl.BlockSpec((BLOCK, columns), lambda i: (begin + i, 0))

    return line.call(
        functools.partial(proj_kernel, begin),
        [shape((rows, columns), kind) for columns, kind in wide],
        [chunked(columns) for columns, _ in wide],
        [x, gain, bias, *tables, wq, wk, wv, ws],
        [chunked(width), const_spec((1, width)), const_spec((1, width))]
        + [const_spec(table.shape) for table in tables]
        + [once_spec(w.shape) for w in (wq, wk, wv, ws)],
        grid=(end - begin,),
        onto=() if before is None else tuple(enumerate(before)),
    )


TILES = 4


def retain_kernel(chunk, q, k, v, switch, seg_row, logs, w, chip, u_out, o_out, p_out, full, sent, got, s1, s2):
    meet_other_core()
    seg_rows = down_rows(seg_row[:, chunk * BLOCK : (chunk + 1) * BLOCK])
    heads = q.shape[1] // KEY
    low = first_key_block(chunk)
    for head in range(heads):
        kpart, vpart = slice(head * KEY, (head + 1) * KEY), slice(head * VALUE, (head + 1) * VALUE)
        total = None
        for block in range(low, chunk + 1):
            rows = slice(block * BLOCK, (block + 1) * BLOCK)
            raw = product_nt(q[:, kpart], k[rows, kpart])
            mask = decay_block(logs[head], seg_rows, seg_row[:, rows], chunk * BLOCK, block * BLOCK)
            weights = (raw * mask).astype(BF16)
            p_out[head, :, (block - low) * BLOCK : (block - low + 1) * BLOCK] = weights
            part = product_nn(weights, v[rows, vpart])
            total = part if total is None else total + part
        o_out[:, vpart] = total
        centred, scale = normal_rows(total, 1.0)
        gate = switch[:, vpart]
        u_out[:, vpart] = (centred * scale * (gate * jax.nn.sigmoid(gate))).astype(BF16)
    tile = w.shape[1] // TILES
    copies = []
    for j in range(TILES):
        columns = slice(j * tile, (j + 1) * tile)
        full[:, columns] = product_nn(u_out[...], w[:, columns])
        sent[j] = full[core_rows(False, 0), columns]
        copies.append(to_other_core(sent.at[j], got.at[j], s1.at[j], s2.at[j]))
        copies[-1].start()
    for j in range(TILES):
        columns = slice(j * tile, (j + 1) * tile)
        copies[j].wait()
        chip[:, columns] = full[core_rows(True, 0), columns] + got[j]


def retention(line, chunk, q, k, v, switch, seg_row, logs, w, before):
    rows, kw = q.shape
    vw, width = v.shape[1], w.shape[1]
    heads = kw // KEY
    blocks = chunk + 1 - first_key_block(chunk)
    return line.call(
        functools.partial(retain_kernel, chunk),
        [
            shape((HALF, width), F32),
            shape((rows, vw), BF16),
            shape((rows, vw), F32),
            shape((heads, BLOCK, blocks * BLOCK), BF16),
        ],
        [
            const_spec((HALF, width)),
            row_spec(BLOCK, vw, chunk),
            row_spec(BLOCK, vw, chunk),
            const_spec((heads, BLOCK, blocks * BLOCK)),
        ],
        [q, k, v, switch, seg_row, logs, w],
        [
            row_spec(BLOCK, kw, chunk),
            const_spec(k.shape),
            const_spec(v.shape),
            row_spec(BLOCK, vw, chunk),
            const_spec(seg_row.shape),
            SMEM,
            const_spec(w.shape),
        ],
        scratch=[
            pltpu.VMEM((BLOCK, width), F32),
            pltpu.VMEM((TILES, HALF, width // TILES), F32),
            pltpu.VMEM((TILES, HALF, width // TILES), F32),
            pltpu.SemaphoreType.DMA((TILES,)),
            pltpu.SemaphoreType.DMA((TILES,)),
        ],
        onto=() if before is None else ((1, before[0]), (2, before[1])),
        paired=True,
    )


def feed_kernel(a, c, wg, wu, wd, hid_out, dg_out, du_out):
    gate = product_nn(a[...], wg[...])
    up = product_nn(a[...], wu[...])
    back = product_nt(c[...], wd[...])
    factor = 0.7978845608028654
    bent = jnp.tanh(factor * (gate + 0.044715 * (gate * gate * gate)))
    half = 0.5 * (1.0 + bent)
    active = gate * half
    slope = half + 0.5 * gate * (1.0 - bent * bent) * (factor * (1.0 + 3 * 0.044715 * gate * gate))
    hid_out[...] = (active * up).astype(BF16)
    dg_out[...] = (back * up * slope).astype(BF16)
    du_out[...] = (back * active).astype(BF16)


def feed_forward(line, chunk, rows, a, c, wg, wu, wd, before):
    width, ff = wg.shape
    tile = min(256, ff)
    whole = a.shape[0]
    return line.call(
        feed_kernel,
        [shape((whole, ff), BF16)] * 3,
        [pl.BlockSpec((rows, tile), lambda i: (chunk, i))] * 3,
        [a, c, wg, wu, wd],
        [
            row_spec(rows, width, chunk),
            row_spec(rows, width, chunk),
            pl.BlockSpec((width, tile), lambda i: (0, i)),
            pl.BlockSpec((width, tile), lambda i: (0, i)),
            pl.BlockSpec((tile, width), lambda i: (i, 0)),
        ],
        grid=(ff // tile,),
        onto=() if before is None else tuple(enumerate(before)),
    )


def chip_kernel(count, transposed, steps, *refs):
    lefts, rights = refs[:count], refs[count : 2 * count]
    out, full, kept, sent, got, s1, s2 = refs[2 * count :]
    half = kept.shape[1]
    j = pl.program_id(0)

    @pl.when(j == 0)
    def _():
        meet_other_core()

    @pl.when(j < steps)
    def _():
        total = None
        for left, right in zip(lefts, rights):
            part = product_nt(left[...], right[...]) if transposed else product_nn(left[...], right[...])
            total = part if total is None else total + part
        full[...] = total
        for n in range(half // HALF):
            part = slice(n * HALF, (n + 1) * HALF)
            sent[j, part] = full[core_rows(False, n), :]
            kept[j, part] = full[core_rows(True, n), :]
        to_other_core(sent.at[j], got.at[j], s1.at[j], s2.at[j]).start()

    @pl.when(j > 0)
    def _():
        to_other_core(sent.at[j - 1], got.at[j - 1], s1.at[j - 1], s2.at[j - 1]).wait()
        out[...] = kept[j - 1] + got[j - 1]


def chip_sum(line, rows, lefts, rights, transposed, chunk):
    width = rights[0].shape[0] if transposed else rights[0].shape[1]
    tile = 512
    steps = width // tile
    half = rows // 2
    right_specs = [
        pl.BlockSpec((tile, right.shape[1]), lambda i: (jnp.minimum(i, steps - 1), 0))
        if transposed
        else pl.BlockSpec((right.shape[0], tile), lambda i: (0, jnp.minimum(i, steps - 1)))
        for right in rights
    ]
    left_specs = [row_spec(rows, left.shape[1], chunk) for left in lefts]
    return line.call(
        functools.partial(chip_kernel, len(lefts), transposed, steps),
        [shape((half, width), F32)],
        [pl.BlockSpec((half, tile), lambda i: (0, jnp.maximum(i, 1) - 1))],
        list(lefts) + list(rights),
        left_specs + right_specs,
        grid=(steps + 1,),
        scratch=[
            pltpu.VMEM((rows, tile), F32),
            pltpu.VMEM((steps, half, tile), F32),
            pltpu.VMEM((steps, half, tile), F32),
            pltpu.VMEM((steps, half, tile), F32),
            pltpu.SemaphoreType.DMA((steps,)),
            pltpu.SemaphoreType.DMA((steps,)),
        ],
        paired=True,
    )[0]


def shared_kernel(work, in_count, *refs):
    ins, out = refs[:in_count], refs[in_count]
    extras, (sent, got, s1, s2) = refs[in_count + 1 : -4], refs[-4:]
    meet_other_core()
    copies = []
    for n in range(sent.shape[0] // HALF):
        part = pl.ds(n * HALF, HALF)
        value = work(n, part, core_rows(True, n), *ins, *extras)
        sent[part, :] = value
        copies.append(to_other_core(sent.at[part], got.at[part], s1.at[n], s2.at[n]))
        copies[-1].start()
        out[core_rows(True, n), :] = value.astype(out.dtype)
    for n, copy in enumerate(copies):
        copy.wait()
        out[core_rows(False, n), :] = got[pl.ds(n * HALF, HALF), :].astype(out.dtype)


def shared_rows(line, work, chunk, rows, ins, in_specs, kind, total_rows, width, extras, before):
    half = rows // 2
    return line.call(
        functools.partial(shared_kernel, work, len(ins)),
        [shape((total_rows, width), kind)] + [shape(dims, F32) for dims, _ in extras],
        [row_spec(rows, width, chunk)] + [spec for _, spec in extras],
        ins,
        in_specs,
        scratch=[
            pltpu.VMEM((half, width), F32),
            pltpu.VMEM((half, width), F32),
            pltpu.SemaphoreType.DMA((half // HALF,)),
            pltpu.SemaphoreType.DMA((half // HALF,)),
        ],
        onto=before,
        paired=True,
    )


def core_half_kernel(x, out):
    out[...] = x[core_rows(True, 0), :].astype(F32)


def core_half(line, x):
    rows, width = x.shape
    return line.call(
        core_half_kernel,
        [shape((rows // 2, width), F32)],
        [pl.BlockSpec((HALF, width), lambda i: (i, 0))],
        [x],
        [pl.BlockSpec((BLOCK, width), lambda i: (i, 0))],
        grid=(rows // BLOCK,),
    )[0]


def partner_work(n, part, rows, got, gain, bias):
    centred, scale = normal_rows(got[part, :], 1e-05)
    return (centred * scale * gain[...] + bias[...]).astype(BF16).astype(F32)


def partner_rows(line, got, gain, bias):
    half, width = got.shape
    specs = [const_spec(got.shape), const_spec((1, width)), const_spec((1, width))]
    return shared_rows(
        line, partner_work, 0, 2 * half, [got, gain, bias], specs, BF16, 2 * half, width, [], ()
    )[0]


def norm_work(n, part, rows, chip, crossed, x, gain, bias, h_out):
    middle = x[rows, :].astype(F32) + (chip[part, :] + crossed[part, :])
    h_out[part, :] = middle
    centred, scale = normal_rows(middle, 1e-05)
    return (centred * scale * gain[...] + bias[...]).astype(BF16).astype(F32)


def second_norm(line, chunk, rows, chip, crossed, x, gain, bias, before):
    total, width = x.shape
    half = rows // 2
    return shared_rows(
        line,
        norm_work,
        chunk,
        rows,
        [chip, crossed, x, gain, bias],
        [const_spec((half, width)), const_spec((half, width)), row_spec(rows, width, chunk)]
        + [const_spec((1, width))] * 2,
        BF16,
        total,
        width,
        [((total // 2, width), row_spec(half, width, chunk))],
        () if before is None else tuple(enumerate(before)),
    )


def norm_back(n, back, centred, scale, gain, gain_out, bias_out):
    normed = centred * scale
    one, two = jnp.sum(back * normed, axis=0, keepdims=True), jnp.sum(back, axis=0, keepdims=True)
    gain_out[...] = one if n == 0 else gain_out[...] + one
    bias_out[...] = two if n == 0 else bias_out[...] + two
    scaled = back * gain[...]
    first = jnp.mean(scaled, axis=-1, keepdims=True)
    second = jnp.mean(scaled * normed, axis=-1, keepdims=True)
    return scale * (scaled - first - normed * second)


def mid_work(n, part, rows, chip, crossed, h, gain, c, dh_out, gain_out, bias_out):
    centred, scale = normal_rows(h[part, :], 1e-05)
    back = chip[part, :] + crossed[part, :]
    value = c[rows, :].astype(F32) + norm_back(n, back, centred, scale, gain, gain_out, bias_out)
    dh_out[part, :] = value
    return value


def second_norm_back(line, chunk, rows, chip, crossed, h, gain, c, before):
    total, width = c.shape
    half = rows // 2
    owned = row_spec(half, width, chunk)
    return shared_rows(
        line,
        mid_work,
        chunk,
        rows,
        [chip, crossed, h, gain, c],
        [const_spec((half, width))] * 2 + [owned, const_spec((1, width)), row_spec(rows, width, chunk)],
        BF16,
        total,
        width,
        [((total // 2, width), owned)] + [((1, width), const_spec((1, width)))] * 2,
        () if before is None else ((0, before[0]), (1, before[1])),
    )


def first_work(n, part, rows, chip, crossed, x, gain, dh, gain_out, bias_out):
    centred, scale = normal_rows(x[rows, :].astype(F32), 1e-05)
    back = chip[part, :] + crossed[part, :]
    return dh[part, :] + norm_back(n, back, centred, scale, gain, gain_out, bias_out)


def first_norm_back(line, chunk, rows, chip, crossed, x, gain, dh, before):
    total, width = x.shape
    half = rows // 2
    return shared_rows(
        line,
        first_work,
        chunk,
        rows,
        [chip, crossed, x, gain, dh],
        [const_spec((half, width))] * 2
        + [row_spec(rows, width, chunk), const_spec((1, width)), row_spec(half, width, chunk)],
        F32,
        total,
        width,
        [((1, width), const_spec((1, width)))] * 2,
        () if before is None else ((0, before[0]),),
    )


def output_work(n, part, rows, chip, crossed, h):
    return h[part, :] + (chip[part, :] + crossed[part, :])


def output_rows(line, chunk, rows, chip, crossed, h, before):
    half_total, width = h.shape
    half = rows // 2
    return shared_rows(
        line,
        output_work,
        chunk,
        rows,
        [chip, crossed, h],
        [const_spec((half, width))] * 2 + [row_spec(half, width, chunk)],
        BF16,
        2 * half_total,
        width,
        [],
        () if before is None else ((0, before),),
    )[0]


def copy_kernel(source, out):
    out[...] = source[...]


def own_copy(line, source):
    rows, width = source.shape
    spec = pl.BlockSpec((BLOCK, width), lambda i: (i, 0))
    return line.call(copy_kernel, [shape(source.shape, source.dtype)], [spec], [source], [spec], grid=(rows // BLOCK,))[0]


def add_kernel(a, b, out):
    out[...] = a[...] + b[...]


def add(line, a, b):
    spec = const_spec(a.shape)
    return line.call(add_kernel, [shape(a.shape, F32)], [spec], [a, b], [spec, spec])[0]


def gate_kernel(dz, w, o, switch, do_out, ds_out):
    grad = product_nt(dz[...], w[...])
    centred, scale = normal_rows(o[...], 1.0)
    gate = switch[...]
    sig = jax.nn.sigmoid(gate)
    ds_out[...] = (grad * (centred * scale) * (sig * (1.0 + gate * (1.0 - sig)))).astype(BF16)
    dn = grad * (gate * sig)
    one = jnp.mean(dn, axis=-1, keepdims=True)
    two = jnp.mean(dn * centred, axis=-1, keepdims=True)
    do_out[...] = (scale * (dn - one) - (scale * scale * scale) * centred * two).astype(BF16)


def gate_back(line, dz, w, o, switch):
    rows, width = dz.shape
    vw = w.shape[0]
    part = 512
    tiled = pl.BlockSpec((part, VALUE), lambda h, i: (i, h))
    return line.call(
        gate_kernel,
        [shape((rows, vw), BF16)] * 2,
        [tiled] * 2,
        [dz, w, o, switch],
        [
            pl.BlockSpec((part, width), lambda h, i: (i, 0)),
            pl.BlockSpec((VALUE, width), lambda h, i: (h, 0)),
            tiled,
            tiled,
        ],
        grid=(vw // VALUE, rows // part),
    )


def retain_back_kernel(q, k, v, do, seg_row, logs, cos, sin, *rest):
    weights = rest[:CHUNKS]
    dq_out, dk_out, dv_out, both_out, dq_sum, dk_sum, dv_sum = rest[CHUNKS:]
    head = pl.program_id(0)
    dk_sum[...] = jnp.zeros_like(dk_sum)
    dv_sum[...] = jnp.zeros_like(dv_sum)
    for chunk in range(CHUNKS):
        low = first_key_block(chunk)
        here = slice(chunk * BLOCK, (chunk + 1) * BLOCK)
        seg_rows = down_rows(seg_row[:, here])
        total = None
        for block in range(low, chunk + 1):
            rows = slice(block * BLOCK, (block + 1) * BLOCK)
            part = slice((block - low) * BLOCK, (block - low + 1) * BLOCK)
            mask = decay_block(logs[head], seg_rows, seg_row[:, rows], chunk * BLOCK, block * BLOCK)
            scores = (product_nt(do[here, :], v[rows, :]) * mask).astype(BF16)
            dv_sum[rows, :] += product_tn(weights[chunk][0, :, part], do[here, :])
            dk_sum[rows, :] += product_tn(scores, q[here, :])
            term = product_nn(scores, k[rows, :])
            total = term if total is None else total + term
        dq_sum[here, :] = total
    dq = rotate(dq_sum[...], cos[...], sin[...], -1.0).astype(BF16)
    dk = (rotate(dk_sum[...], cos[...], sin[...], -1.0) * float(KEY) ** (-0.5)).astype(BF16)
    dq_out[...] = dq
    dk_out[...] = dk
    both_out[:, :KEY] = dq
    both_out[:, KEY:] = dk
    dv_out[...] = dv_sum[...].astype(BF16)


def retention_back(line, q, k, v, do, seg_row, logs, cos, sin, weights):
    rows, kw = q.shape
    vw = v.shape[1]

    def headed(columns):
        return pl.BlockSpec((rows, columns), lambda h: (0, h))

    return line.call(
        retain_back_kernel,
        [shape((rows, columns), BF16) for columns in (kw, kw, vw, 2 * kw)],
        [headed(KEY), headed(KEY), headed(VALUE), headed(2 * KEY)],
        [q, k, v, do, seg_row, logs, cos, sin] + list(weights),
        [
            headed(KEY),
            headed(KEY),
            headed(VALUE),
            headed(VALUE),
            const_spec(seg_row.shape),
            SMEM,
            const_spec(cos.shape),
            const_spec(sin.shape),
        ]
        + [pl.BlockSpec((1,) + part.shape[1:], lambda h: (h, 0, 0)) for part in weights],
        grid=(kw // KEY,),
        scratch=[pltpu.VMEM((rows, KEY), F32), pltpu.VMEM((rows, KEY), F32), pltpu.VMEM((rows, VALUE), F32)],
    )


def outer_place(where, position, groups):
    return lax.rem(where[1] + 2 * groups - 1 - position, groups)


def column_block(where, position, groups, own):
    return outer_place(where, position, groups) * 2 + (where[0] if own else 1 - where[0])


def plain_block(where, left, right, by_rows, groups, position, own, extra):
    width = (left if by_rows else right).shape[1] // (2 * groups)
    column = column_block(where, position, groups, own) * width
    if by_rows:
        return product_tn(lax.dynamic_slice_in_dim(left, column, width, 1), right)
    block = product_tn(left, lax.dynamic_slice_in_dim(right, column, width, 1))
    if extra:
        more = lax.dynamic_slice_in_dim(extra[0] + extra[1], column, width, 1)
        block = jnp.concatenate([block, more], axis=0)
    return block


def sent_kernel(where, left, right, *rest):
    extra, out = rest[:-1], rest[-1]
    rows = left.shape[1]
    out[0, :rows] = product_tn(left[...], right[...])
    if extra:
        out[0, rows:] = extra[0][...] + extra[1][...]


def sent_blocks(line, where, left, right, by_rows, groups, first, count, extra=()):
    width = (left if by_rows else right).shape[1] // (2 * groups)
    if width % 128:
        blocks = [plain_block(where, left, right, by_rows, groups, first + j, False, extra) for j in range(count)]
        return jnp.stack(blocks)
    rows = left.shape[0]
    moving = pl.BlockSpec((rows, width), lambda j, w: (0, column_block(w, first + j, groups, False)))
    more = extra[0].shape[0] if extra else 0
    block = (width, right.shape[1]) if by_rows else (left.shape[1] + more, width)
    specs = [moving if by_rows else const_spec(left.shape), const_spec(right.shape) if by_rows else moving]
    small = pl.BlockSpec((more, width), lambda j, w: (0, column_block(w, first + j, groups, False)))
    return line.call(
        sent_kernel,
        [shape((count,) + block, F32)],
        [pl.BlockSpec((1,) + block, lambda j, w: (j, 0, 0))],
        [left, right, *extra],
        specs + [small] * len(extra),
        grid=(count,),
        scalars=where,
    )[0]


def kept_kernel(has_travelling, extra_count, where, left, right, received, *rest):
    more, rest = rest[:extra_count], rest[extra_count:]
    total = product_tn(left[...], right[...])
    rows = total.shape[0]
    total = total + received[0, :rows]
    if has_travelling:
        total = total + rest[0][:rows]
    if not extra_count:
        rest[-1][...] = total
        return
    small = more[0][...] + more[1][...] + received[0, rows:]
    if has_travelling:
        small = small + rest[0][rows:]
    outs = rest[1:] if has_travelling else rest
    outs[0][:rows] = total
    if len(outs) == 2:
        outs[1][...] = small
    else:
        outs[0][rows:] = small


def kept_block(
    line, where, left, right, by_rows, groups, position, received, index, travelling, extra=(), last=False
):
    width = (left if by_rows else right).shape[1] // (2 * groups)
    if width % 128:
        block = plain_block(where, left, right, by_rows, groups, position, True, extra) + received[index]
        block = block if travelling is None else block + travelling
        return (block[: left.shape[1]], block[left.shape[1] :]) if extra and last else block
    if extra:
        return extended_block(line, where, left, right, groups, position, received, index, travelling, extra, last)
    rows, tiles = left.shape[0], 2
    moving = pl.BlockSpec((rows, width), lambda j, w: (0, column_block(w, position, groups, True)))
    if by_rows:
        part = right.shape[1] // tiles
        left_spec, right_spec = moving, pl.BlockSpec((rows, part), lambda j, w: (0, j))
        block, piece, at = (width, right.shape[1]), (width, part), lambda j: (0, j)
    else:
        part = left.shape[1] // tiles
        left_spec, right_spec = pl.BlockSpec((rows, part), lambda j, w: (0, j)), moving
        block, piece, at = (left.shape[1], width), (part, width), lambda j: (j, 0)
    flat = pl.BlockSpec(piece, lambda j, w: at(j))
    ins = [left, right, received] + ([] if travelling is None else [travelling])
    specs = [left_spec, right_spec, pl.BlockSpec((1,) + piece, lambda j, w: (index,) + at(j))]
    return line.call(
        functools.partial(kept_kernel, travelling is not None, 0),
        [shape(block, F32)],
        [flat],
        ins,
        specs + ([] if travelling is None else [flat]),
        grid=(tiles,),
        scalars=where,
    )[0]


def extended_block(line, where, left, right, groups, position, received, index, travelling, extra, last):
    width = right.shape[1] // (2 * groups)
    rows, more = left.shape[0], extra[0].shape[0]
    block = (left.shape[1] + more, width)
    moving = pl.BlockSpec((rows, width), lambda j, w: (0, column_block(w, position, groups, True)))
    small = pl.BlockSpec((more, width), lambda j, w: (0, column_block(w, position, groups, True)))
    ins = [left, right, received, *extra] + ([] if travelling is None else [travelling])
    specs = [const_spec(left.shape), moving, pl.BlockSpec((1,) + block, lambda j, w: (index, 0, 0)), small, small]
    outs = [(left.shape[1], width), (more, width)] if last else [block]
    result = line.call(
        functools.partial(kept_kernel, travelling is not None, len(extra)),
        [shape(dims, F32) for dims in outs],
        [const_spec(dims) for dims in outs],
        ins,
        specs + ([] if travelling is None else [const_spec(block)]),
        scalars=where,
    )
    return result if last else result[0]


def wide_kernel(pair_count, has_travelling, last, where, *refs):
    total = None
    for n in range(pair_count):
        part = product_tn(refs[2 * n][...], refs[2 * n + 1][...].astype(BF16))
        total = part if total is None else total + part
    rest = refs[2 * pair_count :]
    if has_travelling:
        total = total + rest[0][...]
        rest = rest[1:]
    if not last:
        rest[0][...] = total
        return
    send, keep, full = rest
    full[...] = total
    half = send.shape[0]
    keep[...] = full[pl.ds(pl.multiple_of(where[0] * half, half), half), :]
    send[...] = full[pl.ds(pl.multiple_of((1 - where[0]) * half, half), half), :]


def wide_block(line, where, pairs, groups, position, travelling, last, columns):
    rows, depth = pairs[0][0].shape
    width = depth // groups
    tiles = 2
    part = columns // tiles
    ins, specs = [], []
    for left, right in pairs:
        ins += [left, right]
        specs.append(pl.BlockSpec((rows, width), lambda j, w: (0, outer_place(w, position, groups))))
        if right.shape[1] > columns:
            specs.append(pl.BlockSpec((rows, part), lambda j, w: (0, w[0] * tiles + j)))
        else:
            specs.append(pl.BlockSpec((rows, part), lambda j, w: (0, j)))
    if travelling is not None:
        ins.append(travelling)
        specs.append(pl.BlockSpec((width, part), lambda j, w: (0, j)))
    height = width // 2 if last else width
    result = line.call(
        functools.partial(wide_kernel, len(pairs), travelling is not None, last),
        [shape((height, columns), F32)] * (2 if last else 1),
        [pl.BlockSpec((height, part), lambda j, w: (0, j))] * (2 if last else 1),
        ins,
        specs,
        grid=(tiles,),
        scalars=where,
        scratch=[pltpu.VMEM((width, part), F32)] if last else [],
    )
    return result if last else result[0]


def half_kernel(where, source, out):
    out[...] = source[...].astype(F32)


def neighbour_half(line, where, source):
    rows, columns = source.shape
    part = rows // 2
    return line.call(
        half_kernel,
        [shape((rows, columns // 2), F32)],
        [pl.BlockSpec((part, columns // 2), lambda i, w: (i, 0))],
        [source],
        [pl.BlockSpec((part, columns // 2), lambda i, w: (i, 1 - w[0]))],
        grid=(2,),
        scalars=where,
    )[0]


def join_kernel(where, keep, got, *outs):
    mine, theirs = keep[...], got[...]
    low = where[0] == 0
    first, second = jnp.where(low, mine, theirs), jnp.where(low, theirs, mine)
    part = first.shape[1] // len(outs)
    for n, out in enumerate(outs):
        out[:, :part] = first[:, n * part : (n + 1) * part]
        out[:, part:] = second[:, n * part : (n + 1) * part]


def join_halves(line, where, keep, got, count):
    rows, columns = keep.shape
    out = (rows, 2 * columns // count)
    return line.call(
        join_kernel,
        [shape(out, F32)] * count,
        [const_spec(out)] * count,
        [keep, got],
        [const_spec(keep.shape)] * 2,
        scalars=where,
    )


class Plan:
    def __init__(self, line):
        self.line, self.steps, self.found, self.sent = line, {}, {}, {}

    def step(self, name, needs, work):
        self.steps[name] = (needs, work)

    def run(self, *names):
        for name in names:
            if name.startswith("~"):
                if name[1:] in self.sent:
                    self.line.last.append(self.sent[name[1:]])
            elif name in self.steps and name not in self.found:
                needs, work = self.steps[name]
                self.run(*needs)
                self.found[name] = work()

    def __getitem__(self, name):
        return self.found[name]


def on_device(
    dp,
    tensor,
    inputs,
    segments,
    decay_order,
    ln1_gain,
    ln1_bias,
    w_query,
    w_key,
    w_value,
    w_swish,
    w_out,
    ln2_gain,
    ln2_bias,
    w_gate,
    w_up,
    w_down,
    cotangent,
):
    line = Line()
    plan = Plan(line)
    groups = dp // 2
    place = lax.axis_index("dp")
    where = jnp.stack([lax.rem(place, 2), lax.div(place, 2)]).astype(jnp.int32)
    tables = angle_tables(SEQ_LEN)
    logs = jnp.log1p(-jnp.exp2(-(decay_order + 5).astype(F32)))
    seg_row = segments.reshape(1, SEQ_LEN)
    gain1, bias1, gain2, bias2 = (v.reshape(1, -1) for v in (ln1_gain, ln1_bias, ln2_gain, ln2_bias))
    rows = 2 * BLOCK

    def beside(name, values):
        plan.sent[name] = lax.ppermute(values, "dp", [(i, i ^ 1) for i in range(dp)])
        return plan.sent[name]

    def onward(name, values):
        plan.sent[name] = lax.ppermute(values, "dp", [(i, (i + 2) % dp) for i in range(dp)])
        return plan.sent[name]

    def across(name, values):
        plan.sent[name] = lax.ppermute(values, "tensor", [(i, i ^ 2) for i in range(tensor)])
        return plan.sent[name]


    def projected(n, begin, end):
        before = plan["P0"] if n else None
        return projections(line, begin, end, inputs, gain1, bias1, tables, w_query, w_key, w_value, w_swish, before)

    def retained(i):
        a, q, k, v, switch, cos, sin = plan["P1" if i else "P0"]
        before = plan[f"R{i - 1}"][1:3] if i else None
        chip, u, o, p = retention(line, i, q, k, v, switch, seg_row, logs, w_out, before)
        return (chip, across(f"R{i}", chip)), u, o, p

    def normed(i):
        before = plan[f"N{i - 1}"] if i else None
        return second_norm(line, i, BLOCK, *plan[f"R{i}"][0], inputs, gain2, bias2, before)

    def fed(i):
        before = plan[f"F{i - 1}"] if i else None
        return feed_forward(line, i, BLOCK, plan[f"N{i}"][0], cotangent, w_gate, w_up, w_down, before)

    last = CHUNKS - 1
    plan.step("P0", [], lambda: projected(0, 0, 1))
    plan.step("R0", ["P0"], lambda: retained(0))
    plan.step("P1", ["R0"], lambda: projected(1, 1, CHUNKS))
    for i in range(CHUNKS):
        plan.step(f"R{i}", ["P1", f"R{i - 1}"] if i else ["P0"], lambda i=i: retained(i))
        plan.step(f"N{i}", [f"R{i}"] + ([f"N{i - 1}"] if i else []), lambda i=i: normed(i))
        plan.step(f"F{i}", [f"N{i}"] + ([f"F{i - 1}"] if i else []), lambda i=i: fed(i))
    plan.step("H", [], lambda: beside("H", core_half(line, inputs)))
    plan.step("G", ["H"], lambda: partner_rows(line, plan["H"], gain1, bias1))

    def first(n):
        return plan["P1"][n]


    def summed(name, lefts, rights, transposed, i):
        chip = chip_sum(line, rows, lefts, rights, transposed, i)
        return chip, across(f"{name}{i}", chip)

    pair = range(2)

    def second_sum(i):
        _, dg, du = plan[f"F{last}"]
        return summed("B", [dg, du], [w_gate, w_up], True, i)

    def middle_back(i):
        before = plan["M1"] if i == 0 else None
        return second_norm_back(line, i, rows, *plan[f"B{i}"], plan[f"N{last}"][1], gain2, cotangent, before)

    def first_sum(i):
        dq, dk, dv, _ = plan["AB"]
        return summed("C", [dq, dk, dv, plan["GB"][1]], [w_query, w_key, w_value, w_swish], True, i)

    def inputs_back(i):
        before = plan["I1"] if i == 0 else None
        return first_norm_back(line, i, rows, *plan[f"C{i}"], inputs, gain1, plan["M0"][1], before)

    def output_part(i):
        before = plan["O1"] if i == 0 else None
        return output_rows(line, i, rows, *plan[f"D{i}"], plan[f"N{last}"][1], before)

    def retention_grads():
        _, q, k, v, _, cos, sin = plan["P1"]
        weights = [plan[f"R{i}"][3] for i in range(CHUNKS)]
        return retention_back(line, q, k, v, plan["GB"][0], seg_row, logs, cos, sin, weights)

    for i in reversed(pair):
        after = [] if i else ["M1"]
        plan.step(f"B{i}", [f"F{last}"], lambda i=i: second_sum(i))
        plan.step(f"M{i}", [f"B{i}"] + after, lambda i=i: middle_back(i))
        plan.step(f"D{i}", [f"F{last}"], lambda i=i: summed("D", [plan[f"F{last}"][0]], [w_down], False, i))
        plan.step(f"O{i}", [f"D{i}"] + ([] if i else ["O1"]), lambda i=i: output_part(i))
    plan.step("GB", ["M0"], lambda: gate_back(line, plan["M0"][0], w_out, plan[f"R{last}"][2], first(4)))
    plan.step("AB", ["GB"], retention_grads)
    for i in reversed(pair):
        plan.step(f"C{i}", ["AB"], lambda i=i: first_sum(i))
        plan.step(f"I{i}", [f"C{i}", "M0"] + ([] if i else ["I1"]), lambda i=i: inputs_back(i))
    plan.step("CI", ["I0"], lambda: own_copy(line, plan["I0"][0]))
    plan.step("CO", ["O0"], lambda: own_copy(line, plan["O0"]))


    def small_sums():
        ln1 = [plan[f"I{i}"][n] for n in (1, 2) for i in pair]
        ln2 = [plan[f"M{i}"][n] for n in (2, 3) for i in pair]
        parts = ln1 + ln2
        own = [parts[2 * n] + parts[2 * n + 1] for n in range(4)]
        own = jnp.concatenate(own + [jnp.zeros((4, own[0].shape[1]), F32)], axis=0)
        plan.sent["L"] = lax.ppermute(own, "tensor", [(i, i ^ 1) for i in range(tensor)])
        return own, plan.sent["L"]

    plan.step("L", ["I0", "M0"], small_sums)


    def products(name, needs, operands, by_rows, extra=tuple):
        cut = (groups + 1) // 2

        def send(part, begin, end):
            left, right = operands()
            blocks = sent_blocks(line, where, left, right, by_rows, groups, begin, end - begin, extra())
            return beside(f"S{name}{part}", blocks)

        def ring(j):
            part, index = ("A", j) if j < cut else ("B", j - cut)
            travelling = plan[f"K{name}{j - 1}"] if j else None
            left, right = operands()
            received = plan[f"S{name}{part}"]
            block = kept_block(
                line, where, left, right, by_rows, groups, j, received, index, travelling, extra(), j == groups - 1
            )
            return onward(f"K{name}{j}", block) if j < groups - 1 else block

        plan.step(f"S{name}A", needs, lambda: send("A", 0, cut))
        plan.step(f"S{name}B", needs, lambda: send("B", cut, groups))
        for j in range(groups):
            before = [f"K{name}{j - 1}"] if j else []
            plan.step(f"K{name}{j}", [f"S{name}A" if j < cut else f"S{name}B"] + before, lambda j=j: ring(j))
        return lambda: plan[f"K{name}{groups - 1}"]


    def ring_first(name, needs, operands):
        def ring(j):
            travelling = plan[f"K{name}{j - 1}"] if j else None
            left, right = operands()
            block = wide_block(
                line, where, [(left, right)], groups, j, travelling, j == groups - 1, right.shape[1]
            )
            if j < groups - 1:
                return onward(f"K{name}{j}", block)
            return beside(f"K{name}{j}", block[0]), block[1]

        for j in range(groups):
            plan.step(f"K{name}{j}", [f"K{name}{j - 1}"] if j else needs, lambda j=j: ring(j))
        plan.step(f"E{name}", [f"K{name}{groups - 1}"], lambda: add(line, *plan[f"K{name}{groups - 1}"]))
        return lambda: plan[f"E{name}"]


    def shares(name, needs, operand, count):
        def ring(j):
            travelling = plan[f"J{name}{j - 1}"] if j else None
            right = operand()
            pairs = [(first(0), right), (plan["G"], plan[f"T{name}"])]
            block = wide_block(
                line, where, pairs, groups, j, travelling, j == groups - 1, right.shape[1] // 2
            )
            if j < groups - 1:
                return onward(f"J{name}{j}", block)
            return block[1], beside(f"J{name}{j}", block[0])

        plan.step(f"T{name}", needs, lambda: beside(f"T{name}", neighbour_half(line, where, operand())))
        for j in range(groups):
            plan.step(f"J{name}{j}", [f"T{name}", "G"] + ([f"J{name}{j - 1}"] if j else []), lambda j=j: ring(j))
        plan.step(f"E{name}", [f"J{name}{groups - 1}"], lambda: join_halves(line, where, *plan[f"J{name}{groups - 1}"], count))
        return lambda: plan[f"E{name}"]

    fed_all = lambda n: plan[f"F{last}"][n]
    normed2 = lambda: plan[f"N{last}"][0]
    down = products("d", [f"F{last}"], lambda: (fed_all(0), cotangent), False)
    gate = products("g", [f"F{last}"], lambda: (normed2(), fed_all(1)), True)
    up = ring_first("u", [f"F{last}"], lambda: (normed2(), fed_all(2)))
    out = products("o", ["M0", "L"], lambda: (plan[f"R{last}"][1], plan["M0"][0]), False, lambda: plan["L"])
    swish = shares("s", ["GB"], lambda: plan["GB"][1], 1)
    vgrad = shares("v", ["AB"], lambda: plan["AB"][2], 1)
    both = shares("q", ["AB"], lambda: plan["AB"][3], 2)

    plan.run(
        "P0", "R0", "P1", "R1", "N0", "R2", "R3", "F0", "N1", "F1", "H", "N2", "F2", "N3", "F3", "Ku0", "B1", "SdA",
        "B0", "Ku1", "SgA", "M1", "SdB", "G", "Kd0", "Ku2", "M0", "Kd1", "GB", "AB", "Ts", "Kg0", "C1", "Tv", "C0",
        "Ku3", "Kg1", "Tq", "Kd2", "Js0", "SgB", "~Kg1", "D1", "I1", "Kd3", "Jv0", "I0", "L", "Js1", "SoA", "Jv1",
        "Jq0", "Js2", "D0", "Jv2", "SoB", "Jq1", "~Js2", "Kg2", "Ko0", "O1", "Jq2", "Js3", "CI", "Ko1", "O0", "CO",
        "Jq3", "Eu", "Eq", "Ko2", "Es", "Jv3", "Ev", "Ko3", "Kg3",
    )
    plan.run(*plan.steps)
    query, key = both()
    grad_out, small = out()
    return (
        plan["CO"],
        plan["CI"],
        small[0],
        small[1],
        query,
        key,
        vgrad()[0],
        swish()[0],
        grad_out,
        small[2],
        small[3],
        gate(),
        up(),
        down(),
    )


def solution(mesh):
    dp, tensor = mesh.shape["dp"], mesh.shape["tensor"]

    def body(*arrays):
        return on_device(dp, tensor, *arrays)

    return jax.shard_map(
        body,
        mesh=mesh,
        in_specs=(
            P("dp", None),
            P("dp", None),
            P("tensor"),
            P(),
            P(),
            P(None, "tensor"),
            P(None, "tensor"),
            P(None, "tensor"),
            P(None, "tensor"),
            P("tensor", None),
            P(),
            P(),
            P(None, "tensor"),
            P(None, "tensor"),
            P("tensor", None),
            P("dp", None),
        ),
        out_specs=(
            P("dp", None),
            P("dp", None),
            P("dp"),
            P("dp"),
            P("dp", "tensor"),
            P("dp", "tensor"),
            P("dp", "tensor"),
            P("dp", "tensor"),
            P("tensor", "dp"),
            P("dp"),
            P("dp"),
            P("dp", "tensor"),
            P("dp", "tensor"),
            P("tensor", "dp"),
        ),
        check_vma=False,
    )
```

```python
import functools

import jax
import jax.numpy as jnp
from jax import lax
from jax.experimental import pallas as pl
from jax.experimental.pallas import tpu as pltpu
from jax.sharding import PartitionSpec as P

KEY = 256
VALUE = 512
SEQ_LEN = 1024
DOC_MOST = 512
BLOCK = 256
CHUNKS = SEQ_LEN // BLOCK
HALF = BLOCK // 2
BF16 = jnp.bfloat16
F32 = jnp.float32
MIB = 1 << 20


def product_tn(left, right):
    return lax.dot_general(left, right, (((0,), (0,)), ((), ())), preferred_element_type=F32)


def product_nt(left, right):
    return lax.dot_general(left, right, (((1,), (1,)), ((), ())), preferred_element_type=F32)


def product_nn(left, right):
    return jnp.dot(left, right, preferred_element_type=F32)


def angle_tables(length):
    half_width = KEY // 2
    column = jnp.arange(KEY, dtype=jnp.int32) // 2
    frequency = jnp.power(10000.0, -column.astype(F32) / (half_width - 1))
    inside = jnp.arange(BLOCK, dtype=jnp.int32).astype(F32)[:, None] * frequency[None, :]
    starts = jnp.arange(0, length, BLOCK, dtype=jnp.int32).astype(F32)[:, None] * frequency[None, :]
    return jnp.cos(inside), jnp.sin(inside), jnp.cos(starts), jnp.sin(starts)


def rotate(values, cosines, sines, sign):
    even = lax.broadcasted_iota(jnp.int32, values.shape, 1) % 2 == 0
    after = pltpu.roll(values, KEY - 1, 1)
    before = pltpu.roll(values, 1, 1)
    return values * cosines + sign * jnp.where(even, -after, before) * sines


def normal_rows(values, eps):
    average = jnp.mean(values, axis=-1, keepdims=True)
    centred = values - average
    spread = jnp.mean(centred * centred, axis=-1, keepdims=True)
    return centred, lax.rsqrt(spread + eps)


def down_rows(seg):
    return jnp.transpose(jnp.broadcast_to(seg.astype(F32), (BLOCK, BLOCK)))


def decay_block(log_keep, seg_rows, seg, row_start, column_start):
    rows = row_start + lax.broadcasted_iota(jnp.int32, (BLOCK, BLOCK), 0)
    columns = column_start + lax.broadcasted_iota(jnp.int32, (BLOCK, BLOCK), 1)
    gap = rows - columns
    keep = (seg_rows == seg.astype(F32)) & (gap >= 0)
    return jnp.where(keep, jnp.exp(jnp.maximum(gap, 0).astype(F32) * log_keep), 0.0)


def first_key_block(chunk):
    return max(0, chunk - (DOC_MOST + BLOCK - 2) // BLOCK)


class Line:
    def __init__(self):
        self.last = []
        self.shared = 0

    def call(
        self,
        kernel,
        outs,
        out_specs,
        ins,
        in_specs,
        grid=(1,),
        scalars=None,
        scratch=(),
        vmem=63,
        onto=(),
        paired=False,
    ):
        held = list(ins) + [array for _, array in onto]
        extra = held[len(ins) :] + [array for array in self.last if not any(array is other for other in held)]
        scalar_count = 0 if scalars is None else 1
        in_count = len(ins)
        skipped = len(extra)

        def body(*refs):
            head, rest = refs[: scalar_count + in_count], refs[scalar_count + in_count + skipped :]
            kernel(*head, *rest)

        specs = list(in_specs) + [pl.BlockSpec(memory_space=pl.ANY)] * skipped
        arguments = ([] if scalars is None else [scalars]) + list(ins) + extra
        extras = {}
        if paired:
            extras = dict(collective_id=self.shared, has_side_effects=True)
            self.shared += 1
        result = pl.pallas_call(
            body,
            out_shape=tuple(outs),
            grid_spec=pltpu.PrefetchScalarGridSpec(
                num_scalar_prefetch=scalar_count,
                grid=grid,
                in_specs=specs,
                out_specs=tuple(out_specs),
                scratch_shapes=list(scratch),
            ),
            input_output_aliases={scalar_count + in_count + n: out for n, (out, _) in enumerate(onto)},
            compiler_params=pltpu.CompilerParams(
                vmem_limit_bytes=vmem * MIB,
                dimension_semantics=("arbitrary",) * len(grid),
                **extras,
            ),
            cost_estimate=pl.CostEstimate(flops=1, bytes_accessed=1, transcendentals=0),
        )(*arguments)
        self.last = [result[0]]
        return result


def my_core():
    return lax.rem(lax.axis_index("tensor"), 2)


def other_core():
    rank = lax.axis_index("tensor")
    return {"tensor": rank + 1 - 2 * lax.rem(rank, 2)}


def meet_other_core():
    barrier = pltpu.get_barrier_semaphore()
    pl.semaphore_signal(barrier, inc=1, device_id=other_core(), device_id_type=pl.DeviceIdType.MESH)
    pl.semaphore_wait(barrier, 1)


def to_other_core(source, target, sent, arrived):
    return pltpu.make_async_remote_copy(
        src_ref=source,
        dst_ref=target,
        send_sem=sent,
        recv_sem=arrived,
        device_id=other_core(),
        device_id_type=pl.DeviceIdType.MESH,
    )


def core_rows(mine, block):
    core = my_core() if mine else 1 - my_core()
    return pl.ds(pl.multiple_of(block * BLOCK + core * HALF, HALF), HALF)


def shape(dims, kind):
    return jax.ShapeDtypeStruct(dims, kind)


def const_spec(dims):
    return pl.BlockSpec(dims, lambda *_: (0,) * len(dims))


def once_spec(dims):
    return pl.BlockSpec(dims, lambda *_: (0,) * len(dims), pipeline_mode=pl.Buffered(1))


def row_spec(rows, columns, chunk):
    return pl.BlockSpec((rows, columns), lambda *_: (chunk, 0))


SMEM = pl.BlockSpec(memory_space=pltpu.SMEM)
ANY = pl.BlockSpec(memory_space=pl.ANY)


def fetch_scratch(*arrays):
    return [pltpu.VMEM(a.shape, a.dtype) for a in arrays] + [pltpu.SemaphoreType.DMA((len(arrays),))]


def fetched(sources, held):
    places, done = held[:-1], held[-1]
    copies = [pltpu.make_async_copy(s, p, done.at[n]) for n, (s, p) in enumerate(zip(sources, places))]
    return places, copies


def proj_kernel(
    begin, x, gain, bias, cos, sin, cos0, sin0, wq, wk, wv, ws, a_out, q_out, k_out, v_out, s_out, c_out, n_out
):
    chunk = begin + pl.program_id(0)
    centred, scale = normal_rows(x[...].astype(F32), 1e-05)
    normed = (centred * scale * gain[...] + bias[...]).astype(BF16)
    a_out[...] = normed
    first_cos, first_sin = cos0[pl.ds(chunk, 1), :], sin0[pl.ds(chunk, 1), :]
    cosines = cos[...] * first_cos - sin[...] * first_sin
    sines = sin[...] * first_cos + cos[...] * first_sin
    c_out[...] = cosines
    n_out[...] = sines
    query = product_nn(normed, wq[...])
    key = product_nn(normed, wk[...])
    for first in range(0, query.shape[1], KEY):
        part = slice(first, first + KEY)
        q_out[:, part] = rotate(query[:, part], cosines, sines, 1.0).astype(BF16)
        turned = rotate(key[:, part], cosines, sines, 1.0) * float(KEY) ** (-0.5)
        k_out[:, part] = turned.astype(BF16)
    v_out[...] = product_nn(normed, wv[...]).astype(BF16)
    s_out[...] = product_nn(normed, ws[...])


def projections(line, begin, end, x, gain, bias, tables, wq, wk, wv, ws, before):
    rows, width = x.shape
    kw, vw = wq.shape[1], wv.shape[1]
    wide = [(width, BF16), (kw, BF16), (kw, BF16), (vw, BF16), (vw, F32), (KEY, F32), (KEY, F32)]

    def chunked(columns):
        return pl.BlockSpec((BLOCK, columns), lambda i: (begin + i, 0))

    return line.call(
        functools.partial(proj_kernel, begin),
        [shape((rows, columns), kind) for columns, kind in wide],
        [chunked(columns) for columns, _ in wide],
        [x, gain, bias, *tables, wq, wk, wv, ws],
        [chunked(width), const_spec((1, width)), const_spec((1, width))]
        + [const_spec(table.shape) for table in tables]
        + [once_spec(w.shape) for w in (wq, wk, wv, ws)],
        grid=(end - begin,),
        onto=() if before is None else tuple(enumerate(before)),
    )


TILES = 4


def retain_kernel(
    chunk, q, k, v, switch, seg_row, logs, w, chip, u_out, o_out, p_out, full, sent, got, s1, s2, *held
):
    (w,), (fetch,) = fetched((w,), held)
    fetch.start()
    meet_other_core()
    seg_rows = down_rows(seg_row[:, chunk * BLOCK : (chunk + 1) * BLOCK])
    heads = q.shape[1] // KEY
    low = first_key_block(chunk)
    for head in range(heads):
        kpart, vpart = slice(head * KEY, (head + 1) * KEY), slice(head * VALUE, (head + 1) * VALUE)
        total = None
        for block in range(low, chunk + 1):
            rows = slice(block * BLOCK, (block + 1) * BLOCK)
            raw = product_nt(q[:, kpart], k[rows, kpart])
            mask = decay_block(logs[head], seg_rows, seg_row[:, rows], chunk * BLOCK, block * BLOCK)
            weights = (raw * mask).astype(BF16)
            p_out[head, :, (block - low) * BLOCK : (block - low + 1) * BLOCK] = weights
            part = product_nn(weights, v[rows, vpart])
            total = part if total is None else total + part
        o_out[:, vpart] = total
        centred, scale = normal_rows(total, 1.0)
        gate = switch[:, vpart]
        u_out[:, vpart] = (centred * scale * (gate * jax.nn.sigmoid(gate))).astype(BF16)
    tile = w.shape[1] // TILES
    copies = []
    fetch.wait()
    for j in range(TILES):
        columns = slice(j * tile, (j + 1) * tile)
        full[:, columns] = product_nn(u_out[...], w[:, columns])
        sent[j] = full[core_rows(False, 0), columns]
        copies.append(to_other_core(sent.at[j], got.at[j], s1.at[j], s2.at[j]))
        copies[-1].start()
    for j in range(TILES):
        columns = slice(j * tile, (j + 1) * tile)
        copies[j].wait()
        chip[:, columns] = full[core_rows(True, 0), columns] + got[j]


def retention(line, chunk, q, k, v, switch, seg_row, logs, w, before):
    rows, kw = q.shape
    vw, width = v.shape[1], w.shape[1]
    heads = kw // KEY
    blocks = chunk + 1 - first_key_block(chunk)
    return line.call(
        functools.partial(retain_kernel, chunk),
        [
            shape((HALF, width), F32),
            shape((rows, vw), BF16),
            shape((rows, vw), F32),
            shape((heads, BLOCK, blocks * BLOCK), BF16),
        ],
        [
            const_spec((HALF, width)),
            row_spec(BLOCK, vw, chunk),
            row_spec(BLOCK, vw, chunk),
            const_spec((heads, BLOCK, blocks * BLOCK)),
        ],
        [q, k, v, switch, seg_row, logs, w],
        [
            row_spec(BLOCK, kw, chunk),
            const_spec(k.shape),
            const_spec(v.shape),
            row_spec(BLOCK, vw, chunk),
            const_spec(seg_row.shape),
            SMEM,
            ANY,
        ],
        scratch=[
            pltpu.VMEM((BLOCK, width), F32),
            pltpu.VMEM((TILES, HALF, width // TILES), F32),
            pltpu.VMEM((TILES, HALF, width // TILES), F32),
            pltpu.SemaphoreType.DMA((TILES,)),
            pltpu.SemaphoreType.DMA((TILES,)),
            *fetch_scratch(w),
        ],
        onto=() if before is None else ((1, before[0]), (2, before[1])),
        paired=True,
    )


def feed_kernel(
    chip, crossed, x, gain, bias, c, wg, wu, wd, hid_out, dg_out, du_out, a_out, h_out, sent, got, s1, s2
):
    copy = to_other_core(sent, got, s1, s2)
    begin = pl.program_id(0) == 0

    @pl.when(begin)
    def _():
        meet_other_core()
        middle = x[core_rows(True, 0), :].astype(F32) + (chip[...] + crossed[...])
        h_out[...] = middle
        centred, scale = normal_rows(middle, 1e-05)
        normed = (centred * scale * gain[...] + bias[...]).astype(BF16)
        sent[...] = normed.astype(F32)
        copy.start()
        a_out[core_rows(True, 0), :] = normed

    back = product_nt(c[...], wd[...])

    @pl.when(begin)
    def _():
        copy.wait()
        a_out[core_rows(False, 0), :] = got[...].astype(BF16)

    gate = product_nn(a_out[...], wg[...])
    up = product_nn(a_out[...], wu[...])
    factor = 0.7978845608028654
    bent = jnp.tanh(factor * (gate + 0.044715 * (gate * gate * gate)))
    half = 0.5 * (1.0 + bent)
    active = gate * half
    slope = half + 0.5 * gate * (1.0 - bent * bent) * (factor * (1.0 + 3 * 0.044715 * gate * gate))
    hid_out[...] = (active * up).astype(BF16)
    dg_out[...] = (back * up * slope).astype(BF16)
    du_out[...] = (back * active).astype(BF16)


def feed_forward(line, chunk, chip, crossed, x, gain, bias, c, wg, wu, wd, before):
    total, width = x.shape
    ff = wg.shape[1]
    tile = min(256, ff)
    return line.call(
        feed_kernel,
        [shape((total, ff), BF16)] * 3 + [shape((total, width), BF16), shape((total // 2, width), F32)],
        [pl.BlockSpec((BLOCK, tile), lambda i: (chunk, i))] * 3
        + [row_spec(BLOCK, width, chunk), row_spec(HALF, width, chunk)],
        [chip, crossed, x, gain, bias, c, wg, wu, wd],
        [
            const_spec((HALF, width)),
            const_spec((HALF, width)),
            row_spec(BLOCK, width, chunk),
            const_spec((1, width)),
            const_spec((1, width)),
            row_spec(BLOCK, width, chunk),
            pl.BlockSpec((width, tile), lambda i: (0, i)),
            pl.BlockSpec((width, tile), lambda i: (0, i)),
            pl.BlockSpec((tile, width), lambda i: (i, 0)),
        ],
        grid=(ff // tile,),
        scratch=[
            pltpu.VMEM((HALF, width), F32),
            pltpu.VMEM((HALF, width), F32),
            pltpu.SemaphoreType.DMA,
            pltpu.SemaphoreType.DMA,
        ],
        onto=() if before is None else tuple(enumerate(before)),
        paired=True,
    )


def chip_kernel(count, transposed, steps, *refs):
    lefts, rights = refs[:count], refs[count : 2 * count]
    out, full, kept, sent, got, s1, s2 = refs[2 * count :]
    half = kept.shape[1]
    j = pl.program_id(0)

    @pl.when(j == 0)
    def _():
        meet_other_core()

    @pl.when(j < steps)
    def _():
        total = None
        for left, right in zip(lefts, rights):
            part = product_nt(left[...], right[...]) if transposed else product_nn(left[...], right[...])
            total = part if total is None else total + part
        full[...] = total
        for n in range(half // HALF):
            part = slice(n * HALF, (n + 1) * HALF)
            sent[j, part] = full[core_rows(False, n), :]
            kept[j, part] = full[core_rows(True, n), :]
        to_other_core(sent.at[j], got.at[j], s1.at[j], s2.at[j]).start()

    @pl.when(j > 0)
    def _():
        to_other_core(sent.at[j - 1], got.at[j - 1], s1.at[j - 1], s2.at[j - 1]).wait()
        out[...] = kept[j - 1] + got[j - 1]


def chip_sum(line, rows, lefts, rights, transposed, chunk):
    width = rights[0].shape[0] if transposed else rights[0].shape[1]
    tile = 512
    steps = width // tile
    half = rows // 2
    right_specs = [
        pl.BlockSpec((tile, right.shape[1]), lambda i: (jnp.minimum(i, steps - 1), 0))
        if transposed
        else pl.BlockSpec((right.shape[0], tile), lambda i: (0, jnp.minimum(i, steps - 1)))
        for right in rights
    ]
    left_specs = [row_spec(rows, left.shape[1], chunk) for left in lefts]
    return line.call(
        functools.partial(chip_kernel, len(lefts), transposed, steps),
        [shape((half, width), F32)],
        [pl.BlockSpec((half, tile), lambda i: (0, jnp.maximum(i, 1) - 1))],
        list(lefts) + list(rights),
        left_specs + right_specs,
        grid=(steps + 1,),
        scratch=[
            pltpu.VMEM((rows, tile), F32),
            pltpu.VMEM((steps, half, tile), F32),
            pltpu.VMEM((steps, half, tile), F32),
            pltpu.VMEM((steps, half, tile), F32),
            pltpu.SemaphoreType.DMA((steps,)),
            pltpu.SemaphoreType.DMA((steps,)),
        ],
        paired=True,
    )[0]


def shared_kernel(work, in_count, *refs):
    ins, out = refs[:in_count], refs[in_count]
    extras, (sent, got, s1, s2) = refs[in_count + 1 : -4], refs[-4:]
    meet_other_core()
    copies = []
    for n in range(sent.shape[0] // HALF):
        part = pl.ds(n * HALF, HALF)
        value = work(n, part, core_rows(True, n), *ins, *extras)
        sent[part, :] = value
        copies.append(to_other_core(sent.at[part], got.at[part], s1.at[n], s2.at[n]))
        copies[-1].start()
        out[core_rows(True, n), :] = value.astype(out.dtype)
    for n, copy in enumerate(copies):
        copy.wait()
        out[core_rows(False, n), :] = got[pl.ds(n * HALF, HALF), :].astype(out.dtype)


def shared_rows(line, work, chunk, rows, ins, in_specs, kind, total_rows, width, extras, before):
    half = rows // 2
    return line.call(
        functools.partial(shared_kernel, work, len(ins)),
        [shape((total_rows, width), kind)] + [shape(dims, F32) for dims, _ in extras],
        [row_spec(rows, width, chunk)] + [spec for _, spec in extras],
        ins,
        in_specs,
        scratch=[
            pltpu.VMEM((half, width), F32),
            pltpu.VMEM((half, width), F32),
            pltpu.SemaphoreType.DMA((half // HALF,)),
            pltpu.SemaphoreType.DMA((half // HALF,)),
        ],
        onto=before,
        paired=True,
    )


def core_half_kernel(x, out):
    out[...] = x[core_rows(True, 0), :].astype(F32)


def core_half(line, x):
    rows, width = x.shape
    return line.call(
        core_half_kernel,
        [shape((rows // 2, width), F32)],
        [pl.BlockSpec((HALF, width), lambda i: (i, 0))],
        [x],
        [pl.BlockSpec((BLOCK, width), lambda i: (i, 0))],
        grid=(rows // BLOCK,),
    )[0]


def partner_work(n, part, rows, got, gain, bias):
    centred, scale = normal_rows(got[part, :], 1e-05)
    return (centred * scale * gain[...] + bias[...]).astype(BF16).astype(F32)


def partner_rows(line, got, gain, bias):
    half, width = got.shape
    specs = [const_spec(got.shape), const_spec((1, width)), const_spec((1, width))]
    return shared_rows(
        line, partner_work, 0, 2 * half, [got, gain, bias], specs, BF16, 2 * half, width, [], ()
    )[0]


def norm_back(n, back, centred, scale, gain, gain_out, bias_out):
    normed = centred * scale
    one, two = jnp.sum(back * normed, axis=0, keepdims=True), jnp.sum(back, axis=0, keepdims=True)
    gain_out[...] = one if n == 0 else gain_out[...] + one
    bias_out[...] = two if n == 0 else bias_out[...] + two
    scaled = back * gain[...]
    first = jnp.mean(scaled, axis=-1, keepdims=True)
    second = jnp.mean(scaled * normed, axis=-1, keepdims=True)
    return scale * (scaled - first - normed * second)


def mid_work(n, part, rows, chip, crossed, h, gain, c, dh_out, gain_out, bias_out):
    centred, scale = normal_rows(h[part, :], 1e-05)
    back = chip[part, :] + crossed[part, :]
    value = c[rows, :].astype(F32) + norm_back(n, back, centred, scale, gain, gain_out, bias_out)
    dh_out[part, :] = value
    return value


def second_norm_back(line, chunk, rows, chip, crossed, h, gain, c, before):
    total, width = c.shape
    half = rows // 2
    owned = row_spec(half, width, chunk)
    return shared_rows(
        line,
        mid_work,
        chunk,
        rows,
        [chip, crossed, h, gain, c],
        [const_spec((half, width))] * 2 + [owned, const_spec((1, width)), row_spec(rows, width, chunk)],
        BF16,
        total,
        width,
        [((total // 2, width), owned)] + [((1, width), const_spec((1, width)))] * 2,
        () if before is None else ((0, before[0]), (1, before[1])),
    )


def first_work(n, part, rows, chip, crossed, x, gain, dh, gain_out, bias_out):
    centred, scale = normal_rows(x[rows, :].astype(F32), 1e-05)
    back = chip[part, :] + crossed[part, :]
    return dh[part, :] + norm_back(n, back, centred, scale, gain, gain_out, bias_out)


def first_norm_back(line, chunk, rows, chip, crossed, x, gain, dh, before):
    total, width = x.shape
    half = rows // 2
    return shared_rows(
        line,
        first_work,
        chunk,
        rows,
        [chip, crossed, x, gain, dh],
        [const_spec((half, width))] * 2
        + [row_spec(rows, width, chunk), const_spec((1, width)), row_spec(half, width, chunk)],
        F32,
        total,
        width,
        [((1, width), const_spec((1, width)))] * 2,
        () if before is None else ((0, before[0]),),
    )


def output_work(n, part, rows, chip, crossed, h):
    return h[part, :] + (chip[part, :] + crossed[part, :])


def output_rows(line, chunk, rows, chip, crossed, h, before):
    half_total, width = h.shape
    half = rows // 2
    return shared_rows(
        line,
        output_work,
        chunk,
        rows,
        [chip, crossed, h],
        [const_spec((half, width))] * 2 + [row_spec(half, width, chunk)],
        BF16,
        2 * half_total,
        width,
        [],
        () if before is None else ((0, before),),
    )[0]


def copy_kernel(source, out):
    out[...] = source[...]


def own_copy(line, source):
    rows, width = source.shape
    spec = pl.BlockSpec((BLOCK, width), lambda i: (i, 0))
    return line.call(copy_kernel, [shape(source.shape, source.dtype)], [spec], [source], [spec], grid=(rows // BLOCK,))[0]


def add_kernel(a, b, out):
    out[...] = a[...] + b[...]


def add(line, a, b):
    spec = const_spec(a.shape)
    return line.call(add_kernel, [shape(a.shape, F32)], [spec], [a, b], [spec, spec])[0]


def gate_kernel(dz, w, o, switch, do_out, ds_out):
    grad = product_nt(dz[...], w[...])
    centred, scale = normal_rows(o[...], 1.0)
    gate = switch[...]
    sig = jax.nn.sigmoid(gate)
    ds_out[...] = (grad * (centred * scale) * (sig * (1.0 + gate * (1.0 - sig)))).astype(BF16)
    dn = grad * (gate * sig)
    one = jnp.mean(dn, axis=-1, keepdims=True)
    two = jnp.mean(dn * centred, axis=-1, keepdims=True)
    do_out[...] = (scale * (dn - one) - (scale * scale * scale) * centred * two).astype(BF16)


def gate_back(line, dz, w, o, switch):
    rows, width = dz.shape
    vw = w.shape[0]
    part = 512
    tiled = pl.BlockSpec((part, VALUE), lambda h, i: (i, h))
    return line.call(
        gate_kernel,
        [shape((rows, vw), BF16)] * 2,
        [tiled] * 2,
        [dz, w, o, switch],
        [
            pl.BlockSpec((part, width), lambda h, i: (i, 0)),
            pl.BlockSpec((VALUE, width), lambda h, i: (h, 0)),
            tiled,
            tiled,
        ],
        grid=(vw // VALUE, rows // part),
    )


def retain_back_kernel(q, k, v, do, seg_row, logs, cos, sin, *rest):
    weights = rest[:CHUNKS]
    dq_out, dk_out, dv_out, both_out, dq_sum, dk_sum, dv_sum = rest[CHUNKS:]
    head = pl.program_id(0)
    dk_sum[...] = jnp.zeros_like(dk_sum)
    dv_sum[...] = jnp.zeros_like(dv_sum)
    for chunk in range(CHUNKS):
        low = first_key_block(chunk)
        here = slice(chunk * BLOCK, (chunk + 1) * BLOCK)
        seg_rows = down_rows(seg_row[:, here])
        total = None
        for block in range(low, chunk + 1):
            rows = slice(block * BLOCK, (block + 1) * BLOCK)
            part = slice((block - low) * BLOCK, (block - low + 1) * BLOCK)
            mask = decay_block(logs[head], seg_rows, seg_row[:, rows], chunk * BLOCK, block * BLOCK)
            scores = (product_nt(do[here, :], v[rows, :]) * mask).astype(BF16)
            dv_sum[rows, :] += product_tn(weights[chunk][0, :, part], do[here, :])
            dk_sum[rows, :] += product_tn(scores, q[here, :])
            term = product_nn(scores, k[rows, :])
            total = term if total is None else total + term
        dq_sum[here, :] = total
    dq = rotate(dq_sum[...], cos[...], sin[...], -1.0).astype(BF16)
    dk = (rotate(dk_sum[...], cos[...], sin[...], -1.0) * float(KEY) ** (-0.5)).astype(BF16)
    dq_out[...] = dq
    dk_out[...] = dk
    both_out[:, :KEY] = dq
    both_out[:, KEY:] = dk
    dv_out[...] = dv_sum[...].astype(BF16)


def retention_back(line, q, k, v, do, seg_row, logs, cos, sin, weights):
    rows, kw = q.shape
    vw = v.shape[1]

    def headed(columns):
        return pl.BlockSpec((rows, columns), lambda h: (0, h))

    return line.call(
        retain_back_kernel,
        [shape((rows, columns), BF16) for columns in (kw, kw, vw, 2 * kw)],
        [headed(KEY), headed(KEY), headed(VALUE), headed(2 * KEY)],
        [q, k, v, do, seg_row, logs, cos, sin] + list(weights),
        [
            headed(KEY),
            headed(KEY),
            headed(VALUE),
            headed(VALUE),
            const_spec(seg_row.shape),
            SMEM,
            const_spec(cos.shape),
            const_spec(sin.shape),
        ]
        + [pl.BlockSpec((1,) + part.shape[1:], lambda h: (h, 0, 0)) for part in weights],
        grid=(kw // KEY,),
        scratch=[pltpu.VMEM((rows, KEY), F32), pltpu.VMEM((rows, KEY), F32), pltpu.VMEM((rows, VALUE), F32)],
    )


def outer_place(where, position, groups):
    return lax.rem(where[1] + 2 * groups - 1 - position, groups)


def column_block(where, position, groups, own):
    return outer_place(where, position, groups) * 2 + (where[0] if own else 1 - where[0])


def plain_block(where, left, right, by_rows, groups, position, own, extra, skip):
    width = (left if by_rows else right).shape[1] // (2 * groups)
    column = column_block(where, position, groups, own) * width
    if by_rows:
        return product_tn(lax.dynamic_slice_in_dim(left, column, width, 1), right[:, skip:])
    block = product_tn(left, lax.dynamic_slice_in_dim(right, column, width, 1))
    if extra:
        more = lax.dynamic_slice_in_dim(extra[0] + extra[1], column, width, 1)
        block = jnp.concatenate([block, more], axis=0)
    return block


def sent_kernel(where, left, right, *rest):
    extra, out = rest[:-1], rest[-1]
    rows = left.shape[1]
    out[0, :rows] = product_tn(left[...], right[...])
    if extra:
        out[0, rows:] = extra[0][...] + extra[1][...]


def sent_blocks(line, where, left, right, by_rows, groups, first, count, extra=(), skip=0):
    width = (left if by_rows else right).shape[1] // (2 * groups)
    if width % 128:
        blocks = [plain_block(where, left, right, by_rows, groups, first + j, False, extra, skip) for j in range(count)]
        return jnp.stack(blocks)
    rows = left.shape[0]
    moving = pl.BlockSpec((rows, width), lambda j, w: (0, column_block(w, first + j, groups, False)))
    more = extra[0].shape[0] if extra else 0
    columns = right.shape[1] - skip
    block = (width, columns) if by_rows else (left.shape[1] + more, width)
    fixed = pl.BlockSpec((rows, columns), lambda j, w: (0, skip // columns))
    specs = [moving if by_rows else const_spec(left.shape), fixed if by_rows else moving]
    small = pl.BlockSpec((more, width), lambda j, w: (0, column_block(w, first + j, groups, False)))
    return line.call(
        sent_kernel,
        [shape((count,) + block, F32)],
        [pl.BlockSpec((1,) + block, lambda j, w: (j, 0, 0))],
        [left, right, *extra],
        specs + [small] * len(extra),
        grid=(count,),
        scalars=where,
    )[0]


def kept_kernel(has_travelling, extra_count, where, left, right, received, *rest):
    more, rest = rest[:extra_count], rest[extra_count:]
    total = product_tn(left[...], right[...])
    rows = total.shape[0]
    total = total + received[0, :rows]
    if has_travelling:
        total = total + rest[0][:rows]
    if not extra_count:
        rest[-1][...] = total
        return
    small = more[0][...] + more[1][...] + received[0, rows:]
    if has_travelling:
        small = small + rest[0][rows:]
    outs = rest[1:] if has_travelling else rest
    outs[0][:rows] = total
    if len(outs) == 2:
        outs[1][...] = small
    else:
        outs[0][rows:] = small


def kept_block(
    line, where, left, right, by_rows, groups, position, received, index, travelling, extra=(), last=False, skip=0
):
    width = (left if by_rows else right).shape[1] // (2 * groups)
    if width % 128:
        block = plain_block(where, left, right, by_rows, groups, position, True, extra, skip) + received[index]
        block = block if travelling is None else block + travelling
        return (block[: left.shape[1]], block[left.shape[1] :]) if extra and last else block
    if extra:
        return extended_block(line, where, left, right, groups, position, received, index, travelling, extra, last)
    rows, columns = left.shape[0], right.shape[1] - skip
    tiles = 1 if skip else 2
    moving = pl.BlockSpec((rows, width), lambda j, w: (0, column_block(w, position, groups, True)))
    if by_rows:
        part = columns // tiles
        left_spec, right_spec = moving, pl.BlockSpec((rows, part), lambda j, w: (0, skip // part + j))
        block, piece, at = (width, columns), (width, part), lambda j: (0, j)
    else:
        part = left.shape[1] // tiles
        left_spec, right_spec = pl.BlockSpec((rows, part), lambda j, w: (0, j)), moving
        block, piece, at = (left.shape[1], width), (part, width), lambda j: (j, 0)
    flat = pl.BlockSpec(piece, lambda j, w: at(j))
    ins = [left, right, received] + ([] if travelling is None else [travelling])
    specs = [left_spec, right_spec, pl.BlockSpec((1,) + piece, lambda j, w: (index,) + at(j))]
    return line.call(
        functools.partial(kept_kernel, travelling is not None, 0),
        [shape(block, F32)],
        [flat],
        ins,
        specs + ([] if travelling is None else [flat]),
        grid=(tiles,),
        scalars=where,
    )[0]


def extended_block(line, where, left, right, groups, position, received, index, travelling, extra, last):
    width = right.shape[1] // (2 * groups)
    rows, more = left.shape[0], extra[0].shape[0]
    block = (left.shape[1] + more, width)
    moving = pl.BlockSpec((rows, width), lambda j, w: (0, column_block(w, position, groups, True)))
    small = pl.BlockSpec((more, width), lambda j, w: (0, column_block(w, position, groups, True)))
    ins = [left, right, received, *extra] + ([] if travelling is None else [travelling])
    specs = [const_spec(left.shape), moving, pl.BlockSpec((1,) + block, lambda j, w: (index, 0, 0)), small, small]
    outs = [(left.shape[1], width), (more, width)] if last else [block]
    result = line.call(
        functools.partial(kept_kernel, travelling is not None, len(extra)),
        [shape(dims, F32) for dims in outs],
        [const_spec(dims) for dims in outs],
        ins,
        specs + ([] if travelling is None else [const_spec(block)]),
        scalars=where,
    )
    return result if last else result[0]


def wide_kernel(pair_count, has_travelling, last, where, *refs):
    total = None
    for n in range(pair_count):
        part = product_tn(refs[2 * n][...], refs[2 * n + 1][...].astype(BF16))
        total = part if total is None else total + part
    rest = refs[2 * pair_count :]
    if has_travelling:
        total = total + rest[0][...]
        rest = rest[1:]
    if not last:
        rest[0][...] = total
        return
    send, keep, full = rest
    full[...] = total
    half = send.shape[0]
    keep[...] = full[pl.ds(pl.multiple_of(where[0] * half, half), half), :]
    send[...] = full[pl.ds(pl.multiple_of((1 - where[0]) * half, half), half), :]


def wide_block(line, where, pairs, groups, position, travelling, last, columns, shared):
    rows, depth = pairs[0][0].shape
    width = depth // groups
    tiles = 2
    part = columns // tiles
    ins, specs = [], []
    for left, right in pairs:
        ins += [left, right]
        specs.append(pl.BlockSpec((rows, width), lambda j, w: (0, outer_place(w, position, groups))))
        if shared and right.shape[1] > columns:
            specs.append(pl.BlockSpec((rows, part), lambda j, w: (0, w[0] * tiles + j)))
        else:
            specs.append(pl.BlockSpec((rows, part), lambda j, w: (0, j)))
    if travelling is not None:
        ins.append(travelling)
        specs.append(pl.BlockSpec((width, part), lambda j, w: (0, j)))
    height = width // 2 if last else width
    result = line.call(
        functools.partial(wide_kernel, len(pairs), travelling is not None, last),
        [shape((height, columns), F32)] * (2 if last else 1),
        [pl.BlockSpec((height, part), lambda j, w: (0, j))] * (2 if last else 1),
        ins,
        specs,
        grid=(tiles,),
        scalars=where,
        scratch=[pltpu.VMEM((width, part), F32)] if last else [],
    )
    return result if last else result[0]


def half_kernel(where, source, out):
    out[...] = source[...].astype(F32)


def neighbour_half(line, where, source):
    rows, columns = source.shape
    part = rows // 2
    return line.call(
        half_kernel,
        [shape((rows, columns // 2), F32)],
        [pl.BlockSpec((part, columns // 2), lambda i, w: (i, 0))],
        [source],
        [pl.BlockSpec((part, columns // 2), lambda i, w: (i, 1 - w[0]))],
        grid=(2,),
        scalars=where,
    )[0]


def join_kernel(where, keep, got, *outs):
    mine, theirs = keep[...], got[...]
    low = where[0] == 0
    first, second = jnp.where(low, mine, theirs), jnp.where(low, theirs, mine)
    part = first.shape[1] // len(outs)
    for n, out in enumerate(outs):
        out[:, :part] = first[:, n * part : (n + 1) * part]
        out[:, part:] = second[:, n * part : (n + 1) * part]


def join_halves(line, where, keep, got, count):
    rows, columns = keep.shape
    out = (rows, 2 * columns // count)
    return line.call(
        join_kernel,
        [shape(out, F32)] * count,
        [const_spec(out)] * count,
        [keep, got],
        [const_spec(keep.shape)] * 2,
        scalars=where,
    )


def side_kernel(first, second, out):
    part = first.shape[1]
    out[:, :part] = first[...]
    out[:, part:] = second[...]


def side_by_side(line, first, second):
    rows, columns = first.shape
    spec = const_spec(first.shape)
    out = (rows, 2 * columns)
    return line.call(side_kernel, [shape(out, F32)], [const_spec(out)], [first, second], [spec, spec])[0]


class Plan:
    def __init__(self, line):
        self.line, self.steps, self.found, self.sent = line, {}, {}, {}

    def step(self, name, needs, work):
        self.steps[name] = (needs, work)

    def run(self, *names):
        for name in names:
            if name.startswith("~"):
                if name[1:] in self.sent:
                    self.line.last.append(self.sent[name[1:]])
            elif name in self.steps and name not in self.found:
                needs, work = self.steps[name]
                self.run(*needs)
                self.found[name] = work()

    def __getitem__(self, name):
        return self.found[name]


def on_device(
    dp,
    tensor,
    inputs,
    segments,
    decay_order,
    ln1_gain,
    ln1_bias,
    w_query,
    w_key,
    w_value,
    w_swish,
    w_out,
    ln2_gain,
    ln2_bias,
    w_gate,
    w_up,
    w_down,
    cotangent,
):
    line = Line()
    plan = Plan(line)
    groups = dp // 2
    place = lax.axis_index("dp")
    where = jnp.stack([lax.rem(place, 2), lax.div(place, 2)]).astype(jnp.int32)
    tables = angle_tables(SEQ_LEN)
    logs = jnp.log1p(-jnp.exp2(-(decay_order + 5).astype(F32)))
    seg_row = segments.reshape(1, SEQ_LEN)
    gain1, bias1, gain2, bias2 = (v.reshape(1, -1) for v in (ln1_gain, ln1_bias, ln2_gain, ln2_bias))
    rows = 2 * BLOCK

    def beside(name, values):
        plan.sent[name] = lax.ppermute(values, "dp", [(i, i ^ 1) for i in range(dp)])
        return plan.sent[name]

    def onward(name, values):
        plan.sent[name] = lax.ppermute(values, "dp", [(i, (i + 2) % dp) for i in range(dp)])
        return plan.sent[name]

    def across(name, values):
        plan.sent[name] = lax.ppermute(values, "tensor", [(i, i ^ 2) for i in range(tensor)])
        return plan.sent[name]


    def projected(n, begin, end):
        before = plan["P0"] if n else None
        return projections(line, begin, end, inputs, gain1, bias1, tables, w_query, w_key, w_value, w_swish, before)

    def retained(i):
        a, q, k, v, switch, cos, sin = plan["P1" if i else "P0"]
        before = plan[f"R{i - 1}"][1:3] if i else None
        chip, u, o, p = retention(line, i, q, k, v, switch, seg_row, logs, w_out, before)
        return (chip, across(f"R{i}", chip)), u, o, p

    def fed(i):
        before = plan[f"F{i - 1}"] if i else None
        sums = plan[f"R{i}"][0]
        return feed_forward(line, i, *sums, inputs, gain2, bias2, cotangent, w_gate, w_up, w_down, before)

    last = CHUNKS - 1
    plan.step("P0", [], lambda: projected(0, 0, 1))
    plan.step("R0", ["P0"], lambda: retained(0))
    plan.step("P1", ["R0"], lambda: projected(1, 1, CHUNKS))
    for i in range(CHUNKS):
        plan.step(f"R{i}", ["P1", f"R{i - 1}"] if i else ["P0"], lambda i=i: retained(i))
        plan.step(f"F{i}", [f"R{i}"] + ([f"F{i - 1}"] if i else []), lambda i=i: fed(i))
    plan.step("H", [], lambda: beside("H", core_half(line, inputs)))
    plan.step("G", ["H"], lambda: partner_rows(line, plan["H"], gain1, bias1))

    def first(n):
        return plan["P1"][n]


    def summed(name, lefts, rights, transposed, i, count=rows):
        chip = chip_sum(line, count, lefts, rights, transposed, i)
        return chip, across(name, chip)

    pair = range(2)

    def second_sum(i):
        dg, du = plan[f"F{last}"][1:3]
        return summed(f"B{i}", [dg, du], [w_gate, w_up], True, i)

    def middle_back(i):
        before = plan["M1"] if i == 0 else None
        return second_norm_back(line, i, rows, *plan[f"B{i}"], plan[f"F{last}"][4], gain2, cotangent, before)

    def first_sum(i):
        dq, dk, dv, _ = plan["AB"]
        return summed(f"C{i}", [dq, dk, dv, plan["GB"][1]], [w_query, w_key, w_value, w_swish], True, i)

    def inputs_back(i):
        before = plan["I1"] if i == 0 else None
        return first_norm_back(line, i, rows, *plan[f"C{i}"], inputs, gain1, plan["M0"][1], before)

    def feed_sum():
        return summed("D", [plan[f"F{last}"][0]], [w_down], False, 0, SEQ_LEN)

    def output_rows_all():
        return output_rows(line, 0, SEQ_LEN, *plan["D"], plan[f"F{last}"][4], None)

    def retention_grads():
        _, q, k, v, _, cos, sin = plan["P1"]
        weights = [plan[f"R{i}"][3] for i in range(CHUNKS)]
        return retention_back(line, q, k, v, plan["GB"][0], seg_row, logs, cos, sin, weights)

    for i in reversed(pair):
        after = [] if i else ["M1"]
        plan.step(f"B{i}", [f"F{last}"], lambda i=i: second_sum(i))
        plan.step(f"M{i}", [f"B{i}"] + after, lambda i=i: middle_back(i))
    plan.step("D", [f"F{last}"], feed_sum)
    plan.step("O", ["D"], output_rows_all)
    plan.step("GB", ["M0"], lambda: gate_back(line, plan["M0"][0], w_out, plan[f"R{last}"][2], first(4)))
    plan.step("AB", ["GB"], retention_grads)
    for i in reversed(pair):
        plan.step(f"C{i}", ["AB"], lambda i=i: first_sum(i))
        plan.step(f"I{i}", [f"C{i}", "M0"] + ([] if i else ["I1"]), lambda i=i: inputs_back(i))
    plan.step("CI", ["I0"], lambda: own_copy(line, plan["I0"][0]))
    plan.step("CO", ["O"], lambda: own_copy(line, plan["O"]))


    def small_sums():
        ln1 = [plan[f"I{i}"][n] for n in (1, 2) for i in pair]
        ln2 = [plan[f"M{i}"][n] for n in (2, 3) for i in pair]
        parts = ln1 + ln2
        own = [parts[2 * n] + parts[2 * n + 1] for n in range(4)]
        own = jnp.concatenate(own + [jnp.zeros((4, own[0].shape[1]), F32)], axis=0)
        plan.sent["L"] = lax.ppermute(own, "tensor", [(i, i ^ 1) for i in range(tensor)])
        return own, plan.sent["L"]

    plan.step("L", ["I0", "M0"], small_sums)


    def products(name, needs, operands, by_rows, extra=tuple, skip=0):
        cut = (groups + 1) // 2

        def send(part, begin, end):
            left, right = operands()
            blocks = sent_blocks(line, where, left, right, by_rows, groups, begin, end - begin, extra(), skip)
            return beside(f"S{name}{part}", blocks)

        def ring(j):
            part, index = ("A", j) if j < cut else ("B", j - cut)
            travelling = plan[f"K{name}{j - 1}"] if j else None
            left, right = operands()
            received = plan[f"S{name}{part}"]
            done = j == groups - 1
            block = kept_block(
                line, where, left, right, by_rows, groups, j, received, index, travelling, extra(), done, skip
            )
            return onward(f"K{name}{j}", block) if j < groups - 1 else block

        plan.step(f"S{name}A", needs, lambda: send("A", 0, cut))
        plan.step(f"S{name}B", needs, lambda: send("B", cut, groups))
        for j in range(groups):
            before = [f"K{name}{j - 1}"] if j else []
            plan.step(f"K{name}{j}", [f"S{name}A" if j < cut else f"S{name}B"] + before, lambda j=j: ring(j))
        return lambda: plan[f"K{name}{groups - 1}"]


    def ring_first(name, needs, operands, columns):
        def ring(j):
            travelling = plan[f"K{name}{j - 1}"] if j else None
            block = wide_block(
                line, where, [operands()], groups, j, travelling, j == groups - 1, columns, False
            )
            if j < groups - 1:
                return onward(f"K{name}{j}", block)
            return beside(f"K{name}{j}", block[0]), block[1]

        for j in range(groups):
            plan.step(f"K{name}{j}", [f"K{name}{j - 1}"] if j else needs, lambda j=j: ring(j))
        plan.step(f"E{name}", [f"K{name}{groups - 1}"], lambda: add(line, *plan[f"K{name}{groups - 1}"]))
        return lambda: plan[f"E{name}"]


    def shares(name, needs, operand, count):
        def ring(j):
            travelling = plan[f"J{name}{j - 1}"] if j else None
            right = operand()
            pairs = [(first(0), right), (plan["G"], plan[f"T{name}"])]
            block = wide_block(
                line, where, pairs, groups, j, travelling, j == groups - 1, right.shape[1] // 2, True
            )
            if j < groups - 1:
                return onward(f"J{name}{j}", block)
            return block[1], beside(f"J{name}{j}", block[0])

        plan.step(f"T{name}", needs, lambda: beside(f"T{name}", neighbour_half(line, where, operand())))
        for j in range(groups):
            plan.step(f"J{name}{j}", [f"T{name}", "G"] + ([f"J{name}{j - 1}"] if j else []), lambda j=j: ring(j))
        plan.step(f"E{name}", [f"J{name}{groups - 1}"], lambda: join_halves(line, where, *plan[f"J{name}{groups - 1}"], count))
        return lambda: plan[f"E{name}"]

    fed_all = lambda n: plan[f"F{last}"][n]
    normed2 = lambda: plan[f"F{last}"][3]
    down = products("d", [f"F{last}"], lambda: (fed_all(0), cotangent), False)
    gate = products("g", [f"F{last}"], lambda: (normed2(), fed_all(1)), True)
    half_ff = w_up.shape[1] // 2
    up = ring_first("u", [f"F{last}"], lambda: (normed2(), fed_all(2)), half_ff)
    more_up = products("w", [f"F{last}"], lambda: (normed2(), fed_all(2)), True, skip=half_ff)
    out = products("o", ["M0", "L"], lambda: (plan[f"R{last}"][1], plan["M0"][0]), False, lambda: plan["L"])
    plan.step("U", ["Eu", f"Kw{groups - 1}"], lambda: side_by_side(line, up(), more_up()))
    swish = shares("s", ["GB"], lambda: plan["GB"][1], 1)
    vgrad = shares("v", ["AB"], lambda: plan["AB"][2], 1)
    both = shares("q", ["AB"], lambda: plan["AB"][3], 2)

    plan.run(
        "P0", "R0", "P1", "R1", "H", "R2", "F0", "~R1", "R3", "F1", "F2", "F3", "B1", "SwA", "Ku0", "SgA", "SwB",
        "B0", "Kw0", "Ku1", "G", "Kw1", "~B1", "SdA", "M1", "Ku2", "~Kw1", "Kg0", "M0", "GB", "Ts", "~Ku2", "Kd0",
        "AB", "Kg1", "C1", "Kd1", "Tq", "Ku3", "~Kg1", "Tv", "Js0", "C0", "~Kd1", "Kw2", "I1", "Js1", "Kw3", "Jv0",
        "Js2", "I0", "L", "SgB", "SoA", "Jq0", "Jv1", "D", "CI", "SdB", "Js3", "Jq1", "Jv2", "Ko0", "Jq2", "SoB",
        "Eu", "Kg2", "Ko1", "Jv3", "O", "U", "CO", "Ko2", "Jq3", "Kd2", "Eq", "Kg3", "Ko3", "Es", "Ev", "Kd3",
    )
    plan.run(*plan.steps)
    query, key = both()
    grad_out, small = out()
    return (
        plan["CO"],
        plan["CI"],
        small[0],
        small[1],
        query,
        key,
        vgrad()[0],
        swish()[0],
        grad_out,
        small[2],
        small[3],
        gate(),
        plan["U"],
        down(),
    )


def solution(mesh):
    dp, tensor = mesh.shape["dp"], mesh.shape["tensor"]

    def body(*arrays):
        return on_device(dp, tensor, *arrays)

    return jax.shard_map(
        body,
        mesh=mesh,
        in_specs=(
            P("dp", None),
            P("dp", None),
            P("tensor"),
            P(),
            P(),
            P(None, "tensor"),
            P(None, "tensor"),
            P(None, "tensor"),
            P(None, "tensor"),
            P("tensor", None),
            P(),
            P(),
            P(None, "tensor"),
            P(None, "tensor"),
            P("tensor", None),
            P("dp", None),
        ),
        out_specs=(
            P("dp", None),
            P("dp", None),
            P("dp"),
            P("dp"),
            P("dp", "tensor"),
            P("dp", "tensor"),
            P("dp", "tensor"),
            P("dp", "tensor"),
            P("tensor", "dp"),
            P("dp"),
            P("dp"),
            P("dp", "tensor"),
            P("dp", "tensor"),
            P("tensor", "dp"),
        ),
        check_vma=False,
    )
```

```python
import functools

import jax
import jax.numpy as jnp
from jax import lax
from jax.experimental import pallas as pl
from jax.experimental.pallas import tpu as pltpu
from jax.sharding import PartitionSpec as P

KEY = 256
VALUE = 512
SEQ_LEN = 1024
DOC_MOST = 512
BLOCK = 256
CHUNKS = SEQ_LEN // BLOCK
HALF = BLOCK // 2
BF16 = jnp.bfloat16
F32 = jnp.float32
MIB = 1 << 20


def product_tn(left, right):
    return lax.dot_general(left, right, (((0,), (0,)), ((), ())), preferred_element_type=F32)


def product_nt(left, right):
    return lax.dot_general(left, right, (((1,), (1,)), ((), ())), preferred_element_type=F32)


def product_nn(left, right):
    return jnp.dot(left, right, preferred_element_type=F32)


def angle_tables(length):
    half_width = KEY // 2
    column = jnp.arange(KEY, dtype=jnp.int32) // 2
    frequency = jnp.power(10000.0, -column.astype(F32) / (half_width - 1))
    inside = jnp.arange(BLOCK, dtype=jnp.int32).astype(F32)[:, None] * frequency[None, :]
    starts = jnp.arange(0, length, BLOCK, dtype=jnp.int32).astype(F32)[:, None] * frequency[None, :]
    return jnp.cos(inside), jnp.sin(inside), jnp.cos(starts), jnp.sin(starts)


def rotate(values, cosines, sines, sign):
    even = lax.broadcasted_iota(jnp.int32, values.shape, 1) % 2 == 0
    after = pltpu.roll(values, KEY - 1, 1)
    before = pltpu.roll(values, 1, 1)
    return values * cosines + sign * jnp.where(even, -after, before) * sines


def normal_rows(values, eps):
    average = jnp.mean(values, axis=-1, keepdims=True)
    centred = values - average
    spread = jnp.mean(centred * centred, axis=-1, keepdims=True)
    return centred, lax.rsqrt(spread + eps)


def down_rows(seg):
    return jnp.transpose(jnp.broadcast_to(seg.astype(F32), (BLOCK, BLOCK)))


def decay_block(log_keep, seg_rows, seg, row_start, column_start):
    rows = row_start + lax.broadcasted_iota(jnp.int32, (BLOCK, BLOCK), 0)
    columns = column_start + lax.broadcasted_iota(jnp.int32, (BLOCK, BLOCK), 1)
    gap = rows - columns
    keep = (seg_rows == seg.astype(F32)) & (gap >= 0)
    return jnp.where(keep, jnp.exp(jnp.maximum(gap, 0).astype(F32) * log_keep), 0.0)


def first_key_block(chunk):
    return max(0, chunk - (DOC_MOST + BLOCK - 2) // BLOCK)


class Line:
    def __init__(self):
        self.last = []
        self.shared = 0

    def call(
        self,
        kernel,
        outs,
        out_specs,
        ins,
        in_specs,
        grid=(1,),
        scalars=None,
        scratch=(),
        vmem=63,
        onto=(),
        paired=False,
    ):
        held = list(ins) + [array for _, array in onto]
        extra = held[len(ins) :] + [array for array in self.last if not any(array is other for other in held)]
        scalar_count = 0 if scalars is None else 1
        in_count = len(ins)
        skipped = len(extra)

        def body(*refs):
            head, rest = refs[: scalar_count + in_count], refs[scalar_count + in_count + skipped :]
            kernel(*head, *rest)

        specs = list(in_specs) + [pl.BlockSpec(memory_space=pl.ANY)] * skipped
        arguments = ([] if scalars is None else [scalars]) + list(ins) + extra
        extras = {}
        if paired:
            extras = dict(collective_id=self.shared, has_side_effects=True)
            self.shared += 1
        result = pl.pallas_call(
            body,
            out_shape=tuple(outs),
            grid_spec=pltpu.PrefetchScalarGridSpec(
                num_scalar_prefetch=scalar_count,
                grid=grid,
                in_specs=specs,
                out_specs=tuple(out_specs),
                scratch_shapes=list(scratch),
            ),
            input_output_aliases={scalar_count + in_count + n: out for n, (out, _) in enumerate(onto)},
            compiler_params=pltpu.CompilerParams(
                vmem_limit_bytes=vmem * MIB,
                dimension_semantics=("arbitrary",) * len(grid),
                **extras,
            ),
            cost_estimate=pl.CostEstimate(flops=1, bytes_accessed=1, transcendentals=0),
        )(*arguments)
        self.last = [result[0]]
        return result


def my_core():
    return lax.rem(lax.axis_index("tensor"), 2)


def other_core():
    rank = lax.axis_index("tensor")
    return {"tensor": rank + 1 - 2 * lax.rem(rank, 2)}


def meet_other_core():
    barrier = pltpu.get_barrier_semaphore()
    pl.semaphore_signal(barrier, inc=1, device_id=other_core(), device_id_type=pl.DeviceIdType.MESH)
    pl.semaphore_wait(barrier, 1)


def to_other_core(source, target, sent, arrived):
    return pltpu.make_async_remote_copy(
        src_ref=source,
        dst_ref=target,
        send_sem=sent,
        recv_sem=arrived,
        device_id=other_core(),
        device_id_type=pl.DeviceIdType.MESH,
    )


def core_rows(mine, block):
    core = my_core() if mine else 1 - my_core()
    return pl.ds(pl.multiple_of(block * BLOCK + core * HALF, HALF), HALF)


def shape(dims, kind):
    return jax.ShapeDtypeStruct(dims, kind)


def const_spec(dims):
    return pl.BlockSpec(dims, lambda *_: (0,) * len(dims))


def once_spec(dims):
    return pl.BlockSpec(dims, lambda *_: (0,) * len(dims), pipeline_mode=pl.Buffered(1))


def row_spec(rows, columns, chunk):
    return pl.BlockSpec((rows, columns), lambda *_: (chunk, 0))


SMEM = pl.BlockSpec(memory_space=pltpu.SMEM)
ANY = pl.BlockSpec(memory_space=pl.ANY)


def fetch_scratch(*arrays):
    return [pltpu.VMEM(a.shape, a.dtype) for a in arrays] + [pltpu.SemaphoreType.DMA((len(arrays),))]


def fetched(sources, held):
    places, done = held[:-1], held[-1]
    copies = [pltpu.make_async_copy(s, p, done.at[n]) for n, (s, p) in enumerate(zip(sources, places))]
    return places, copies


def proj_kernel(begin, fetching, x, gain, bias, cos, sin, cos0, sin0, *refs):
    wq, wk, wv, ws, a_out, q_out, k_out, v_out, s_out, c_out, n_out, x_out = refs[:12]
    chunk = begin + pl.program_id(0)
    if fetching:
        (wq, wk, wv, ws), fetch = fetched((wq, wk, wv, ws), refs[12:])
        for copy in fetch:
            copy.start()

    def ready(n):
        if fetching:
            fetch[n].wait()

    centred, scale = normal_rows(x[...].astype(F32), 1e-05)
    normed = (centred * scale * gain[...] + bias[...]).astype(BF16)
    a_out[...] = normed
    x_out[...] = x[core_rows(True, 0), :].astype(F32)
    first_cos, first_sin = cos0[pl.ds(chunk, 1), :], sin0[pl.ds(chunk, 1), :]
    cosines = cos[...] * first_cos - sin[...] * first_sin
    sines = sin[...] * first_cos + cos[...] * first_sin
    c_out[...] = cosines
    n_out[...] = sines
    parts = [slice(n, n + KEY) for n in range(0, wq.shape[1], KEY)]
    ready(0)
    for part in parts:
        query = product_nn(normed, wq[:, part])
        q_out[:, part] = rotate(query, cosines, sines, 1.0).astype(BF16)
    ready(1)
    for part in parts:
        turned = rotate(product_nn(normed, wk[:, part]), cosines, sines, 1.0) * float(KEY) ** (-0.5)
        k_out[:, part] = turned.astype(BF16)
    parts = [slice(n, n + VALUE) for n in range(0, wv.shape[1], VALUE)]
    ready(2)
    for part in parts:
        v_out[:, part] = product_nn(normed, wv[:, part]).astype(BF16)
    ready(3)
    for part in parts:
        s_out[:, part] = product_nn(normed, ws[:, part])


def projections(line, begin, end, x, gain, bias, tables, wq, wk, wv, ws, before):
    rows, width = x.shape
    kw, vw = wq.shape[1], wv.shape[1]
    wide = [(width, BF16), (kw, BF16), (kw, BF16), (vw, BF16), (vw, F32), (KEY, F32), (KEY, F32)]

    def chunked(columns):
        return pl.BlockSpec((BLOCK, columns), lambda i: (begin + i, 0))

    weights = (wq, wk, wv, ws)
    alone = end - begin == 1
    return line.call(
        functools.partial(proj_kernel, begin, alone),
        [shape((rows, columns), kind) for columns, kind in wide] + [shape((rows // 2, width), F32)],
        [chunked(columns) for columns, _ in wide] + [pl.BlockSpec((HALF, width), lambda i: (begin + i, 0))],
        [x, gain, bias, *tables, wq, wk, wv, ws],
        [chunked(width), const_spec((1, width)), const_spec((1, width))]
        + [const_spec(table.shape) for table in tables]
        + ([ANY] * 4 if alone else [once_spec(w.shape) for w in weights]),
        grid=(end - begin,),
        scratch=fetch_scratch(*weights) if alone else [],
        onto=() if before is None else tuple(enumerate(before)),
    )


TILES = 4


def retain_kernel(
    chunk, q, k, v, switch, seg_row, logs, w, chip, u_out, o_out, p_out, full, sent, got, s1, s2, *held
):
    (w,), (fetch,) = fetched((w,), held)
    fetch.start()
    meet_other_core()
    seg_rows = down_rows(seg_row[:, chunk * BLOCK : (chunk + 1) * BLOCK])
    heads = q.shape[1] // KEY
    low = first_key_block(chunk)
    for head in range(heads):
        kpart, vpart = slice(head * KEY, (head + 1) * KEY), slice(head * VALUE, (head + 1) * VALUE)
        total = None
        for block in range(low, chunk + 1):
            rows = slice(block * BLOCK, (block + 1) * BLOCK)
            raw = product_nt(q[:, kpart], k[rows, kpart])
            mask = decay_block(logs[head], seg_rows, seg_row[:, rows], chunk * BLOCK, block * BLOCK)
            weights = (raw * mask).astype(BF16)
            p_out[head, :, (block - low) * BLOCK : (block - low + 1) * BLOCK] = weights
            part = product_nn(weights, v[rows, vpart])
            total = part if total is None else total + part
        o_out[:, vpart] = total
        centred, scale = normal_rows(total, 1.0)
        gate = switch[:, vpart]
        u_out[:, vpart] = (centred * scale * (gate * jax.nn.sigmoid(gate))).astype(BF16)
    tile = w.shape[1] // TILES
    copies = []
    fetch.wait()
    for j in range(TILES):
        columns = slice(j * tile, (j + 1) * tile)
        full[:, columns] = product_nn(u_out[...], w[:, columns])
        sent[j] = full[core_rows(False, 0), columns]
        copies.append(to_other_core(sent.at[j], got.at[j], s1.at[j], s2.at[j]))
        copies[-1].start()
    for j in range(TILES):
        columns = slice(j * tile, (j + 1) * tile)
        copies[j].wait()
        chip[:, columns] = full[core_rows(True, 0), columns] + got[j]


def retention(line, chunk, q, k, v, switch, seg_row, logs, w, before):
    rows, kw = q.shape
    vw, width = v.shape[1], w.shape[1]
    heads = kw // KEY
    blocks = chunk + 1 - first_key_block(chunk)
    return line.call(
        functools.partial(retain_kernel, chunk),
        [
            shape((HALF, width), F32),
            shape((rows, vw), BF16),
            shape((rows, vw), F32),
            shape((heads, BLOCK, blocks * BLOCK), BF16),
        ],
        [
            const_spec((HALF, width)),
            row_spec(BLOCK, vw, chunk),
            row_spec(BLOCK, vw, chunk),
            const_spec((heads, BLOCK, blocks * BLOCK)),
        ],
        [q, k, v, switch, seg_row, logs, w],
        [
            row_spec(BLOCK, kw, chunk),
            const_spec(((chunk + 1) * BLOCK, kw)),
            const_spec(((chunk + 1) * BLOCK, vw)),
            row_spec(BLOCK, vw, chunk),
            const_spec(seg_row.shape),
            SMEM,
            ANY,
        ],
        scratch=[
            pltpu.VMEM((BLOCK, width), F32),
            pltpu.VMEM((TILES, HALF, width // TILES), F32),
            pltpu.VMEM((TILES, HALF, width // TILES), F32),
            pltpu.SemaphoreType.DMA((TILES,)),
            pltpu.SemaphoreType.DMA((TILES,)),
            *fetch_scratch(w),
        ],
        onto=() if before is None else ((1, before[0]), (2, before[1])),
        paired=True,
    )


PIECES = 2


def feed_kernel(
    chunk, chip, crossed, x, gain, bias, c, wg, wu, wd, hid_out, dg_out, du_out, a_out, h_out, back, *held
):
    places, loaded, sent, got, s1, s2 = held[:4], held[4], *held[5:]
    c_in, wd_in, wg_in, wu_in = places
    ff = back.shape[1]
    tile = ff // TILES
    tokens = c.at[pl.ds(chunk * BLOCK, BLOCK)]
    fetch = [pltpu.make_async_copy(tokens, c_in, loaded.at[0]), pltpu.make_async_copy(wd, wd_in, loaded.at[1])]
    for n, (source, place) in enumerate(((wg, wg_in), (wu, wu_in))):
        for t in range(TILES):
            columns = pl.ds(t * tile, tile)
            semaphore = loaded.at[2 + 2 * t + n]
            fetch.append(pltpu.make_async_copy(source.at[:, columns], place.at[:, columns], semaphore))
    for copy in fetch:
        copy.start()
    meet_other_core()
    piece = HALF // PIECES
    copies = []
    for n in range(PIECES):
        part = pl.ds(n * piece, piece)
        rows = pl.ds(pl.multiple_of(my_core() * HALF + n * piece, piece), piece)
        copies.append(to_other_core(sent.at[part], got.at[part], s1.at[n], s2.at[n]))
        middle = x[rows, :].astype(F32) + (chip[part, :] + crossed[part, :])
        h_out[part, :] = middle
        centred, scale = normal_rows(middle, 1e-05)
        normed = (centred * scale * gain[...] + bias[...]).astype(BF16)
        sent[part, :] = normed.astype(F32)
        copies[n].start()
        a_out[rows, :] = normed
    fetch[0].wait()
    fetch[1].wait()
    for t in range(TILES):
        columns = slice(t * tile, (t + 1) * tile)
        back[:, columns] = product_nt(c_in[...], wd_in[columns, :])
    for n in range(PIECES):
        rows = pl.ds(pl.multiple_of((1 - my_core()) * HALF + n * piece, piece), piece)
        copies[n].wait()
        a_out[rows, :] = got[pl.ds(n * piece, piece), :].astype(BF16)
    factor = 0.7978845608028654
    for t in range(TILES):
        columns = slice(t * tile, (t + 1) * tile)
        fetch[2 + t].wait()
        fetch[2 + TILES + t].wait()
        gate = product_nn(a_out[...], wg_in[:, columns])
        up = product_nn(a_out[...], wu_in[:, columns])
        bent = jnp.tanh(factor * (gate + 0.044715 * (gate * gate * gate)))
        half = 0.5 * (1.0 + bent)
        active = gate * half
        slope = half + 0.5 * gate * (1.0 - bent * bent) * (factor * (1.0 + 3 * 0.044715 * gate * gate))
        hid_out[:, columns] = (active * up).astype(BF16)
        dg_out[:, columns] = (back[:, columns] * up * slope).astype(BF16)
        du_out[:, columns] = (back[:, columns] * active).astype(BF16)


def feed_forward(line, chunk, chip, crossed, x, gain, bias, c, wg, wu, wd, before):
    total, width = x.shape
    ff = wg.shape[1]
    return line.call(
        functools.partial(feed_kernel, chunk),
        [shape((total, ff), BF16)] * 3 + [shape((total, width), BF16), shape((total // 2, width), F32)],
        [row_spec(BLOCK, ff, chunk)] * 3 + [row_spec(BLOCK, width, chunk), row_spec(HALF, width, chunk)],
        [chip, crossed, x, gain, bias, c, wg, wu, wd],
        [
            const_spec((HALF, width)),
            const_spec((HALF, width)),
            row_spec(BLOCK, width, chunk),
            const_spec((1, width)),
            const_spec((1, width)),
        ]
        + [ANY] * 4,
        scratch=[
            pltpu.VMEM((BLOCK, ff), F32),
            pltpu.VMEM((BLOCK, width), BF16),
            pltpu.VMEM(wd.shape, BF16),
            pltpu.VMEM(wg.shape, BF16),
            pltpu.VMEM(wu.shape, BF16),
            pltpu.SemaphoreType.DMA((2 + 2 * TILES,)),
            pltpu.VMEM((HALF, width), F32),
            pltpu.VMEM((HALF, width), F32),
            pltpu.SemaphoreType.DMA((PIECES,)),
            pltpu.SemaphoreType.DMA((PIECES,)),
        ],
        onto=() if before is None else tuple(enumerate(before)),
        paired=True,
    )


def chip_kernel(count, transposed, steps, *refs):
    lefts, rights = refs[:count], refs[count : 2 * count]
    out, full, kept, sent, got, s1, s2 = refs[2 * count :]
    half = kept.shape[1]
    j = pl.program_id(0)

    @pl.when(j == 0)
    def _():
        meet_other_core()

    @pl.when(j < steps)
    def _():
        total = None
        for left, right in zip(lefts, rights):
            part = product_nt(left[...], right[...]) if transposed else product_nn(left[...], right[...])
            total = part if total is None else total + part
        full[...] = total
        for n in range(half // HALF):
            part = slice(n * HALF, (n + 1) * HALF)
            sent[j, part] = full[core_rows(False, n), :]
            kept[j, part] = full[core_rows(True, n), :]
        to_other_core(sent.at[j], got.at[j], s1.at[j], s2.at[j]).start()

    @pl.when(j > 0)
    def _():
        to_other_core(sent.at[j - 1], got.at[j - 1], s1.at[j - 1], s2.at[j - 1]).wait()
        out[...] = kept[j - 1] + got[j - 1]


def chip_sum(line, rows, lefts, rights, transposed, chunk):
    width = rights[0].shape[0] if transposed else rights[0].shape[1]
    tile = 512
    steps = width // tile
    half = rows // 2
    right_specs = [
        pl.BlockSpec((tile, right.shape[1]), lambda i: (jnp.minimum(i, steps - 1), 0))
        if transposed
        else pl.BlockSpec((right.shape[0], tile), lambda i: (0, jnp.minimum(i, steps - 1)))
        for right in rights
    ]
    left_specs = [row_spec(rows, left.shape[1], chunk) for left in lefts]
    return line.call(
        functools.partial(chip_kernel, len(lefts), transposed, steps),
        [shape((half, width), F32)],
        [pl.BlockSpec((half, tile), lambda i: (0, jnp.maximum(i, 1) - 1))],
        list(lefts) + list(rights),
        left_specs + right_specs,
        grid=(steps + 1,),
        scratch=[
            pltpu.VMEM((rows, tile), F32),
            pltpu.VMEM((steps, half, tile), F32),
            pltpu.VMEM((steps, half, tile), F32),
            pltpu.VMEM((steps, half, tile), F32),
            pltpu.SemaphoreType.DMA((steps,)),
            pltpu.SemaphoreType.DMA((steps,)),
        ],
        paired=True,
    )[0]


def shared_kernel(work, in_count, steps, *refs):
    ins, out = refs[:in_count], refs[in_count]
    extras, (sent, got, s1, s2) = refs[in_count + 1 : -4], refs[-4:]
    j = pl.program_id(0)

    @pl.when(j == 0)
    def _():
        meet_other_core()

    @pl.when(j < steps)
    def _():
        sent[j] = work(*ins, *extras)
        to_other_core(sent.at[j], got.at[j], s1.at[j], s2.at[j]).start()

    @pl.when(j > 0)
    def _():
        to_other_core(sent.at[j - 1], got.at[j - 1], s1.at[j - 1], s2.at[j - 1]).wait()
        out[core_rows(True, 0), :] = sent[j - 1].astype(out.dtype)
        out[core_rows(False, 0), :] = got[j - 1].astype(out.dtype)


def shared_rows(line, work, begin, steps, ins, in_specs, kind, total_rows, width, extras=(), before=()):
    return line.call(
        functools.partial(shared_kernel, work, len(ins), steps),
        [shape((total_rows, width), kind)] + [shape(dims, F32) for dims, _ in extras],
        [pl.BlockSpec((BLOCK, width), lambda j: (begin + jnp.maximum(j, 1) - 1, 0))] + [spec for _, spec in extras],
        ins,
        in_specs,
        grid=(steps + 1,),
        scratch=[
            pltpu.VMEM((steps, HALF, width), F32),
            pltpu.VMEM((steps, HALF, width), F32),
            pltpu.SemaphoreType.DMA((steps,)),
            pltpu.SemaphoreType.DMA((steps,)),
        ],
        onto=before,
        paired=True,
    )


def stepped(rows, width, steps, begin=0):
    return pl.BlockSpec((rows, width), lambda j: (begin + jnp.minimum(j, steps - 1), 0))


def partner_work(got, gain, bias):
    centred, scale = normal_rows(got[...], 1e-05)
    return (centred * scale * gain[...] + bias[...]).astype(BF16).astype(F32)


def partner_rows(line, got, gain, bias):
    half, width = got.shape
    steps = half // HALF
    specs = [stepped(HALF, width, steps), const_spec((1, width)), const_spec((1, width))]
    return shared_rows(line, partner_work, 0, steps, [got, gain, bias], specs, BF16, 2 * half, width)[0]


def norm_back(back, centred, scale, gain, gain_out, bias_out):
    normed = centred * scale
    begin = pl.program_id(0) == 0
    one, two = jnp.sum(back * normed, axis=0, keepdims=True), jnp.sum(back, axis=0, keepdims=True)

    @pl.when(begin)
    def _():
        gain_out[...] = one
        bias_out[...] = two

    @pl.when(jnp.logical_not(begin))
    def _():
        gain_out[...] += one
        bias_out[...] += two

    scaled = back * gain[...]
    first = jnp.mean(scaled, axis=-1, keepdims=True)
    second = jnp.mean(scaled * normed, axis=-1, keepdims=True)
    return scale * (scaled - first - normed * second)


def middle_work(chip, crossed, h, gain, c, dh_out, gain_out, bias_out):
    centred, scale = normal_rows(h[...], 1e-05)
    back = chip[...] + crossed[...]
    value = c[core_rows(True, 0), :].astype(F32) + norm_back(back, centred, scale, gain, gain_out, bias_out)
    dh_out[...] = value
    return value


def second_norm_back(line, begin, chip, crossed, h, gain, c, before):
    total, width = c.shape
    steps = chip.shape[0] // HALF
    part, own = stepped(HALF, width, steps), stepped(HALF, width, steps, begin)
    small = ((1, width), const_spec((1, width)))
    return shared_rows(
        line,
        middle_work,
        begin,
        steps,
        [chip, crossed, h, gain, c],
        [part, part, own, const_spec((1, width)), stepped(BLOCK, width, steps, begin)],
        BF16,
        total,
        width,
        [((total // 2, width), own), small, small],
        () if before is None else ((0, before[0]), (1, before[1])),
    )


def first_work(chip, crossed, x, gain, dh, gain_out, bias_out):
    centred, scale = normal_rows(x[core_rows(True, 0), :].astype(F32), 1e-05)
    back = chip[...] + crossed[...]
    return dh[...] + norm_back(back, centred, scale, gain, gain_out, bias_out)


def first_norm_back(line, begin, chip, crossed, x, gain, dh, before):
    total, width = x.shape
    steps = chip.shape[0] // HALF
    part, own = stepped(HALF, width, steps), stepped(HALF, width, steps, begin)
    small = ((1, width), const_spec((1, width)))
    return shared_rows(
        line,
        first_work,
        begin,
        steps,
        [chip, crossed, x, gain, dh],
        [part, part, stepped(BLOCK, width, steps, begin), const_spec((1, width)), own],
        F32,
        total,
        width,
        [small, small],
        () if before is None else ((0, before[0]),),
    )


def output_work(chip, crossed, h):
    return h[...] + (chip[...] + crossed[...])


def output_rows(line, chip, crossed, h):
    half, width = h.shape
    steps = half // HALF
    specs = [stepped(HALF, width, steps)] * 3
    return shared_rows(line, output_work, 0, steps, [chip, crossed, h], specs, BF16, 2 * half, width)[0]


def copy_kernel(source, out):
    out[...] = source[...]


def own_copy(line, source):
    rows, width = source.shape
    spec = pl.BlockSpec((BLOCK, width), lambda i: (i, 0))
    return line.call(copy_kernel, [shape(source.shape, source.dtype)], [spec], [source], [spec], grid=(rows // BLOCK,))[0]


def add_kernel(a, b, out):
    out[...] = a[...] + b[...]


def add(line, a, b):
    spec = const_spec(a.shape)
    return line.call(add_kernel, [shape(a.shape, F32)], [spec], [a, b], [spec, spec])[0]


def gate_kernel(where, dz, w, o, switch, do_out, ds_out, far_out):
    for head in range(o.shape[1] // VALUE):
        part = slice(head * VALUE, (head + 1) * VALUE)
        grad = product_nt(dz[...], w[part, :])
        centred, scale = normal_rows(o[:, part], 1.0)
        gate = switch[:, part]
        sig = jax.nn.sigmoid(gate)
        ds = (grad * (centred * scale) * (sig * (1.0 + gate * (1.0 - sig)))).astype(BF16)
        ds_out[:, part] = ds
        dn = grad * (gate * sig)
        one = jnp.mean(dn, axis=-1, keepdims=True)
        two = jnp.mean(dn * centred, axis=-1, keepdims=True)
        do_out[:, part] = (scale * (dn - one) - (scale * scale * scale) * centred * two).astype(BF16)

        @pl.when(where[0] != head)
        def _(ds=ds):
            far_out[...] = ds.astype(F32)


def gate_back(line, where, dz, w, o, switch):
    rows, vw = o.shape

    def rowed(columns):
        return pl.BlockSpec((BLOCK, columns), lambda n, w: (n, 0))

    return line.call(
        gate_kernel,
        [shape((rows, vw), BF16), shape((rows, vw), BF16), shape((rows, vw // 2), F32)],
        [rowed(vw), rowed(vw), rowed(vw // 2)],
        [dz, w, o, switch],
        [rowed(dz.shape[1]), const_spec(w.shape), rowed(vw), rowed(vw)],
        grid=(rows // BLOCK,),
        scalars=where,
    )


def retain_back_kernel(where, q, k, v, do, seg_row, logs, cos, sin, *rest):
    weights = rest[:CHUNKS]
    dq_out, dk_out, dv_out, both_out, far_out, far_v_out, dq_sum, dk_sum, dv_sum = rest[CHUNKS:]
    head = pl.program_id(0)
    dk_sum[...] = jnp.zeros_like(dk_sum)
    dv_sum[...] = jnp.zeros_like(dv_sum)
    for chunk in range(CHUNKS):
        low = first_key_block(chunk)
        here = slice(chunk * BLOCK, (chunk + 1) * BLOCK)
        seg_rows = down_rows(seg_row[:, here])
        total = None
        for block in range(low, chunk + 1):
            rows = slice(block * BLOCK, (block + 1) * BLOCK)
            part = slice((block - low) * BLOCK, (block - low + 1) * BLOCK)
            mask = decay_block(logs[head], seg_rows, seg_row[:, rows], chunk * BLOCK, block * BLOCK)
            scores = (product_nt(do[here, :], v[rows, :]) * mask).astype(BF16)
            dv_sum[rows, :] += product_tn(weights[chunk][0, :, part], do[here, :])
            dk_sum[rows, :] += product_tn(scores, q[here, :])
            term = product_nn(scores, k[rows, :])
            total = term if total is None else total + term
        dq_sum[here, :] = total
    dq = rotate(dq_sum[...], cos[...], sin[...], -1.0).astype(BF16)
    dk = (rotate(dk_sum[...], cos[...], sin[...], -1.0) * float(KEY) ** (-0.5)).astype(BF16)
    dq_out[...] = dq
    dk_out[...] = dk
    both_out[:, :KEY] = dq
    both_out[:, KEY:] = dk
    dv = dv_sum[...].astype(BF16)
    dv_out[...] = dv

    @pl.when(where[0] != head)
    def _():
        far_out[:, :KEY] = dq.astype(F32)
        far_out[:, KEY:] = dk.astype(F32)
        far_v_out[...] = dv.astype(F32)


def retention_back(line, where, q, k, v, do, seg_row, logs, cos, sin, weights):
    rows, kw = q.shape
    vw = v.shape[1]

    def headed(columns):
        return pl.BlockSpec((rows, columns), lambda h, w: (0, h))

    return line.call(
        retain_back_kernel,
        [shape((rows, columns), BF16) for columns in (kw, kw, vw, 2 * kw)]
        + [shape((rows, 2 * KEY), F32), shape((rows, VALUE), F32)],
        [headed(KEY), headed(KEY), headed(VALUE), headed(2 * KEY)]
        + [const_spec((rows, 2 * KEY)), const_spec((rows, VALUE))],
        [q, k, v, do, seg_row, logs, cos, sin] + list(weights),
        [
            headed(KEY),
            headed(KEY),
            headed(VALUE),
            headed(VALUE),
            const_spec(seg_row.shape),
            SMEM,
            const_spec(cos.shape),
            const_spec(sin.shape),
        ]
        + [pl.BlockSpec((1,) + part.shape[1:], lambda h, w: (h, 0, 0)) for part in weights],
        grid=(kw // KEY,),
        scalars=where,
        scratch=[pltpu.VMEM((rows, KEY), F32), pltpu.VMEM((rows, KEY), F32), pltpu.VMEM((rows, VALUE), F32)],
    )


def outer_place(where, position, groups):
    return lax.rem(where[1] + 2 * groups - 1 - position, groups)


def column_block(where, position, groups, own):
    return outer_place(where, position, groups) * 2 + (where[0] if own else 1 - where[0])


def plain_block(where, left, right, by_rows, groups, position, own, extra, skip):
    width = (left if by_rows else right).shape[1] // (2 * groups)
    column = column_block(where, position, groups, own) * width
    if by_rows:
        return product_tn(lax.dynamic_slice_in_dim(left, column, width, 1), right[:, skip:])
    block = product_tn(left, lax.dynamic_slice_in_dim(right, column, width, 1))
    if extra:
        more = lax.dynamic_slice_in_dim(extra[0] + extra[1], column, width, 1)
        block = jnp.concatenate([block, more], axis=0)
    return block


def sent_kernel(where, left, right, *rest):
    extra, out = rest[:-1], rest[-1]
    rows = left.shape[1]
    out[0, :rows] = product_tn(left[...], right[...])
    if extra:
        out[0, rows:] = extra[0][...] + extra[1][...]


def sent_blocks(line, where, left, right, by_rows, groups, first, count, extra=(), skip=0):
    width = (left if by_rows else right).shape[1] // (2 * groups)
    if width % 128:
        blocks = [plain_block(where, left, right, by_rows, groups, first + j, False, extra, skip) for j in range(count)]
        return jnp.stack(blocks)
    rows = left.shape[0]
    moving = pl.BlockSpec((rows, width), lambda j, w: (0, column_block(w, first + j, groups, False)))
    more = extra[0].shape[0] if extra else 0
    columns = right.shape[1] - skip
    block = (width, columns) if by_rows else (left.shape[1] + more, width)
    fixed = pl.BlockSpec((rows, columns), lambda j, w: (0, skip // columns))
    specs = [moving if by_rows else const_spec(left.shape), fixed if by_rows else moving]
    small = pl.BlockSpec((more, width), lambda j, w: (0, column_block(w, first + j, groups, False)))
    return line.call(
        sent_kernel,
        [shape((count,) + block, F32)],
        [pl.BlockSpec((1,) + block, lambda j, w: (j, 0, 0))],
        [left, right, *extra],
        specs + [small] * len(extra),
        grid=(count,),
        scalars=where,
    )[0]


def kept_kernel(has_travelling, extra_count, where, left, right, received, *rest):
    more, rest = rest[:extra_count], rest[extra_count:]
    total = product_tn(left[...], right[...])
    rows = total.shape[0]
    total = total + received[0, :rows]
    if has_travelling:
        total = total + rest[0][:rows]
    if not extra_count:
        rest[-1][...] = total
        return
    small = more[0][...] + more[1][...] + received[0, rows:]
    if has_travelling:
        small = small + rest[0][rows:]
    outs = rest[1:] if has_travelling else rest
    outs[0][:rows] = total
    if len(outs) == 2:
        outs[1][...] = small
    else:
        outs[0][rows:] = small


def kept_block(
    line, where, left, right, by_rows, groups, position, received, index, travelling, extra=(), last=False, skip=0
):
    width = (left if by_rows else right).shape[1] // (2 * groups)
    if width % 128:
        block = plain_block(where, left, right, by_rows, groups, position, True, extra, skip) + received[index]
        block = block if travelling is None else block + travelling
        return (block[: left.shape[1]], block[left.shape[1] :]) if extra and last else block
    if extra:
        return extended_block(line, where, left, right, groups, position, received, index, travelling, extra, last)
    rows, columns = left.shape[0], right.shape[1] - skip
    tiles = 1 if skip else 2
    moving = pl.BlockSpec((rows, width), lambda j, w: (0, column_block(w, position, groups, True)))
    if by_rows:
        part = columns // tiles
        left_spec, right_spec = moving, pl.BlockSpec((rows, part), lambda j, w: (0, skip // part + j))
        block, piece, at = (width, columns), (width, part), lambda j: (0, j)
    else:
        part = left.shape[1] // tiles
        left_spec, right_spec = pl.BlockSpec((rows, part), lambda j, w: (0, j)), moving
        block, piece, at = (left.shape[1], width), (part, width), lambda j: (j, 0)
    flat = pl.BlockSpec(piece, lambda j, w: at(j))
    ins = [left, right, received] + ([] if travelling is None else [travelling])
    specs = [left_spec, right_spec, pl.BlockSpec((1,) + piece, lambda j, w: (index,) + at(j))]
    return line.call(
        functools.partial(kept_kernel, travelling is not None, 0),
        [shape(block, F32)],
        [flat],
        ins,
        specs + ([] if travelling is None else [flat]),
        grid=(tiles,),
        scalars=where,
    )[0]


def extended_block(line, where, left, right, groups, position, received, index, travelling, extra, last):
    width = right.shape[1] // (2 * groups)
    rows, more = left.shape[0], extra[0].shape[0]
    block = (left.shape[1] + more, width)
    moving = pl.BlockSpec((rows, width), lambda j, w: (0, column_block(w, position, groups, True)))
    small = pl.BlockSpec((more, width), lambda j, w: (0, column_block(w, position, groups, True)))
    ins = [left, right, received, *extra] + ([] if travelling is None else [travelling])
    specs = [const_spec(left.shape), moving, pl.BlockSpec((1,) + block, lambda j, w: (index, 0, 0)), small, small]
    outs = [(left.shape[1], width), (more, width)] if last else [block]
    result = line.call(
        functools.partial(kept_kernel, travelling is not None, len(extra)),
        [shape(dims, F32) for dims in outs],
        [const_spec(dims) for dims in outs],
        ins,
        specs + ([] if travelling is None else [const_spec(block)]),
        scalars=where,
    )
    return result if last else result[0]


def wide_kernel(pair_count, has_travelling, last, where, *refs):
    total = None
    for n in range(pair_count):
        part = product_tn(refs[2 * n][...], refs[2 * n + 1][...].astype(BF16))
        total = part if total is None else total + part
    rest = refs[2 * pair_count :]
    if has_travelling:
        total = total + rest[0][...]
        rest = rest[1:]
    if not last:
        rest[0][...] = total
        return
    send, keep, full = rest
    full[...] = total
    half = send.shape[0]
    keep[...] = full[pl.ds(pl.multiple_of(where[0] * half, half), half), :]
    send[...] = full[pl.ds(pl.multiple_of((1 - where[0]) * half, half), half), :]


def wide_block(line, where, pairs, groups, position, travelling, last, columns, shared):
    rows, depth = pairs[0][0].shape
    width = depth // groups
    tiles = 2
    part = columns // tiles
    ins, specs = [], []
    for left, right in pairs:
        ins += [left, right]
        specs.append(pl.BlockSpec((rows, width), lambda j, w: (0, outer_place(w, position, groups))))
        if shared and right.shape[1] > columns:
            specs.append(pl.BlockSpec((rows, part), lambda j, w: (0, w[0] * tiles + j)))
        else:
            specs.append(pl.BlockSpec((rows, part), lambda j, w: (0, j)))
    if travelling is not None:
        ins.append(travelling)
        specs.append(pl.BlockSpec((width, part), lambda j, w: (0, j)))
    height = width // 2 if last else width
    result = line.call(
        functools.partial(wide_kernel, len(pairs), travelling is not None, last),
        [shape((height, columns), F32)] * (2 if last else 1),
        [pl.BlockSpec((height, part), lambda j, w: (0, j))] * (2 if last else 1),
        ins,
        specs,
        grid=(tiles,),
        scalars=where,
        scratch=[pltpu.VMEM((width, part), F32)] if last else [],
    )
    return result if last else result[0]


def join_kernel(where, keep, got, *outs):
    mine, theirs = keep[...], got[...]
    low = where[0] == 0
    first, second = jnp.where(low, mine, theirs), jnp.where(low, theirs, mine)
    part = first.shape[1] // len(outs)
    for n, out in enumerate(outs):
        out[:, :part] = first[:, n * part : (n + 1) * part]
        out[:, part:] = second[:, n * part : (n + 1) * part]


def join_halves(line, where, keep, got, count):
    rows, columns = keep.shape
    out = (rows, 2 * columns // count)
    return line.call(
        join_kernel,
        [shape(out, F32)] * count,
        [const_spec(out)] * count,
        [keep, got],
        [const_spec(keep.shape)] * 2,
        scalars=where,
    )


def side_kernel(first, second, out):
    part = first.shape[1]
    out[:, :part] = first[...]
    out[:, part:] = second[...]


def side_by_side(line, first, second):
    rows, columns = first.shape
    spec = const_spec(first.shape)
    out = (rows, 2 * columns)
    return line.call(side_kernel, [shape(out, F32)], [const_spec(out)], [first, second], [spec, spec])[0]


class Plan:
    def __init__(self, line):
        self.line, self.steps, self.found, self.sent = line, {}, {}, {}

    def step(self, name, needs, work):
        self.steps[name] = (needs, work)

    def run(self, *names):
        for name in names:
            if name.startswith("~"):
                if name[1:] in self.sent:
                    self.line.last.append(self.sent[name[1:]])
            elif name in self.steps and name not in self.found:
                needs, work = self.steps[name]
                self.run(*needs)
                self.found[name] = work()

    def __getitem__(self, name):
        return self.found[name]


def on_device(
    dp,
    tensor,
    inputs,
    segments,
    decay_order,
    ln1_gain,
    ln1_bias,
    w_query,
    w_key,
    w_value,
    w_swish,
    w_out,
    ln2_gain,
    ln2_bias,
    w_gate,
    w_up,
    w_down,
    cotangent,
):
    line = Line()
    plan = Plan(line)
    groups = dp // 2
    place = lax.axis_index("dp")
    where = jnp.stack([lax.rem(place, 2), lax.div(place, 2), my_core()]).astype(jnp.int32)
    tables = angle_tables(SEQ_LEN)
    logs = jnp.log1p(-jnp.exp2(-(decay_order + 5).astype(F32)))
    seg_row = segments.reshape(1, SEQ_LEN)
    gain1, bias1, gain2, bias2 = (v.reshape(1, -1) for v in (ln1_gain, ln1_bias, ln2_gain, ln2_bias))
    rows = 2 * BLOCK

    def beside(name, values):
        plan.sent[name] = lax.ppermute(values, "dp", [(i, i ^ 1) for i in range(dp)])
        return plan.sent[name]

    def onward(name, values):
        plan.sent[name] = lax.ppermute(values, "dp", [(i, (i + 2) % dp) for i in range(dp)])
        return plan.sent[name]

    def across(name, values):
        plan.sent[name] = lax.ppermute(values, "tensor", [(i, i ^ 2) for i in range(tensor)])
        return plan.sent[name]


    def projected(n, begin, end):
        before = plan["P0"] if n else None
        result = projections(line, begin, end, inputs, gain1, bias1, tables, w_query, w_key, w_value, w_swish, before)
        return tuple(result[:7]) + (beside("H", result[7]) if n else result[7],)

    def retained(i):
        a, q, k, v, switch = plan["P1" if i else "P0"][:5]
        before = plan[f"R{i - 1}"][1:3] if i else None
        chip, u, o, p = retention(line, i, q, k, v, switch, seg_row, logs, w_out, before)
        return (chip, across(f"R{i}", chip)), u, o, p

    def fed(i):
        before = plan[f"F{i - 1}"] if i else None
        sums = plan[f"R{i}"][0]
        return feed_forward(line, i, *sums, inputs, gain2, bias2, cotangent, w_gate, w_up, w_down, before)

    last = CHUNKS - 1
    plan.step("P0", [], lambda: projected(0, 0, 1))
    plan.step("R0", ["P0"], lambda: retained(0))
    plan.step("P1", ["R0"], lambda: projected(1, 1, CHUNKS))
    for i in range(CHUNKS):
        plan.step(f"R{i}", ["P1", f"R{i - 1}"] if i else ["P0"], lambda i=i: retained(i))
        plan.step(f"F{i}", [f"R{i}"] + ([f"F{i - 1}"] if i else []), lambda i=i: fed(i))
    plan.step("G", ["P1"], lambda: partner_rows(line, plan["P1"][7], gain1, bias1))

    def first(n):
        return plan["P1"][n]


    def summed(name, lefts, rights, transposed, i, count=rows):
        chip = chip_sum(line, count, lefts, rights, transposed, i)
        return chip, across(name, chip)

    pair = range(2)

    def second_sum(i):
        dg, du = plan[f"F{last}"][1:3]
        return summed(f"B{i}", [dg, du], [w_gate, w_up], True, i)

    def middle_back(i):
        before = plan["M1"] if i == 0 else None
        return second_norm_back(line, 2 * i, *plan[f"B{i}"], plan[f"F{last}"][4], gain2, cotangent, before)

    def first_sum(i):
        dq, dk, dv = plan["AB"][:3]
        return summed(f"C{i}", [dq, dk, dv, plan["GB"][1]], [w_query, w_key, w_value, w_swish], True, i)

    def inputs_back(i):
        before = plan["I1"] if i == 0 else None
        return first_norm_back(line, 2 * i, *plan[f"C{i}"], inputs, gain1, plan["M0"][1], before)

    def feed_sum():
        return summed("D", [plan[f"F{last}"][0]], [w_down], False, 0, SEQ_LEN)

    def retention_grads():
        _, q, k, v, _, cos, sin = plan["P1"][:7]
        weights = [plan[f"R{i}"][3] for i in range(CHUNKS)]
        result = retention_back(line, where, q, k, v, plan["GB"][0], seg_row, logs, cos, sin, weights)
        return result[:4] + (beside("Tq", result[4]), beside("Tv", result[5]))

    def gate_grads():
        result = gate_back(line, where, plan["M0"][0], w_out, plan[f"R{last}"][2], first(4))
        return result[:2] + (beside("Ts", result[2]),)

    for i in reversed(pair):
        plan.step(f"B{i}", [f"F{last}"], lambda i=i: second_sum(i))
        plan.step(f"M{i}", [f"B{i}"] + ([] if i else ["M1"]), lambda i=i: middle_back(i))
        plan.step(f"C{i}", ["AB"], lambda i=i: first_sum(i))
        plan.step(f"I{i}", [f"C{i}", "M0"] + ([] if i else ["I1"]), lambda i=i: inputs_back(i))
    plan.step("GB", ["M0"], gate_grads)
    plan.step("AB", ["GB"], retention_grads)
    plan.step("D", [f"F{last}"], feed_sum)
    plan.step("O", ["D"], lambda: output_rows(line, *plan["D"], plan[f"F{last}"][4]))
    plan.step("CI", ["I0"], lambda: own_copy(line, plan["I0"][0]))
    plan.step("CO", ["O"], lambda: own_copy(line, plan["O"]))


    def small_sums():
        ln1 = [plan[f"I{i}"][n] for n in (1, 2) for i in pair]
        ln2 = [plan[f"M{i}"][n] for n in (2, 3) for i in pair]
        parts = ln1 + ln2
        own = [parts[2 * n] + parts[2 * n + 1] for n in range(4)]
        own = jnp.concatenate(own + [jnp.zeros((4, own[0].shape[1]), F32)], axis=0)
        plan.sent["L"] = lax.ppermute(own, "tensor", [(i, i ^ 1) for i in range(tensor)])
        return own, plan.sent["L"]

    plan.step("L", ["I0", "I1", "M0", "M1"], small_sums)


    def products(name, needs, operands, by_rows, extra=tuple, skip=0):
        cut = (groups + 1) // 2

        def send(part, begin, end):
            left, right = operands()
            blocks = sent_blocks(line, where, left, right, by_rows, groups, begin, end - begin, extra(), skip)
            return beside(f"S{name}{part}", blocks)

        def ring(j):
            part, index = ("A", j) if j < cut else ("B", j - cut)
            travelling = plan[f"K{name}{j - 1}"] if j else None
            left, right = operands()
            received = plan[f"S{name}{part}"]
            done = j == groups - 1
            block = kept_block(
                line, where, left, right, by_rows, groups, j, received, index, travelling, extra(), done, skip
            )
            return onward(f"K{name}{j}", block) if j < groups - 1 else block

        plan.step(f"S{name}A", needs, lambda: send("A", 0, cut))
        plan.step(f"S{name}B", needs, lambda: send("B", cut, groups))
        for j in range(groups):
            before = [f"K{name}{j - 1}"] if j else []
            plan.step(f"K{name}{j}", [f"S{name}A" if j < cut else f"S{name}B"] + before, lambda j=j: ring(j))
        return lambda: plan[f"K{name}{groups - 1}"]


    def ring_first(name, needs, operands, columns):
        def ring(j):
            travelling = plan[f"K{name}{j - 1}"] if j else None
            block = wide_block(
                line, where, [operands()], groups, j, travelling, j == groups - 1, columns, False
            )
            if j < groups - 1:
                return onward(f"K{name}{j}", block)
            return beside(f"K{name}{j}", block[0]), block[1]

        for j in range(groups):
            plan.step(f"K{name}{j}", [f"K{name}{j - 1}"] if j else needs, lambda j=j: ring(j))
        plan.step(f"E{name}", [f"K{name}{groups - 1}"], lambda: add(line, *plan[f"K{name}{groups - 1}"]))
        return lambda: plan[f"E{name}"]


    def shares(name, needs, operand, far, count):
        def ring(j):
            travelling = plan[f"J{name}{j - 1}"] if j else None
            right = operand()
            pairs = [(first(0), right), (plan["G"], far())]
            block = wide_block(
                line, where, pairs, groups, j, travelling, j == groups - 1, right.shape[1] // 2, True
            )
            if j < groups - 1:
                return onward(f"J{name}{j}", block)
            return block[1], beside(f"J{name}{j}", block[0])

        for j in range(groups):
            plan.step(f"J{name}{j}", ["G", f"J{name}{j - 1}"] if j else ["G", *needs], lambda j=j: ring(j))
        plan.step(f"E{name}", [f"J{name}{groups - 1}"], lambda: join_halves(line, where, *plan[f"J{name}{groups - 1}"], count))
        return lambda: plan[f"E{name}"]

    fed_all = lambda n: plan[f"F{last}"][n]
    normed2 = lambda: plan[f"F{last}"][3]
    down = products("d", [f"F{last}"], lambda: (fed_all(0), cotangent), False)
    gate = products("g", [f"F{last}"], lambda: (normed2(), fed_all(1)), True)
    half_ff = w_up.shape[1] // 2
    up = ring_first("u", [f"F{last}"], lambda: (normed2(), fed_all(2)), half_ff)
    more_up = products("w", [f"F{last}"], lambda: (normed2(), fed_all(2)), True, skip=half_ff)
    out = products("o", ["M0", "L"], lambda: (plan[f"R{last}"][1], plan["M0"][0]), False, lambda: plan["L"])
    plan.step("U", ["Eu", f"Kw{groups - 1}"], lambda: side_by_side(line, up(), more_up()))
    swish = shares("s", ["GB"], lambda: plan["GB"][1], lambda: plan["GB"][2], 1)
    vgrad = shares("v", ["AB"], lambda: plan["AB"][2], lambda: plan["AB"][5], 1)
    both = shares("q", ["AB"], lambda: plan["AB"][3], lambda: plan["AB"][4], 2)

    plan.run(
        "P0", "R0", "P1", "R1", "F0", "R2", "R3", "F1", "F2", "F3", "SgA", "Ku0", "B1", "SdA", "SwA", "Ku1", "B0",
        "Kg0", "SgB", "G", "Ku2", "Kg1", "M1", "SwB", "Kd0", "~Ku2", "M0", "Kw0", "GB", "AB", "Kd1", "Kg2", "Kw1",
        "C1", "Kg3", "Jq0", "~Kd1", "C0", "Jq1", "I1", "~Kw1", "Js0", "D", "Jq2", "Kw2", "I0", "Js1", "SoA", "Jq3",
        "SdB", "SoB", "Jv0", "Js2", "Kw3", "Ku3", "Ko0", "Jv1", "Kd2", "Ko1", "Js3", "O", "Jv2", "Eu", "CO", "Ko2",
        "U", "Jv3", "Eq", "Ko3", "Ev", "Es", "CI", "Kd3",
    )
    plan.run(*plan.steps)
    query, key = both()
    grad_out, small = out()
    return (
        plan["CO"],
        plan["CI"],
        small[0],
        small[1],
        query,
        key,
        vgrad()[0],
        swish()[0],
        grad_out,
        small[2],
        small[3],
        gate(),
        plan["U"],
        down(),
    )


def solution(mesh):
    dp, tensor = mesh.shape["dp"], mesh.shape["tensor"]

    def body(*arrays):
        return on_device(dp, tensor, *arrays)

    return jax.shard_map(
        body,
        mesh=mesh,
        in_specs=(
            P("dp", None),
            P("dp", None),
            P("tensor"),
            P(),
            P(),
            P(None, "tensor"),
            P(None, "tensor"),
            P(None, "tensor"),
            P(None, "tensor"),
            P("tensor", None),
            P(),
            P(),
            P(None, "tensor"),
            P(None, "tensor"),
            P("tensor", None),
            P("dp", None),
        ),
        out_specs=(
            P("dp", None),
            P("dp", None),
            P("dp"),
            P("dp"),
            P("dp", "tensor"),
            P("dp", "tensor"),
            P("dp", "tensor"),
            P("dp", "tensor"),
            P("tensor", "dp"),
            P("dp"),
            P("dp"),
            P("dp", "tensor"),
            P("dp", "tensor"),
            P("tensor", "dp"),
        ),
        check_vma=False,
    )
```

```python
import functools

import jax
import jax.numpy as jnp
import numpy as np
from jax import lax
from jax.experimental import pallas as pl
from jax.experimental.pallas import tpu as pltpu
from jax.sharding import PartitionSpec as P

KEY = 256
VALUE = 512
SEQ_LEN = 1024
DOC_MOST = 512
BLOCK = 256
CHUNKS = SEQ_LEN // BLOCK
HALF = BLOCK // 2
BF16 = jnp.bfloat16
F32 = jnp.float32
MIB = 1 << 20


def product_tn(left, right):
    return lax.dot_general(left, right, (((0,), (0,)), ((), ())), preferred_element_type=F32)


def product_nt(left, right):
    return lax.dot_general(left, right, (((1,), (1,)), ((), ())), preferred_element_type=F32)


def product_nn(left, right):
    return jnp.dot(left, right, preferred_element_type=F32)


def angle_tables(length):
    column = np.arange(KEY) // 2
    frequency = 10000.0 ** (-column / (KEY // 2 - 1))
    inside = np.arange(BLOCK)[:, None] * frequency[None, :]
    starts = np.arange(0, length, BLOCK)[:, None] * frequency[None, :]
    tables = (np.cos(inside), np.sin(inside), np.cos(starts), np.sin(starts))
    return tuple(jnp.asarray(table.astype(np.float32)) for table in tables)


def rotate(values, cosines, sines, sign):
    even = lax.broadcasted_iota(jnp.int32, values.shape, 1) % 2 == 0
    after = pltpu.roll(values, KEY - 1, 1)
    before = pltpu.roll(values, 1, 1)
    return values * cosines + sign * jnp.where(even, -after, before) * sines


def normal_rows(values, eps):
    average = jnp.mean(values, axis=-1, keepdims=True)
    centred = values - average
    spread = jnp.mean(centred * centred, axis=-1, keepdims=True)
    return centred, lax.rsqrt(spread + eps)


def down_rows(seg):
    return jnp.transpose(jnp.broadcast_to(seg.astype(F32), (BLOCK, BLOCK)))


def decay_block(log_keep, seg_rows, seg, row_start, column_start):
    rows = row_start + lax.broadcasted_iota(jnp.int32, (BLOCK, BLOCK), 0)
    columns = column_start + lax.broadcasted_iota(jnp.int32, (BLOCK, BLOCK), 1)
    gap = rows - columns
    keep = (seg_rows == seg.astype(F32)) & (gap >= 0)
    return jnp.where(keep, jnp.exp(jnp.maximum(gap, 0).astype(F32) * log_keep), 0.0)


def first_key_block(chunk):
    return max(0, chunk - (DOC_MOST + BLOCK - 2) // BLOCK)


class Line:
    def __init__(self):
        self.last = []
        self.shared = 0

    def call(
        self,
        kernel,
        outs,
        out_specs,
        ins,
        in_specs,
        grid=(1,),
        scalars=None,
        scratch=(),
        vmem=63,
        onto=(),
        paired=False,
    ):
        held = list(ins) + [array for _, array in onto]
        extra = held[len(ins) :] + [array for array in self.last if not any(array is other for other in held)]
        scalar_count = 0 if scalars is None else 1
        in_count = len(ins)
        skipped = len(extra)

        def body(*refs):
            head, rest = refs[: scalar_count + in_count], refs[scalar_count + in_count + skipped :]
            kernel(*head, *rest)

        specs = list(in_specs) + [pl.BlockSpec(memory_space=pl.ANY)] * skipped
        arguments = ([] if scalars is None else [scalars]) + list(ins) + extra
        extras = {}
        if paired:
            extras = dict(collective_id=self.shared, has_side_effects=True)
            self.shared += 1
        result = pl.pallas_call(
            body,
            out_shape=tuple(outs),
            grid_spec=pltpu.PrefetchScalarGridSpec(
                num_scalar_prefetch=scalar_count,
                grid=grid,
                in_specs=specs,
                out_specs=tuple(out_specs),
                scratch_shapes=list(scratch),
            ),
            input_output_aliases={scalar_count + in_count + n: out for n, (out, _) in enumerate(onto)},
            compiler_params=pltpu.CompilerParams(
                vmem_limit_bytes=vmem * MIB,
                dimension_semantics=("arbitrary",) * len(grid),
                **extras,
            ),
            cost_estimate=pl.CostEstimate(flops=1, bytes_accessed=1, transcendentals=0),
        )(*arguments)
        self.last = [result[0]]
        return result


def my_core():
    return lax.rem(lax.axis_index("tensor"), 2)


def other_core():
    rank = lax.axis_index("tensor")
    return {"tensor": rank + 1 - 2 * lax.rem(rank, 2)}


def meet_other_core():
    barrier = pltpu.get_barrier_semaphore()
    pl.semaphore_signal(barrier, inc=1, device_id=other_core(), device_id_type=pl.DeviceIdType.MESH)
    pl.semaphore_wait(barrier, 1)


def to_other_core(source, target, sent, arrived):
    return pltpu.make_async_remote_copy(
        src_ref=source,
        dst_ref=target,
        send_sem=sent,
        recv_sem=arrived,
        device_id=other_core(),
        device_id_type=pl.DeviceIdType.MESH,
    )


def core_rows(mine, block):
    core = my_core() if mine else 1 - my_core()
    return pl.ds(pl.multiple_of(block * BLOCK + core * HALF, HALF), HALF)


def shape(dims, kind):
    return jax.ShapeDtypeStruct(dims, kind)


def const_spec(dims):
    return pl.BlockSpec(dims, lambda *_: (0,) * len(dims))


def once_spec(dims):
    return pl.BlockSpec(dims, lambda *_: (0,) * len(dims), pipeline_mode=pl.Buffered(1))


def row_spec(rows, columns, chunk):
    return pl.BlockSpec((rows, columns), lambda *_: (chunk, 0))


SMEM = pl.BlockSpec(memory_space=pltpu.SMEM)
ANY = pl.BlockSpec(memory_space=pl.ANY)


def fetch_scratch(*arrays):
    return [pltpu.VMEM(a.shape, a.dtype) for a in arrays] + [pltpu.SemaphoreType.DMA((len(arrays),))]


def fetched(sources, held):
    places, done = held[:-1], held[-1]
    copies = [pltpu.make_async_copy(s, p, done.at[n]) for n, (s, p) in enumerate(zip(sources, places))]
    return places, copies


def proj_kernel(begin, fetching, x, gain, bias, cos, sin, cos0, sin0, *refs):
    wq, wk, wv, ws, a_out, q_out, k_out, v_out, s_out, c_out, n_out, x_out = refs[:12]
    chunk = begin + pl.program_id(0)
    if fetching:
        (wq, wk, wv, ws), fetch = fetched((wq, wk, wv, ws), refs[12:])
        for copy in fetch:
            copy.start()

    def ready(n):
        if fetching:
            fetch[n].wait()

    centred, scale = normal_rows(x[...].astype(F32), 1e-05)
    normed = (centred * scale * gain[...] + bias[...]).astype(BF16)
    a_out[...] = normed
    x_out[...] = x[core_rows(True, 0), :].astype(F32)
    first_cos, first_sin = cos0[pl.ds(chunk, 1), :], sin0[pl.ds(chunk, 1), :]
    cosines = cos[...] * first_cos - sin[...] * first_sin
    sines = sin[...] * first_cos + cos[...] * first_sin
    c_out[...] = cosines
    n_out[...] = sines
    parts = [slice(n, n + KEY) for n in range(0, wq.shape[1], KEY)]
    ready(0)
    for part in parts:
        query = product_nn(normed, wq[:, part])
        q_out[:, part] = rotate(query, cosines, sines, 1.0).astype(BF16)
    ready(1)
    for part in parts:
        turned = rotate(product_nn(normed, wk[:, part]), cosines, sines, 1.0) * float(KEY) ** (-0.5)
        k_out[:, part] = turned.astype(BF16)
    parts = [slice(n, n + VALUE) for n in range(0, wv.shape[1], VALUE)]
    ready(2)
    for part in parts:
        v_out[:, part] = product_nn(normed, wv[:, part]).astype(BF16)
    ready(3)
    for part in parts:
        s_out[:, part] = product_nn(normed, ws[:, part])


def projections(line, begin, end, x, gain, bias, tables, wq, wk, wv, ws, before):
    rows, width = x.shape
    kw, vw = wq.shape[1], wv.shape[1]
    wide = [(width, BF16), (kw, BF16), (kw, BF16), (vw, BF16), (vw, F32), (KEY, F32), (KEY, F32)]

    def chunked(columns):
        return pl.BlockSpec((BLOCK, columns), lambda i: (begin + i, 0))

    weights = (wq, wk, wv, ws)
    alone = end - begin == 1
    return line.call(
        functools.partial(proj_kernel, begin, alone),
        [shape((rows, columns), kind) for columns, kind in wide] + [shape((rows // 2, width), F32)],
        [chunked(columns) for columns, _ in wide] + [pl.BlockSpec((HALF, width), lambda i: (begin + i, 0))],
        [x, gain, bias, *tables, wq, wk, wv, ws],
        [chunked(width), const_spec((1, width)), const_spec((1, width))]
        + [const_spec(table.shape) for table in tables]
        + ([ANY] * 4 if alone else [once_spec(w.shape) for w in weights]),
        grid=(end - begin,),
        scratch=fetch_scratch(*weights) if alone else [],
        onto=() if before is None else tuple(enumerate(before)),
    )


TILES = 4


def retain_kernel(
    chunk, q, k, v, switch, seg_row, logs, w, chip, u_out, o_out, p_out, full, sent, got, s1, s2, *held
):
    (w,), (fetch,) = fetched((w,), held)
    fetch.start()
    meet_other_core()
    seg_rows = down_rows(seg_row[:, chunk * BLOCK : (chunk + 1) * BLOCK])
    heads = q.shape[1] // KEY
    low = first_key_block(chunk)
    for head in range(heads):
        kpart, vpart = slice(head * KEY, (head + 1) * KEY), slice(head * VALUE, (head + 1) * VALUE)
        total = None
        for block in range(low, chunk + 1):
            rows = slice(block * BLOCK, (block + 1) * BLOCK)
            raw = product_nt(q[:, kpart], k[rows, kpart])
            mask = decay_block(logs[head], seg_rows, seg_row[:, rows], chunk * BLOCK, block * BLOCK)
            weights = (raw * mask).astype(BF16)
            p_out[head, :, (block - low) * BLOCK : (block - low + 1) * BLOCK] = weights
            part = product_nn(weights, v[rows, vpart])
            total = part if total is None else total + part
        o_out[:, vpart] = total
        centred, scale = normal_rows(total, 1.0)
        gate = switch[:, vpart]
        u_out[:, vpart] = (centred * scale * (gate * jax.nn.sigmoid(gate))).astype(BF16)
    tile = w.shape[1] // TILES
    copies = []
    fetch.wait()
    for j in range(TILES):
        columns = slice(j * tile, (j + 1) * tile)
        full[:, columns] = product_nn(u_out[...], w[:, columns])
        sent[j] = full[core_rows(False, 0), columns]
        copies.append(to_other_core(sent.at[j], got.at[j], s1.at[j], s2.at[j]))
        copies[-1].start()
    for j in range(TILES):
        columns = slice(j * tile, (j + 1) * tile)
        copies[j].wait()
        chip[:, columns] = full[core_rows(True, 0), columns] + got[j]


def retention(line, chunk, q, k, v, switch, seg_row, logs, w, before):
    rows, kw = q.shape
    vw, width = v.shape[1], w.shape[1]
    heads = kw // KEY
    blocks = chunk + 1 - first_key_block(chunk)
    return line.call(
        functools.partial(retain_kernel, chunk),
        [
            shape((HALF, width), F32),
            shape((rows, vw), BF16),
            shape((rows, vw), F32),
            shape((heads, BLOCK, blocks * BLOCK), BF16),
        ],
        [
            const_spec((HALF, width)),
            row_spec(BLOCK, vw, chunk),
            row_spec(BLOCK, vw, chunk),
            const_spec((heads, BLOCK, blocks * BLOCK)),
        ],
        [q, k, v, switch, seg_row, logs, w],
        [
            row_spec(BLOCK, kw, chunk),
            const_spec(((chunk + 1) * BLOCK, kw)),
            const_spec(((chunk + 1) * BLOCK, vw)),
            row_spec(BLOCK, vw, chunk),
            const_spec(seg_row.shape),
            SMEM,
            ANY,
        ],
        scratch=[
            pltpu.VMEM((BLOCK, width), F32),
            pltpu.VMEM((TILES, HALF, width // TILES), F32),
            pltpu.VMEM((TILES, HALF, width // TILES), F32),
            pltpu.SemaphoreType.DMA((TILES,)),
            pltpu.SemaphoreType.DMA((TILES,)),
            *fetch_scratch(w),
        ],
        onto=() if before is None else ((1, before[0]), (2, before[1])),
        paired=True,
    )


PIECES = 2


def feed_kernel(
    chunk, chip, crossed, x, gain, bias, c, wg, wu, wd, hid_out, dg_out, du_out, a_out, h_out, back, *held
):
    places, loaded, sent, got, s1, s2 = held[:4], held[4], *held[5:]
    c_in, wd_in, wg_in, wu_in = places
    ff = back.shape[1]
    tile = ff // TILES
    tokens = c.at[pl.ds(chunk * BLOCK, BLOCK)]
    fetch = [pltpu.make_async_copy(tokens, c_in, loaded.at[0]), pltpu.make_async_copy(wd, wd_in, loaded.at[1])]
    for n, (source, place) in enumerate(((wg, wg_in), (wu, wu_in))):
        for t in range(TILES):
            columns = pl.ds(t * tile, tile)
            semaphore = loaded.at[2 + 2 * t + n]
            fetch.append(pltpu.make_async_copy(source.at[:, columns], place.at[:, columns], semaphore))
    for copy in fetch:
        copy.start()
    meet_other_core()
    piece = HALF // PIECES
    copies = []
    for n in range(PIECES):
        part = pl.ds(n * piece, piece)
        rows = pl.ds(pl.multiple_of(my_core() * HALF + n * piece, piece), piece)
        copies.append(to_other_core(sent.at[part], got.at[part], s1.at[n], s2.at[n]))
        middle = x[rows, :].astype(F32) + (chip[part, :] + crossed[part, :])
        h_out[part, :] = middle
        centred, scale = normal_rows(middle, 1e-05)
        normed = (centred * scale * gain[...] + bias[...]).astype(BF16)
        sent[part, :] = normed.astype(F32)
        copies[n].start()
        a_out[rows, :] = normed
    fetch[0].wait()
    fetch[1].wait()
    for t in range(TILES):
        columns = slice(t * tile, (t + 1) * tile)
        back[:, columns] = product_nt(c_in[...], wd_in[columns, :])
    for n in range(PIECES):
        rows = pl.ds(pl.multiple_of((1 - my_core()) * HALF + n * piece, piece), piece)
        copies[n].wait()
        a_out[rows, :] = got[pl.ds(n * piece, piece), :].astype(BF16)
    factor = 0.7978845608028654
    for t in range(TILES):
        columns = slice(t * tile, (t + 1) * tile)
        fetch[2 + t].wait()
        fetch[2 + TILES + t].wait()
        gate = product_nn(a_out[...], wg_in[:, columns])
        up = product_nn(a_out[...], wu_in[:, columns])
        bent = jnp.tanh(factor * (gate + 0.044715 * (gate * gate * gate)))
        half = 0.5 * (1.0 + bent)
        active = gate * half
        slope = half + 0.5 * gate * (1.0 - bent * bent) * (factor * (1.0 + 3 * 0.044715 * gate * gate))
        hid_out[:, columns] = (active * up).astype(BF16)
        dg_out[:, columns] = (back[:, columns] * up * slope).astype(BF16)
        du_out[:, columns] = (back[:, columns] * active).astype(BF16)


def feed_forward(line, chunk, chip, crossed, x, gain, bias, c, wg, wu, wd, before):
    total, width = x.shape
    ff = wg.shape[1]
    return line.call(
        functools.partial(feed_kernel, chunk),
        [shape((total, ff), BF16)] * 3 + [shape((total, width), BF16), shape((total // 2, width), F32)],
        [row_spec(BLOCK, ff, chunk)] * 3 + [row_spec(BLOCK, width, chunk), row_spec(HALF, width, chunk)],
        [chip, crossed, x, gain, bias, c, wg, wu, wd],
        [
            const_spec((HALF, width)),
            const_spec((HALF, width)),
            row_spec(BLOCK, width, chunk),
            const_spec((1, width)),
            const_spec((1, width)),
        ]
        + [ANY] * 4,
        scratch=[
            pltpu.VMEM((BLOCK, ff), F32),
            pltpu.VMEM((BLOCK, width), BF16),
            pltpu.VMEM(wd.shape, BF16),
            pltpu.VMEM(wg.shape, BF16),
            pltpu.VMEM(wu.shape, BF16),
            pltpu.SemaphoreType.DMA((2 + 2 * TILES,)),
            pltpu.VMEM((HALF, width), F32),
            pltpu.VMEM((HALF, width), F32),
            pltpu.SemaphoreType.DMA((PIECES,)),
            pltpu.SemaphoreType.DMA((PIECES,)),
        ],
        onto=() if before is None else tuple(enumerate(before)),
        paired=True,
    )


def chip_kernel(count, transposed, steps, *refs):
    lefts, rights = refs[:count], refs[count : 2 * count]
    out, full, kept, sent, got, s1, s2 = refs[2 * count :]
    half = kept.shape[1]
    j = pl.program_id(0)

    @pl.when(j == 0)
    def _():
        meet_other_core()

    @pl.when(j < steps)
    def _():
        total = None
        for left, right in zip(lefts, rights):
            part = product_nt(left[...], right[...]) if transposed else product_nn(left[...], right[...])
            total = part if total is None else total + part
        full[...] = total
        for n in range(half // HALF):
            part = slice(n * HALF, (n + 1) * HALF)
            sent[j, part] = full[core_rows(False, n), :]
            kept[j, part] = full[core_rows(True, n), :]
        to_other_core(sent.at[j], got.at[j], s1.at[j], s2.at[j]).start()

    @pl.when(j > 0)
    def _():
        to_other_core(sent.at[j - 1], got.at[j - 1], s1.at[j - 1], s2.at[j - 1]).wait()
        out[...] = kept[j - 1] + got[j - 1]


def chip_sum(line, rows, lefts, rights, transposed, chunk):
    width = rights[0].shape[0] if transposed else rights[0].shape[1]
    tile = 512
    steps = width // tile
    half = rows // 2
    right_specs = [
        pl.BlockSpec((tile, right.shape[1]), lambda i: (jnp.minimum(i, steps - 1), 0))
        if transposed
        else pl.BlockSpec((right.shape[0], tile), lambda i: (0, jnp.minimum(i, steps - 1)))
        for right in rights
    ]
    left_specs = [row_spec(rows, left.shape[1], chunk) for left in lefts]
    return line.call(
        functools.partial(chip_kernel, len(lefts), transposed, steps),
        [shape((half, width), F32)],
        [pl.BlockSpec((half, tile), lambda i: (0, jnp.maximum(i, 1) - 1))],
        list(lefts) + list(rights),
        left_specs + right_specs,
        grid=(steps + 1,),
        scratch=[
            pltpu.VMEM((rows, tile), F32),
            pltpu.VMEM((steps, half, tile), F32),
            pltpu.VMEM((steps, half, tile), F32),
            pltpu.VMEM((steps, half, tile), F32),
            pltpu.SemaphoreType.DMA((steps,)),
            pltpu.SemaphoreType.DMA((steps,)),
        ],
        paired=True,
    )[0]


def shared_kernel(work, in_count, steps, *refs):
    ins, out = refs[:in_count], refs[in_count]
    extras, (sent, got, s1, s2) = refs[in_count + 1 : -4], refs[-4:]
    j = pl.program_id(0)

    @pl.when(j == 0)
    def _():
        meet_other_core()

    @pl.when(j < steps)
    def _():
        sent[j] = work(*ins, *extras)
        to_other_core(sent.at[j], got.at[j], s1.at[j], s2.at[j]).start()

    @pl.when(j > 0)
    def _():
        to_other_core(sent.at[j - 1], got.at[j - 1], s1.at[j - 1], s2.at[j - 1]).wait()
        out[core_rows(True, 0), :] = sent[j - 1].astype(out.dtype)
        out[core_rows(False, 0), :] = got[j - 1].astype(out.dtype)


def shared_rows(line, work, begin, steps, ins, in_specs, kind, total_rows, width, extras=(), before=()):
    return line.call(
        functools.partial(shared_kernel, work, len(ins), steps),
        [shape((total_rows, width), kind)] + [shape(dims, F32) for dims, _ in extras],
        [pl.BlockSpec((BLOCK, width), lambda j: (begin + jnp.maximum(j, 1) - 1, 0))] + [spec for _, spec in extras],
        ins,
        in_specs,
        grid=(steps + 1,),
        scratch=[
            pltpu.VMEM((steps, HALF, width), F32),
            pltpu.VMEM((steps, HALF, width), F32),
            pltpu.SemaphoreType.DMA((steps,)),
            pltpu.SemaphoreType.DMA((steps,)),
        ],
        onto=before,
        paired=True,
    )


def stepped(rows, width, steps, begin=0):
    return pl.BlockSpec((rows, width), lambda j: (begin + jnp.minimum(j, steps - 1), 0))


def partner_work(got, gain, bias):
    centred, scale = normal_rows(got[...], 1e-05)
    return (centred * scale * gain[...] + bias[...]).astype(BF16).astype(F32)


def partner_rows(line, got, gain, bias):
    half, width = got.shape
    steps = half // HALF
    specs = [stepped(HALF, width, steps), const_spec((1, width)), const_spec((1, width))]
    return shared_rows(line, partner_work, 0, steps, [got, gain, bias], specs, BF16, 2 * half, width)[0]


def norm_back(back, centred, scale, gain, gain_out, bias_out):
    normed = centred * scale
    begin = pl.program_id(0) == 0
    one, two = jnp.sum(back * normed, axis=0, keepdims=True), jnp.sum(back, axis=0, keepdims=True)

    @pl.when(begin)
    def _():
        gain_out[...] = one
        bias_out[...] = two

    @pl.when(jnp.logical_not(begin))
    def _():
        gain_out[...] += one
        bias_out[...] += two

    scaled = back * gain[...]
    first = jnp.mean(scaled, axis=-1, keepdims=True)
    second = jnp.mean(scaled * normed, axis=-1, keepdims=True)
    return scale * (scaled - first - normed * second)


def middle_work(chip, crossed, h, gain, c, dh_out, gain_out, bias_out):
    centred, scale = normal_rows(h[...], 1e-05)
    back = chip[...] + crossed[...]
    value = c[core_rows(True, 0), :].astype(F32) + norm_back(back, centred, scale, gain, gain_out, bias_out)
    dh_out[...] = value
    return value


def second_norm_back(line, begin, chip, crossed, h, gain, c, before):
    total, width = c.shape
    steps = chip.shape[0] // HALF
    part, own = stepped(HALF, width, steps), stepped(HALF, width, steps, begin)
    small = ((1, width), const_spec((1, width)))
    return shared_rows(
        line,
        middle_work,
        begin,
        steps,
        [chip, crossed, h, gain, c],
        [part, part, own, const_spec((1, width)), stepped(BLOCK, width, steps, begin)],
        BF16,
        total,
        width,
        [((total // 2, width), own), small, small],
        () if before is None else ((0, before[0]), (1, before[1])),
    )


def first_work(chip, crossed, x, gain, dh, gain_out, bias_out):
    centred, scale = normal_rows(x[core_rows(True, 0), :].astype(F32), 1e-05)
    back = chip[...] + crossed[...]
    return dh[...] + norm_back(back, centred, scale, gain, gain_out, bias_out)


def first_norm_back(line, begin, chip, crossed, x, gain, dh, before):
    total, width = x.shape
    steps = chip.shape[0] // HALF
    part, own = stepped(HALF, width, steps), stepped(HALF, width, steps, begin)
    small = ((1, width), const_spec((1, width)))
    return shared_rows(
        line,
        first_work,
        begin,
        steps,
        [chip, crossed, x, gain, dh],
        [part, part, stepped(BLOCK, width, steps, begin), const_spec((1, width)), own],
        F32,
        total,
        width,
        [small, small],
        () if before is None else ((0, before[0]),),
    )


def output_work(chip, crossed, h):
    return h[...] + (chip[...] + crossed[...])


def output_rows(line, chip, crossed, h):
    half, width = h.shape
    steps = half // HALF
    specs = [stepped(HALF, width, steps)] * 3
    return shared_rows(line, output_work, 0, steps, [chip, crossed, h], specs, BF16, 2 * half, width)[0]


def copy_kernel(source, out):
    out[...] = source[...]


def own_copy(line, source):
    rows, width = source.shape
    spec = pl.BlockSpec((BLOCK, width), lambda i: (i, 0))
    return line.call(copy_kernel, [shape(source.shape, source.dtype)], [spec], [source], [spec], grid=(rows // BLOCK,))[0]


def add_kernel(a, b, out):
    out[...] = a[...] + b[...]


def add(line, a, b):
    spec = const_spec(a.shape)
    return line.call(add_kernel, [shape(a.shape, F32)], [spec], [a, b], [spec, spec])[0]


def gate_kernel(where, dz, w, o, switch, do_out, ds_out, far_out):
    for head in range(o.shape[1] // VALUE):
        part = slice(head * VALUE, (head + 1) * VALUE)
        grad = product_nt(dz[...], w[part, :])
        centred, scale = normal_rows(o[:, part], 1.0)
        gate = switch[:, part]
        sig = jax.nn.sigmoid(gate)
        ds = (grad * (centred * scale) * (sig * (1.0 + gate * (1.0 - sig)))).astype(BF16)
        ds_out[:, part] = ds
        dn = grad * (gate * sig)
        one = jnp.mean(dn, axis=-1, keepdims=True)
        two = jnp.mean(dn * centred, axis=-1, keepdims=True)
        do_out[:, part] = (scale * (dn - one) - (scale * scale * scale) * centred * two).astype(BF16)

        @pl.when(where[0] != head)
        def _(ds=ds):
            far_out[...] = ds.astype(F32)


def gate_back(line, where, dz, w, o, switch):
    rows, vw = o.shape

    def rowed(columns):
        return pl.BlockSpec((BLOCK, columns), lambda n, w: (n, 0))

    return line.call(
        gate_kernel,
        [shape((rows, vw), BF16), shape((rows, vw), BF16), shape((rows, vw // 2), F32)],
        [rowed(vw), rowed(vw), rowed(vw // 2)],
        [dz, w, o, switch],
        [rowed(dz.shape[1]), const_spec(w.shape), rowed(vw), rowed(vw)],
        grid=(rows // BLOCK,),
        scalars=where,
    )


def retain_back_kernel(where, q, k, v, do, seg_row, logs, cos, sin, *rest):
    weights = rest[:CHUNKS]
    dq_out, dk_out, dv_out, both_out, far_out, far_v_out, dq_sum, dk_sum, dv_sum = rest[CHUNKS:]
    head = pl.program_id(0)
    dk_sum[...] = jnp.zeros_like(dk_sum)
    dv_sum[...] = jnp.zeros_like(dv_sum)
    for chunk in range(CHUNKS):
        low = first_key_block(chunk)
        here = slice(chunk * BLOCK, (chunk + 1) * BLOCK)
        seg_rows = down_rows(seg_row[:, here])
        total = None
        for block in range(low, chunk + 1):
            rows = slice(block * BLOCK, (block + 1) * BLOCK)
            part = slice((block - low) * BLOCK, (block - low + 1) * BLOCK)
            mask = decay_block(logs[head], seg_rows, seg_row[:, rows], chunk * BLOCK, block * BLOCK)
            scores = (product_nt(do[here, :], v[rows, :]) * mask).astype(BF16)
            dv_sum[rows, :] += product_tn(weights[chunk][0, :, part], do[here, :])
            dk_sum[rows, :] += product_tn(scores, q[here, :])
            term = product_nn(scores, k[rows, :])
            total = term if total is None else total + term
        dq_sum[here, :] = total
    dq = rotate(dq_sum[...], cos[...], sin[...], -1.0).astype(BF16)
    dk = (rotate(dk_sum[...], cos[...], sin[...], -1.0) * float(KEY) ** (-0.5)).astype(BF16)
    dq_out[...] = dq
    dk_out[...] = dk
    both_out[:, :KEY] = dq
    both_out[:, KEY:] = dk
    dv = dv_sum[...].astype(BF16)
    dv_out[...] = dv

    @pl.when(where[0] != head)
    def _():
        far_out[:, :KEY] = dq.astype(F32)
        far_out[:, KEY:] = dk.astype(F32)
        far_v_out[...] = dv.astype(F32)


def retention_back(line, where, q, k, v, do, seg_row, logs, cos, sin, weights):
    rows, kw = q.shape
    vw = v.shape[1]

    def headed(columns):
        return pl.BlockSpec((rows, columns), lambda h, w: (0, h))

    return line.call(
        retain_back_kernel,
        [shape((rows, columns), BF16) for columns in (kw, kw, vw, 2 * kw)]
        + [shape((rows, 2 * KEY), F32), shape((rows, VALUE), F32)],
        [headed(KEY), headed(KEY), headed(VALUE), headed(2 * KEY)]
        + [const_spec((rows, 2 * KEY)), const_spec((rows, VALUE))],
        [q, k, v, do, seg_row, logs, cos, sin] + list(weights),
        [
            headed(KEY),
            headed(KEY),
            headed(VALUE),
            headed(VALUE),
            const_spec(seg_row.shape),
            SMEM,
            const_spec(cos.shape),
            const_spec(sin.shape),
        ]
        + [pl.BlockSpec((1,) + part.shape[1:], lambda h, w: (h, 0, 0)) for part in weights],
        grid=(kw // KEY,),
        scalars=where,
        scratch=[pltpu.VMEM((rows, KEY), F32), pltpu.VMEM((rows, KEY), F32), pltpu.VMEM((rows, VALUE), F32)],
    )


def outer_place(where, position, groups):
    return lax.rem(where[1] + 2 * groups - 1 - position, groups)


def column_block(where, position, groups, own):
    return outer_place(where, position, groups) * 2 + (where[0] if own else 1 - where[0])


def plain_block(where, left, right, by_rows, groups, position, own, extra, skip):
    width = (left if by_rows else right).shape[1] // (2 * groups)
    column = column_block(where, position, groups, own) * width
    if by_rows:
        return product_tn(lax.dynamic_slice_in_dim(left, column, width, 1), right[:, skip:])
    block = product_tn(left, lax.dynamic_slice_in_dim(right, column, width, 1))
    if extra:
        more = lax.dynamic_slice_in_dim(extra[0] + extra[1], column, width, 1)
        block = jnp.concatenate([block, more], axis=0)
    return block


def sent_kernel(where, left, right, *rest):
    extra, out = rest[:-1], rest[-1]
    rows = left.shape[1]
    out[0, :rows] = product_tn(left[...], right[...])
    if extra:
        out[0, rows:] = extra[0][...] + extra[1][...]


def sent_blocks(line, where, left, right, by_rows, groups, first, count, extra=(), skip=0):
    width = (left if by_rows else right).shape[1] // (2 * groups)
    if width % 128:
        blocks = [plain_block(where, left, right, by_rows, groups, first + j, False, extra, skip) for j in range(count)]
        return jnp.stack(blocks)
    rows = left.shape[0]
    moving = pl.BlockSpec((rows, width), lambda j, w: (0, column_block(w, first + j, groups, False)))
    more = extra[0].shape[0] if extra else 0
    columns = right.shape[1] - skip
    block = (width, columns) if by_rows else (left.shape[1] + more, width)
    fixed = pl.BlockSpec((rows, columns), lambda j, w: (0, skip // columns))
    specs = [moving if by_rows else const_spec(left.shape), fixed if by_rows else moving]
    small = pl.BlockSpec((more, width), lambda j, w: (0, column_block(w, first + j, groups, False)))
    return line.call(
        sent_kernel,
        [shape((count,) + block, F32)],
        [pl.BlockSpec((1,) + block, lambda j, w: (j, 0, 0))],
        [left, right, *extra],
        specs + [small] * len(extra),
        grid=(count,),
        scalars=where,
    )[0]


def kept_kernel(has_travelling, extra_count, where, left, right, received, *rest):
    more, rest = rest[:extra_count], rest[extra_count:]
    total = product_tn(left[...], right[...])
    rows = total.shape[0]
    total = total + received[0, :rows]
    if has_travelling:
        total = total + rest[0][:rows]
    if not extra_count:
        rest[-1][...] = total
        return
    small = more[0][...] + more[1][...] + received[0, rows:]
    if has_travelling:
        small = small + rest[0][rows:]
    outs = rest[1:] if has_travelling else rest
    outs[0][:rows] = total
    if len(outs) == 2:
        outs[1][...] = small
    else:
        outs[0][rows:] = small


def kept_block(
    line, where, left, right, by_rows, groups, position, received, index, travelling, extra=(), last=False, skip=0
):
    width = (left if by_rows else right).shape[1] // (2 * groups)
    if width % 128:
        block = plain_block(where, left, right, by_rows, groups, position, True, extra, skip) + received[index]
        block = block if travelling is None else block + travelling
        return (block[: left.shape[1]], block[left.shape[1] :]) if extra and last else block
    if extra:
        return extended_block(line, where, left, right, groups, position, received, index, travelling, extra, last)
    rows, columns = left.shape[0], right.shape[1] - skip
    tiles = 1 if skip else 2
    moving = pl.BlockSpec((rows, width), lambda j, w: (0, column_block(w, position, groups, True)))
    if by_rows:
        part = columns // tiles
        left_spec, right_spec = moving, pl.BlockSpec((rows, part), lambda j, w: (0, skip // part + j))
        block, piece, at = (width, columns), (width, part), lambda j: (0, j)
    else:
        part = left.shape[1] // tiles
        left_spec, right_spec = pl.BlockSpec((rows, part), lambda j, w: (0, j)), moving
        block, piece, at = (left.shape[1], width), (part, width), lambda j: (j, 0)
    flat = pl.BlockSpec(piece, lambda j, w: at(j))
    ins = [left, right, received] + ([] if travelling is None else [travelling])
    specs = [left_spec, right_spec, pl.BlockSpec((1,) + piece, lambda j, w: (index,) + at(j))]
    return line.call(
        functools.partial(kept_kernel, travelling is not None, 0),
        [shape(block, F32)],
        [flat],
        ins,
        specs + ([] if travelling is None else [flat]),
        grid=(tiles,),
        scalars=where,
    )[0]


def extended_block(line, where, left, right, groups, position, received, index, travelling, extra, last):
    width = right.shape[1] // (2 * groups)
    rows, more = left.shape[0], extra[0].shape[0]
    block = (left.shape[1] + more, width)
    moving = pl.BlockSpec((rows, width), lambda j, w: (0, column_block(w, position, groups, True)))
    small = pl.BlockSpec((more, width), lambda j, w: (0, column_block(w, position, groups, True)))
    ins = [left, right, received, *extra] + ([] if travelling is None else [travelling])
    specs = [const_spec(left.shape), moving, pl.BlockSpec((1,) + block, lambda j, w: (index, 0, 0)), small, small]
    outs = [(left.shape[1], width), (more, width)] if last else [block]
    result = line.call(
        functools.partial(kept_kernel, travelling is not None, len(extra)),
        [shape(dims, F32) for dims in outs],
        [const_spec(dims) for dims in outs],
        ins,
        specs + ([] if travelling is None else [const_spec(block)]),
        scalars=where,
    )
    return result if last else result[0]


def wide_kernel(pair_count, has_travelling, last, where, *refs):
    total = None
    for n in range(pair_count):
        part = product_tn(refs[2 * n][...], refs[2 * n + 1][...].astype(BF16))
        total = part if total is None else total + part
    rest = refs[2 * pair_count :]
    if has_travelling:
        total = total + rest[0][...]
        rest = rest[1:]
    if not last:
        rest[0][...] = total
        return
    send, keep, full = rest
    full[...] = total
    half = send.shape[0]
    keep[...] = full[pl.ds(pl.multiple_of(where[0] * half, half), half), :]
    send[...] = full[pl.ds(pl.multiple_of((1 - where[0]) * half, half), half), :]


def wide_block(line, where, pairs, groups, position, travelling, last, columns, shared):
    rows, depth = pairs[0][0].shape
    width = depth // groups
    tiles = 2
    part = columns // tiles
    ins, specs = [], []
    for left, right in pairs:
        ins += [left, right]
        specs.append(pl.BlockSpec((rows, width), lambda j, w: (0, outer_place(w, position, groups))))
        if shared and right.shape[1] > columns:
            specs.append(pl.BlockSpec((rows, part), lambda j, w: (0, w[0] * tiles + j)))
        else:
            specs.append(pl.BlockSpec((rows, part), lambda j, w: (0, j)))
    if travelling is not None:
        ins.append(travelling)
        specs.append(pl.BlockSpec((width, part), lambda j, w: (0, j)))
    height = width // 2 if last else width
    result = line.call(
        functools.partial(wide_kernel, len(pairs), travelling is not None, last),
        [shape((height, columns), F32)] * (2 if last else 1),
        [pl.BlockSpec((height, part), lambda j, w: (0, j))] * (2 if last else 1),
        ins,
        specs,
        grid=(tiles,),
        scalars=where,
        scratch=[pltpu.VMEM((width, part), F32)] if last else [],
    )
    return result if last else result[0]


def join_kernel(where, keep, got, *outs):
    mine, theirs = keep[...], got[...]
    low = where[0] == 0
    first, second = jnp.where(low, mine, theirs), jnp.where(low, theirs, mine)
    part = first.shape[1] // len(outs)
    for n, out in enumerate(outs):
        out[:, :part] = first[:, n * part : (n + 1) * part]
        out[:, part:] = second[:, n * part : (n + 1) * part]


def join_halves(line, where, keep, got, count):
    rows, columns = keep.shape
    out = (rows, 2 * columns // count)
    return line.call(
        join_kernel,
        [shape(out, F32)] * count,
        [const_spec(out)] * count,
        [keep, got],
        [const_spec(keep.shape)] * 2,
        scalars=where,
    )


def side_kernel(first, second, out):
    part = first.shape[1]
    out[:, :part] = first[...]
    out[:, part:] = second[...]


def side_by_side(line, first, second):
    rows, columns = first.shape
    spec = const_spec(first.shape)
    out = (rows, 2 * columns)
    return line.call(side_kernel, [shape(out, F32)], [const_spec(out)], [first, second], [spec, spec])[0]


class Plan:
    def __init__(self, line):
        self.line, self.steps, self.found, self.sent = line, {}, {}, {}

    def step(self, name, needs, work):
        self.steps[name] = (needs, work)

    def run(self, *names):
        for name in names:
            if name.startswith("~"):
                if name[1:] in self.sent:
                    self.line.last.append(self.sent[name[1:]])
            elif name in self.steps and name not in self.found:
                needs, work = self.steps[name]
                self.run(*needs)
                self.found[name] = work()

    def __getitem__(self, name):
        return self.found[name]


def on_device(
    dp,
    tensor,
    inputs,
    segments,
    decay_order,
    ln1_gain,
    ln1_bias,
    w_query,
    w_key,
    w_value,
    w_swish,
    w_out,
    ln2_gain,
    ln2_bias,
    w_gate,
    w_up,
    w_down,
    cotangent,
):
    line = Line()
    plan = Plan(line)
    groups = dp // 2
    place = lax.axis_index("dp")
    where = jnp.stack([lax.rem(place, 2), lax.div(place, 2), my_core()]).astype(jnp.int32)
    tables = angle_tables(SEQ_LEN)
    logs = jnp.log1p(-jnp.exp2(-(decay_order + 5).astype(F32)))
    seg_row = segments.reshape(1, SEQ_LEN)
    gain1, bias1, gain2, bias2 = (v.reshape(1, -1) for v in (ln1_gain, ln1_bias, ln2_gain, ln2_bias))
    rows = 2 * BLOCK

    def beside(name, values):
        plan.sent[name] = lax.ppermute(values, "dp", [(i, i ^ 1) for i in range(dp)])
        return plan.sent[name]

    def onward(name, values):
        plan.sent[name] = lax.ppermute(values, "dp", [(i, (i + 2) % dp) for i in range(dp)])
        return plan.sent[name]

    def across(name, values):
        plan.sent[name] = lax.ppermute(values, "tensor", [(i, i ^ 2) for i in range(tensor)])
        return plan.sent[name]


    def projected(n, begin, end):
        before = plan["P0"] if n else None
        result = projections(line, begin, end, inputs, gain1, bias1, tables, w_query, w_key, w_value, w_swish, before)
        return tuple(result[:7]) + (beside("H", result[7]) if n else result[7],)

    def retained(i):
        a, q, k, v, switch = plan["P1" if i else "P0"][:5]
        before = plan[f"R{i - 1}"][1:3] if i else None
        chip, u, o, p = retention(line, i, q, k, v, switch, seg_row, logs, w_out, before)
        return (chip, across(f"R{i}", chip)), u, o, p

    def fed(i):
        before = plan[f"F{i - 1}"] if i else None
        sums = plan[f"R{i}"][0]
        return feed_forward(line, i, *sums, inputs, gain2, bias2, cotangent, w_gate, w_up, w_down, before)

    last = CHUNKS - 1
    plan.step("P0", [], lambda: projected(0, 0, 1))
    plan.step("R0", ["P0"], lambda: retained(0))
    plan.step("P1", ["R0"], lambda: projected(1, 1, CHUNKS))
    for i in range(CHUNKS):
        plan.step(f"R{i}", ["P1", f"R{i - 1}"] if i else ["P0"], lambda i=i: retained(i))
        plan.step(f"F{i}", [f"R{i}"] + ([f"F{i - 1}"] if i else []), lambda i=i: fed(i))
    plan.step("G", ["P1"], lambda: partner_rows(line, plan["P1"][7], gain1, bias1))

    def first(n):
        return plan["P1"][n]


    def summed(name, lefts, rights, transposed, i, count=rows):
        chip = chip_sum(line, count, lefts, rights, transposed, i)
        return chip, across(name, chip)

    pair = range(2)

    def second_sum(i):
        dg, du = plan[f"F{last}"][1:3]
        return summed(f"B{i}", [dg, du], [w_gate, w_up], True, i)

    def middle_back(i):
        before = plan["M1"] if i == 0 else None
        return second_norm_back(line, 2 * i, *plan[f"B{i}"], plan[f"F{last}"][4], gain2, cotangent, before)

    def first_sum(i):
        dq, dk, dv = plan["AB"][:3]
        return summed(f"C{i}", [dq, dk, dv, plan["GB"][1]], [w_query, w_key, w_value, w_swish], True, i)

    def inputs_back(i):
        before = plan["I1"] if i == 0 else None
        return first_norm_back(line, 2 * i, *plan[f"C{i}"], inputs, gain1, plan["M0"][1], before)

    def feed_sum():
        return summed("D", [plan[f"F{last}"][0]], [w_down], False, 0, SEQ_LEN)

    def retention_grads():
        _, q, k, v, _, cos, sin = plan["P1"][:7]
        weights = [plan[f"R{i}"][3] for i in range(CHUNKS)]
        result = retention_back(line, where, q, k, v, plan["GB"][0], seg_row, logs, cos, sin, weights)
        return result[:4] + (beside("Tq", result[4]), beside("Tv", result[5]))

    def gate_grads():
        result = gate_back(line, where, plan["M0"][0], w_out, plan[f"R{last}"][2], first(4))
        return result[:2] + (beside("Ts", result[2]),)

    for i in reversed(pair):
        plan.step(f"B{i}", [f"F{last}"], lambda i=i: second_sum(i))
        plan.step(f"M{i}", [f"B{i}"] + ([] if i else ["M1"]), lambda i=i: middle_back(i))
        plan.step(f"C{i}", ["AB"], lambda i=i: first_sum(i))
        plan.step(f"I{i}", [f"C{i}", "M0"] + ([] if i else ["I1"]), lambda i=i: inputs_back(i))
    plan.step("GB", ["M0"], gate_grads)
    plan.step("AB", ["GB"], retention_grads)
    plan.step("D", [f"F{last}"], feed_sum)
    plan.step("O", ["D"], lambda: output_rows(line, *plan["D"], plan[f"F{last}"][4]))
    plan.step("CI", ["I0"], lambda: own_copy(line, plan["I0"][0]))
    plan.step("CO", ["O"], lambda: own_copy(line, plan["O"]))


    def small_sums():
        ln1 = [plan[f"I{i}"][n] for n in (1, 2) for i in pair]
        ln2 = [plan[f"M{i}"][n] for n in (2, 3) for i in pair]
        parts = ln1 + ln2
        own = [parts[2 * n] + parts[2 * n + 1] for n in range(4)]
        own = jnp.concatenate(own + [jnp.zeros((4, own[0].shape[1]), F32)], axis=0)
        plan.sent["L"] = lax.ppermute(own, "tensor", [(i, i ^ 1) for i in range(tensor)])
        return own, plan.sent["L"]

    plan.step("L", ["I0", "I1", "M0", "M1"], small_sums)


    def products(name, needs, operands, by_rows, extra=tuple, skip=0):
        cut = (groups + 1) // 2

        def send(part, begin, end):
            left, right = operands()
            blocks = sent_blocks(line, where, left, right, by_rows, groups, begin, end - begin, extra(), skip)
            return beside(f"S{name}{part}", blocks)

        def ring(j):
            part, index = ("A", j) if j < cut else ("B", j - cut)
            travelling = plan[f"K{name}{j - 1}"] if j else None
            left, right = operands()
            received = plan[f"S{name}{part}"]
            done = j == groups - 1
            block = kept_block(
                line, where, left, right, by_rows, groups, j, received, index, travelling, extra(), done, skip
            )
            return onward(f"K{name}{j}", block) if j < groups - 1 else block

        plan.step(f"S{name}A", needs, lambda: send("A", 0, cut))
        plan.step(f"S{name}B", needs, lambda: send("B", cut, groups))
        for j in range(groups):
            before = [f"K{name}{j - 1}"] if j else []
            plan.step(f"K{name}{j}", [f"S{name}A" if j < cut else f"S{name}B"] + before, lambda j=j: ring(j))
        return lambda: plan[f"K{name}{groups - 1}"]


    def ring_first(name, needs, operands, columns):
        def ring(j):
            travelling = plan[f"K{name}{j - 1}"] if j else None
            block = wide_block(
                line, where, [operands()], groups, j, travelling, j == groups - 1, columns, False
            )
            if j < groups - 1:
                return onward(f"K{name}{j}", block)
            return beside(f"K{name}{j}", block[0]), block[1]

        for j in range(groups):
            plan.step(f"K{name}{j}", [f"K{name}{j - 1}"] if j else needs, lambda j=j: ring(j))
        plan.step(f"E{name}", [f"K{name}{groups - 1}"], lambda: add(line, *plan[f"K{name}{groups - 1}"]))
        return lambda: plan[f"E{name}"]


    def shares(name, needs, operand, far, count):
        def ring(j):
            travelling = plan[f"J{name}{j - 1}"] if j else None
            right = operand()
            pairs = [(first(0), right), (plan["G"], far())]
            block = wide_block(
                line, where, pairs, groups, j, travelling, j == groups - 1, right.shape[1] // 2, True
            )
            if j < groups - 1:
                return onward(f"J{name}{j}", block)
            return block[1], beside(f"J{name}{j}", block[0])

        for j in range(groups):
            plan.step(f"J{name}{j}", ["G", f"J{name}{j - 1}"] if j else ["G", *needs], lambda j=j: ring(j))
        plan.step(f"E{name}", [f"J{name}{groups - 1}"], lambda: join_halves(line, where, *plan[f"J{name}{groups - 1}"], count))
        return lambda: plan[f"E{name}"]

    fed_all = lambda n: plan[f"F{last}"][n]
    normed2 = lambda: plan[f"F{last}"][3]
    down = products("d", [f"F{last}"], lambda: (fed_all(0), cotangent), False)
    gate = products("g", [f"F{last}"], lambda: (normed2(), fed_all(1)), True)
    half_ff = w_up.shape[1] // 2
    up = ring_first("u", [f"F{last}"], lambda: (normed2(), fed_all(2)), half_ff)
    more_up = products("w", [f"F{last}"], lambda: (normed2(), fed_all(2)), True, skip=half_ff)
    out = products("o", ["M0", "L"], lambda: (plan[f"R{last}"][1], plan["M0"][0]), False, lambda: plan["L"])
    plan.step("U", ["Eu", f"Kw{groups - 1}"], lambda: side_by_side(line, up(), more_up()))
    swish = shares("s", ["GB"], lambda: plan["GB"][1], lambda: plan["GB"][2], 1)
    vgrad = shares("v", ["AB"], lambda: plan["AB"][2], lambda: plan["AB"][5], 1)
    both = shares("q", ["AB"], lambda: plan["AB"][3], lambda: plan["AB"][4], 2)

    plan.run(
        "P0", "R0", "P1", "R1", "F0", "R2", "R3", "F1", "F2", "F3", "SgA", "Ku0", "B1", "SdA", "SwA", "Ku1", "B0",
        "Kg0", "SgB", "G", "Ku2", "Kg1", "M1", "SwB", "Kd0", "~Ku2", "M0", "Kw0", "GB", "AB", "Kd1", "Kg2", "Kw1",
        "C1", "Kg3", "Jq0", "~Kd1", "C0", "Jq1", "I1", "~Kw1", "Js0", "D", "Jq2", "Kw2", "I0", "Js1", "SoA", "Jq3",
        "SdB", "SoB", "Jv0", "Js2", "Kw3", "Ku3", "Ko0", "Jv1", "Kd2", "Ko1", "Js3", "O", "Jv2", "Eu", "CO", "Ko2",
        "U", "Jv3", "Eq", "Ko3", "Ev", "Es", "CI", "Kd3",
    )
    plan.run(*plan.steps)
    query, key = both()
    grad_out, small = out()
    return (
        plan["CO"],
        plan["CI"],
        small[0],
        small[1],
        query,
        key,
        vgrad()[0],
        swish()[0],
        grad_out,
        small[2],
        small[3],
        gate(),
        plan["U"],
        down(),
    )


def solution(mesh):
    dp, tensor = mesh.shape["dp"], mesh.shape["tensor"]

    def body(*arrays):
        return on_device(dp, tensor, *arrays)

    return jax.shard_map(
        body,
        mesh=mesh,
        in_specs=(
            P("dp", None),
            P("dp", None),
            P("tensor"),
            P(),
            P(),
            P(None, "tensor"),
            P(None, "tensor"),
            P(None, "tensor"),
            P(None, "tensor"),
            P("tensor", None),
            P(),
            P(),
            P(None, "tensor"),
            P(None, "tensor"),
            P("tensor", None),
            P("dp", None),
        ),
        out_specs=(
            P("dp", None),
            P("dp", None),
            P("dp"),
            P("dp"),
            P("dp", "tensor"),
            P("dp", "tensor"),
            P("dp", "tensor"),
            P("dp", "tensor"),
            P("tensor", "dp"),
            P("dp"),
            P("dp"),
            P("dp", "tensor"),
            P("dp", "tensor"),
            P("tensor", "dp"),
        ),
        check_vma=False,
    )
```
